32 devices in a mesh: tok: 8 (over y, x, core), head: 4 (over z).
Axes of the slice: x: 2, y: 2, z: 4, core: 2. Of those that a mesh axis runs over, the one named last changes fastest.
Arguments:
- hidden: float32 [4096, 5376], P('tok', 'head'), may hold values from -8 to 8
- queries: float32 [4096, 2048], P('tok', 'head'), may hold values from -4000 to 4000
- out_grad: float32 [4096, 2048], P('tok', 'head'), may hold values from -6 to 6
- w_key: float32 [5376, 1024], P('head', 'tok'), may hold values from -1 to 1
- w_value: float32 [5376, 1024], P('head', 'tok'), may hold values from -0.078125 to 0.078125
- fork_tile: int32 [7], replicated, may hold values from 0 to 25, as said below
- live_len: int32 [8], replicated, may hold values from 257 to 512, as said below
Outputs:
- grad_query: float32 [4096, 2048], P('tok', 'head')
- grad_key: float32 [4096, 1024], P('tok', 'head')
- grad_value: float32 [4096, 1024], P('tok', 'head')
- grad_w_key: float32 [5376, 1024], P('head', 'tok')
- grad_w_value: float32 [5376, 1024], P('head', 'tok')
The draws below stay inside these ranges and needn't reach their ends.
Inputs may be any that keep to these rules, and one draw needn't show every extreme that they name: fork_tile[b - 1] lies in branch b - 1 or b - 2 (branch 0 counts), among that branch's first 2 tiles, and those tiles are live. `live_len`: branch 0 is fully live.
All inputs are finite; a program needn't handle non-finite values.
Results may differ from the reference program's by a relative error of at most 0.0005.
Values sent between devices are 32-bit elements; how exact they have to be, the bound alone decides.
No kernel may reach another device: no remote copies, remote signals or barrier semaphores. Data moves between devices by JAX's collectives and lax.ppermute only.
A program may use at most 128 MiB of HBM per device.

```python
import jax
import jax.numpy as jnp
from jax import lax

D = 5376
HEADS = 16
KV_HEADS = 8
HEAD_DIM = 128
TILE = 128
CAP = 2
TOK_DEV = 512
TOKENS = 4096
N_TOK = 8


def draw_hidden(key, part):
    return jax.random.normal(jax.random.fold_in(key, 101), (TOKENS, D), jnp.float32)


def draw_w_key(key, part):
    return jax.random.normal(jax.random.fold_in(key, 102), (D, KV_HEADS * HEAD_DIM), jnp.float32) * D ** (-0.5)


def draw_queries(key, part):
    normal_rows = jax.random.normal(jax.random.fold_in(key, 103), (TOKENS, HEADS * HEAD_DIM), jnp.float32)
    return normal_rows


def draw_fork_tile(key, part):
    branches = TOKENS // TOK_DEV
    branch_ids = jnp.arange(1, branches)
    far_pick = jax.random.randint(jax.random.fold_in(key, 105), (branches - 1,), 0, 8)
    step_back = jnp.where(far_pick == 0, 2, 1)
    parent = jnp.maximum(branch_ids - step_back, 0)
    early_pick = jax.random.randint(jax.random.fold_in(key, 106), (branches - 1,), 0, 4)
    within = jnp.where(early_pick == 0, 0, CAP - 1)
    within = within.at[0].set(0)
    parent = parent.at[-1].set(branches - 2)
    within = within.at[-1].set(CAP - 1)
    return (parent * (TOK_DEV // TILE) + within).astype(jnp.int32)


def draw_live_len(key, part):
    branches = TOKENS // TOK_DEV
    lengths = jax.random.randint(jax.random.fold_in(key, 104), (branches,), TOK_DEV // 2 + 1, TOK_DEV + 1)
    lengths = lengths.at[0].set(TOK_DEV)
    lengths = lengths.at[1].set(TOK_DEV // 2 + 1)
    return lengths.astype(jnp.int32)


def level_of(rng, dims, shards, smallest, high):
    loudness, own = 1.0, jax.random.fold_in(rng, 6)
    for position, parts in shards:
        heights = jnp.exp(jax.random.uniform(jax.random.fold_in(own, position), (parts,), jnp.float32, smallest / len(shards), high / len(shards)))
        loudness = loudness * jnp.repeat(heights, dims[position] // parts).reshape([-1 if axis == position else 1 for axis in range(len(dims))])
    return loudness


def centred(key, dims, deviation, bound, cuts=(), kind=jnp.bfloat16):
    level = level_of(key, dims, cuts, -0.22, 0.18) if cuts else 1.0
    drawn = jax.random.normal(key, dims, jnp.float32) * deviation * level
    return jnp.minimum(jnp.maximum(drawn, -bound), bound).astype(kind)


def setup_inputs(seed: int = 0) -> dict:
    key_list = jax.random.split(jax.random.key(seed), 8)
    hidden = draw_hidden(jax.random.fold_in(key_list[7], 71), 0)
    queries = draw_queries(jax.random.fold_in(key_list[7], 71), 0)
    out_grad = centred(key_list[2], (TOKENS, HEADS * HEAD_DIM), 1.0, 6.0, ((0, 8), (1, 4)), jnp.float32)
    w_key = draw_w_key(jax.random.fold_in(key_list[7], 71), 0)
    w_value = centred(key_list[4], (D, KV_HEADS * HEAD_DIM), D ** -0.5, 0.078125, ((0, 4), (1, 8)), jnp.float32)
    fork_tile = draw_fork_tile(jax.random.fold_in(key_list[7], 71), 0)
    live_len = draw_live_len(jax.random.fold_in(key_list[7], 71), 0)
    return {"hidden": hidden, "queries": queries, "out_grad": out_grad, "w_key": w_key, "w_value": w_value, "fork_tile": fork_tile, "live_len": live_len}


logit_scale = 168.0 ** -0.5
highest = lax.Precision.HIGHEST


def path_table(fork_tile, owners, tile_count):
    initial = jnp.full((owners, owners), -1, jnp.int32)

    def visit_branch(branch, path_rows):
        fork_at = fork_tile[branch - 1]
        parent = fork_at // tile_count
        inherited = path_rows[parent].at[parent].set((fork_at % tile_count).astype(jnp.int32))
        return path_rows.at[branch].set(inherited)

    return lax.fori_loop(1, owners, visit_branch, initial)


def visible_mask(entries_row, live_count, row_count, owners):
    slot_index = jnp.arange(owners * CAP * TILE)
    owner_of = slot_index // (CAP * TILE)
    tile_of = (slot_index % (CAP * TILE)) // TILE
    remote = (tile_of <= entries_row[owner_of])[None, :]
    positions = jnp.arange(row_count)
    local_part = (positions[None, :] <= positions[:, None]) & (positions[None, :] < live_count)
    return jnp.concatenate([jnp.broadcast_to(remote, (row_count, remote.shape[1])), local_part], axis=1)


def attend(query_rows, grad_rows, key_rows, value_rows, visible):
    query_heads = query_rows.shape[1] // HEAD_DIM
    kv_heads = key_rows.shape[1] // HEAD_DIM
    group_size = query_heads // kv_heads
    query_grads = []
    key_grads = [jnp.zeros((key_rows.shape[0], HEAD_DIM), jnp.float32) for _ in range(kv_heads)]
    value_grads = [jnp.zeros((key_rows.shape[0], HEAD_DIM), jnp.float32) for _ in range(kv_heads)]
    for head_index in range(query_heads):
        kv_index = head_index // group_size
        query_head = query_rows[:, head_index * HEAD_DIM:(head_index + 1) * HEAD_DIM]
        grad_head = grad_rows[:, head_index * HEAD_DIM:(head_index + 1) * HEAD_DIM]
        key_head = key_rows[:, kv_index * HEAD_DIM:(kv_index + 1) * HEAD_DIM]
        value_head = value_rows[:, kv_index * HEAD_DIM:(kv_index + 1) * HEAD_DIM]
        scores = jnp.dot(query_head, key_head.T, precision=highest) * logit_scale
        scores = jnp.where(visible, scores, -1e30)
        largest = jnp.max(scores, axis=1, keepdims=True)
        weights = jnp.where(visible, jnp.exp(scores - largest), 0.0)
        weights = weights / jnp.sum(weights, axis=1, keepdims=True)
        output = jnp.dot(weights, value_head, precision=highest)
        delta_row = jnp.sum(grad_head * output, axis=1, keepdims=True)
        grad_prob = jnp.dot(grad_head, value_head.T, precision=highest)
        grad_score = weights * (grad_prob - delta_row)
        query_grads.append(jnp.dot(grad_score, key_head, precision=highest) * logit_scale)
        key_grads[kv_index] = key_grads[kv_index] + jnp.dot(grad_score.T, query_head, precision=highest) * logit_scale
        value_grads[kv_index] = value_grads[kv_index] + jnp.dot(weights.T, grad_head, precision=highest)
    return jnp.concatenate(query_grads, axis=1), jnp.concatenate(key_grads, axis=1), jnp.concatenate(value_grads, axis=1)


def reference(hidden, queries, out_grad, w_key, w_value, fork_tile, live_len):
    key_rows = jnp.dot(hidden, w_key, precision=highest)
    value_rows = jnp.dot(hidden, w_value, precision=highest)
    kv_width = key_rows.shape[1]
    fork_span = CAP * TILE
    remote_count = N_TOK * fork_span
    path_rows = path_table(fork_tile, N_TOK, TOK_DEV // TILE)
    fork_keys = key_rows.reshape(N_TOK, TOK_DEV, kv_width)[:, :fork_span].reshape(remote_count, kv_width)
    fork_values = value_rows.reshape(N_TOK, TOK_DEV, kv_width)[:, :fork_span].reshape(remote_count, kv_width)

    def per_branch(totals, branch):
        first_row = branch * TOK_DEV
        query_rows = lax.dynamic_slice_in_dim(queries, first_row, TOK_DEV, 0)
        live_rows = (jnp.arange(TOK_DEV) < live_len[branch]).astype(jnp.float32)[:, None]
        grad_rows = lax.dynamic_slice_in_dim(out_grad, first_row, TOK_DEV, 0) * live_rows
        own_keys = lax.dynamic_slice_in_dim(key_rows, first_row, TOK_DEV, 0)
        own_values = lax.dynamic_slice_in_dim(value_rows, first_row, TOK_DEV, 0)
        visible = visible_mask(path_rows[branch], live_len[branch], TOK_DEV, N_TOK)
        grad_q, grad_k, grad_v = attend(query_rows, grad_rows, jnp.concatenate([fork_keys, own_keys], axis=0), jnp.concatenate([fork_values, own_values], axis=0), visible)
        totals = (totals[0] + grad_k[:remote_count], totals[1] + grad_v[:remote_count])
        return totals, (grad_q, grad_k[remote_count:], grad_v[remote_count:])

    initial = (jnp.zeros((remote_count, kv_width), jnp.float32), jnp.zeros((remote_count, kv_width), jnp.float32))
    totals, outputs = lax.scan(per_branch, initial, jnp.arange(N_TOK, dtype=jnp.int32))
    grad_query = outputs[0].reshape(N_TOK * TOK_DEV, -1)
    grad_key = outputs[1].at[:, :fork_span].add(totals[0].reshape(N_TOK, fork_span, kv_width)).reshape(N_TOK * TOK_DEV, kv_width)
    grad_value = outputs[2].at[:, :fork_span].add(totals[1].reshape(N_TOK, fork_span, kv_width)).reshape(N_TOK * TOK_DEV, kv_width)
    grad_w_key = jnp.dot(hidden.T, grad_key, precision=highest)
    grad_w_value = jnp.dot(hidden.T, grad_value, precision=highest)
    return grad_query, grad_key, grad_value, grad_w_key, grad_w_value
```

```python
import functools

import jax
import jax.numpy as jnp
from jax import lax
from jax.experimental import pallas as pl
from jax.experimental.pallas import tpu as pltpu
from jax.sharding import PartitionSpec as P

HEAD_DIM = 128
TILE = 128
CAP = 2
SPAN = CAP * TILE

logit_scale = 168.0 ** (-0.5)
f32 = jnp.float32
bf16 = jnp.bfloat16
VMEM_LIMIT = 56 * 1024 * 1024


def split(rows):
    high = rows.astype(bf16)
    return high, (rows - high.astype(f32)).astype(bf16)


def pair_cat(rows, axis):
    return jnp.concatenate(split(rows), axis=axis)


def dot(left, right):
    return jnp.dot(left, right, preferred_element_type=f32)


def dot_first(left, right):
    return lax.dot_general(left, right, (((0,), (0,)), ((), ())), preferred_element_type=f32)


def whole_spec(array):
    return pl.BlockSpec(array.shape, lambda *_: (0,) * len(array.shape))


smem_spec = pl.BlockSpec(memory_space=pltpu.SMEM)


def project_body(place_ref, *refs, row_inputs, parts, steps_each):
    x_refs = refs[:row_inputs]
    w_refs = refs[row_inputs : row_inputs + parts]
    out_ref, high_ref, low_ref = refs[row_inputs + parts :]
    step = pl.program_id(0)

    @pl.when(step == 0)
    def _():
        for part in range(parts):
            high, low = split(w_refs[part][...])
            high_ref[:, part * HEAD_DIM : (part + 1) * HEAD_DIM] = high
            low_ref[:, part * HEAD_DIM : (part + 1) * HEAD_DIM] = low

    for source in range(row_inputs):

        @pl.when(step // steps_each == source)
        def _():
            x_high, x_low = split(x_refs[source][...])
            total = dot(x_high, high_ref[...]) + dot(x_high, low_ref[...]) + dot(x_low, high_ref[...])
            for part in range(parts):
                out_ref[place_ref[part]] = total[:, part * HEAD_DIM : (part + 1) * HEAD_DIM]


def project(place, xs, ws):
    rows, depth = xs[0].shape
    parts = len(ws)
    block = 256
    steps_each = rows // block
    steps = steps_each * len(xs)

    def x_map(source):
        return lambda step: (jnp.clip(step - source * steps_each, 0, steps_each - 1), 0)

    return pl.pallas_call(
        functools.partial(project_body, row_inputs=len(xs), parts=parts, steps_each=steps_each),
        grid=(steps,),
        in_specs=[smem_spec]
        + [pl.BlockSpec((block, depth), x_map(source)) for source in range(len(xs))]
        + [whole_spec(w) for w in ws],
        out_specs=pl.BlockSpec((parts, block, HEAD_DIM), lambda step: (0, step, 0)),
        out_shape=jax.ShapeDtypeStruct((parts, rows * len(xs), HEAD_DIM), f32),
        scratch_shapes=[pltpu.VMEM((depth, parts * HEAD_DIM), bf16)] * 2,
        compiler_params=pltpu.CompilerParams(vmem_limit_bytes=VMEM_LIMIT),
        cost_estimate=pl.CostEstimate(
            flops=6 * rows * len(xs) * depth * parts * HEAD_DIM, bytes_accessed=4 * rows * len(xs) * depth, transcendentals=0
        ),
    )(place, *xs, *ws)


def weight_grad_body(place_ref, *refs, row_inputs, parts):
    x_refs = refs[:row_inputs]
    g_ref = refs[row_inputs]
    out_refs = refs[row_inputs + 1 : row_inputs + 1 + parts]
    high_ref, low_ref = refs[row_inputs + 1 + parts :]
    rows = x_refs[0].shape[0]

    @pl.when(pl.program_id(0) == 0)
    def _():
        for part in range(parts):
            high, low = split(g_ref[place_ref[part]])
            high_ref[:, part * HEAD_DIM : (part + 1) * HEAD_DIM] = high
            low_ref[:, part * HEAD_DIM : (part + 1) * HEAD_DIM] = low

    total = jnp.zeros((x_refs[0].shape[1], parts * HEAD_DIM), f32)
    for source in range(row_inputs):
        x_high, x_low = split(x_refs[source][...])
        g_high = high_ref[source * rows : (source + 1) * rows]
        g_low = low_ref[source * rows : (source + 1) * rows]
        total += dot_first(x_high, g_high) + dot_first(x_high, g_low) + dot_first(x_low, g_high)
    for part in range(parts):
        out_refs[part][...] = total[:, part * HEAD_DIM : (part + 1) * HEAD_DIM]


def weight_grad(place, xs, grads):
    rows, depth = xs[0].shape
    parts = grads.shape[0]
    block = 256
    return pl.pallas_call(
        functools.partial(weight_grad_body, row_inputs=len(xs), parts=parts),
        grid=(pl.cdiv(depth, block),),
        in_specs=[smem_spec] + [pl.BlockSpec((rows, block), lambda step: (0, step))] * len(xs) + [whole_spec(grads)],
        out_specs=[pl.BlockSpec((block, HEAD_DIM), lambda step: (step, 0))] * parts,
        out_shape=[jax.ShapeDtypeStruct((depth, HEAD_DIM), f32)] * parts,
        scratch_shapes=[pltpu.VMEM((rows * len(xs), parts * HEAD_DIM), bf16)] * 2,
        compiler_params=pltpu.CompilerParams(vmem_limit_bytes=VMEM_LIMIT),
        cost_estimate=pl.CostEstimate(
            flops=6 * rows * len(xs) * depth * parts * HEAD_DIM, bytes_accessed=4 * rows * len(xs) * depth, transcendentals=0
        ),
    )(place, *xs, grads)


def list_blocks(own_ref, fork_ref, offset_ref, limit_ref, step, tok, owners, halves, tiles, paired):
    branch_slot = step // halves
    half = step % halves
    branch = tok ^ branch_slot
    for block in range(halves):
        offset_ref[block] = (owners + branch_slot * halves + block) * SPAN
        limit_ref[block] = -1
    own_count = half + 1

    def climb(_, carry):
        current, count = carry
        fork_at = fork_ref[jnp.maximum(current - 1, 0)]
        parent = lax.div(fork_at, jnp.int32(tiles))
        inside = lax.rem(fork_at, jnp.int32(tiles))

        @pl.when(current > 0)
        def _():
            offset_ref[count] = ((tok ^ parent) if paired else parent) * SPAN
            limit_ref[count] = (inside + 1) * TILE - 1

        return jnp.where(current > 0, parent, 0), count + (current > 0).astype(jnp.int32)

    _, count = lax.fori_loop(0, owners, climb, (branch, own_count))
    return branch, branch_slot, half, count, own_count


def key_limits(block, limit_ref, own_count, half, live, lanes):
    lane = lax.broadcasted_iota(jnp.int32, (1, lanes), 1)
    position = half * SPAN + lax.rem(lane, jnp.int32(SPAN))
    own_limit = jnp.minimum(position, live - 1) - block * SPAN
    return jnp.where(block < own_count, own_limit, limit_ref[block])


def transposed_pair(rows):
    high, low = split(rows.T)
    return jnp.concatenate([high, high, low, low], axis=0)


def load_rows(ref, half, head):
    return ref[pl.ds(pl.multiple_of(half * SPAN, SPAN), SPAN), head * HEAD_DIM : (head + 1) * HEAD_DIM]


def live_column(half, live):
    position = half * SPAN + lax.broadcasted_iota(jnp.int32, (SPAN, 1), 0)
    return (position < live).astype(f32)


def block_rows(ref, offset):
    return ref[pl.ds(pl.multiple_of(offset, SPAN), SPAN), :]


def slot_rows(block):
    return pl.ds(pl.multiple_of(block * SPAN, SPAN), SPAN)


def stage_rows(target_ref, source_refs, layout):
    for index, start, offset, count in layout:
        for piece in range(0, count, SPAN):
            target_ref[offset + piece : offset + piece + SPAN, :] = pair_cat(
                source_refs[index][start + piece : start + piece + SPAN, :], 1
            )


def write_rows(source_ref, target_refs, layout):
    for index, start, offset, count in layout:
        if index > 0:
            target_refs[index - 1][start : start + count, :] = source_ref[offset : offset + count, :]
    own = layout[0]
    target_refs[-1][...] = source_ref[own[2] : own[2] + own[3], :]
    for index, start, offset, count in layout[1:]:
        if index == 0:
            target_refs[-1][start : start + count, :] += source_ref[offset : offset + count, :]


def scores(keys_ref, offset, queries, limits):
    keys = block_rows(keys_ref, offset)
    result = dot(jnp.concatenate([keys, keys], axis=1), queries)
    row = lax.broadcasted_iota(jnp.int32, result.shape, 0)
    return jnp.where(row <= limits, result, -1e30)


def fold(value, how):
    return how(value.reshape(SPAN // 8, 8, value.shape[1]), axis=0)


def soft_body(tok_ref, fork_ref, live_ref, *refs, conf):
    nb, group, owners, layout, sources, outs = conf["nb"], conf["group"], conf["owners"], conf["layout"], conf["sources"], conf["outs"]
    halves = conf["rows"] // SPAN
    lanes = group * SPAN
    q_refs, g_refs = refs[:nb], refs[nb : 2 * nb]
    key_refs = refs[2 * nb : 2 * nb + sources]
    stats_ref = refs[2 * nb + sources]
    out_refs = refs[2 * nb + sources + 1 : 2 * nb + sources + 1 + outs]
    keys_ref, sum_ref, score_ref, qt_ref, grad_ref, offset_ref, limit_ref = refs[2 * nb + sources + 1 + outs :]
    step = pl.program_id(0)
    tok = tok_ref[0]

    @pl.when(step == 0)
    def _():
        stage_rows(keys_ref, key_refs, layout)
        sum_ref[...] = jnp.zeros_like(sum_ref)

    branch, slot, half, count, own_count = list_blocks(
        tok_ref, fork_ref, offset_ref, limit_ref, step, tok, owners, halves, conf["rows"] // TILE, conf["paired"]
    )
    live = live_ref[branch]
    for source in range(nb):

        @pl.when(slot == source)
        def _():
            for head in range(group):
                qt_ref[:, head * SPAN : (head + 1) * SPAN] = transposed_pair(load_rows(q_refs[source], half, head) * logit_scale)
                grad_ref[head * SPAN : (head + 1) * SPAN, :] = pair_cat(
                    load_rows(g_refs[source], half, head) * live_column(half, live), 1
                )

    def first(block, largest):
        value = scores(keys_ref, offset_ref[block], qt_ref[...], key_limits(block, limit_ref, own_count, half, live, lanes))
        score_ref[slot_rows(block), :] = value
        return jnp.maximum(largest, fold(value, jnp.max))

    largest = lax.fori_loop(0, count, first, jnp.full((8, lanes), -1e30, f32))
    largest = jnp.max(largest, axis=0, keepdims=True)

    def second(block, total):
        value = jnp.exp(score_ref[slot_rows(block), :] - largest)
        score_ref[slot_rows(block), :] = value
        return total + fold(value, jnp.sum)

    total = lax.fori_loop(0, count, second, jnp.zeros((8, lanes), f32))
    inverse = 1.0 / jnp.sum(total, axis=0, keepdims=True)
    stats_ref[0, 0:1, :] = largest
    stats_ref[0, 1:2, :] = inverse

    def third(block, _):
        high, low = split(score_ref[slot_rows(block), :] * inverse)
        grads = grad_ref[...]
        both = dot(high, grads) + dot(low, grads)
        offset = offset_ref[block]
        sum_ref[slot_rows(offset // SPAN), :] += both[:, :HEAD_DIM] + both[:, HEAD_DIM:]
        return 0

    lax.fori_loop(0, count, third, 0)

    @pl.when(step == nb * halves - 1)
    def _():
        write_rows(sum_ref, out_refs, layout)


def grad_body(tok_ref, fork_ref, live_ref, *refs, conf):
    nb, group, owners, layout, sources, outs = conf["nb"], conf["group"], conf["owners"], conf["layout"], conf["sources"], conf["outs"]
    halves = conf["rows"] // SPAN
    lanes = group * SPAN
    q_refs, g_refs = refs[:nb], refs[nb : 2 * nb]
    at = 2 * nb
    key_refs, value_refs = refs[at : at + sources], refs[at + sources : at + 2 * sources]
    at += 2 * sources
    stats_ref = refs[at]
    dq_ref = refs[at + 1]
    out_refs = refs[at + 2 : at + 2 + outs]
    (keys_ref, values_ref, sum_ref, prob_ref, dprob_ref, qt_ref, gt_ref, q_ref, dqt_ref, offset_ref, limit_ref) = refs[at + 2 + outs :]
    step = pl.program_id(0)
    tok = tok_ref[0]

    @pl.when(step == 0)
    def _():
        stage_rows(keys_ref, key_refs, layout)
        stage_rows(values_ref, value_refs, layout)
        sum_ref[...] = jnp.zeros_like(sum_ref)

    branch, slot, half, count, own_count = list_blocks(
        tok_ref, fork_ref, offset_ref, limit_ref, step, tok, owners, halves, conf["rows"] // TILE, conf["paired"]
    )
    live = live_ref[branch]
    for source in range(nb):

        @pl.when(slot == source)
        def _():
            for head in range(group):
                rows = load_rows(q_refs[source], half, head) * logit_scale
                qt_ref[:, head * SPAN : (head + 1) * SPAN] = transposed_pair(rows)
                q_ref[head * SPAN : (head + 1) * SPAN, :] = pair_cat(rows, 1)
                gt_ref[:, head * SPAN : (head + 1) * SPAN] = transposed_pair(
                    load_rows(g_refs[source], half, head) * live_column(half, live)
                )

    largest = stats_ref[0, 0:1, :]
    inverse = stats_ref[0, 1:2, :]

    def first(block, delta):
        offset = offset_ref[block]
        value = scores(keys_ref, offset, qt_ref[...], key_limits(block, limit_ref, own_count, half, live, lanes))
        prob = jnp.exp(value - largest) * inverse
        values = block_rows(values_ref, offset)
        dprob = dot(jnp.concatenate([values, values], axis=1), gt_ref[...])
        prob_ref[slot_rows(block), :] = prob
        dprob_ref[slot_rows(block), :] = dprob
        return delta + fold(prob * dprob, jnp.sum)

    delta = lax.fori_loop(0, count, first, jnp.zeros((8, lanes), f32))
    delta = jnp.sum(delta, axis=0, keepdims=True)
    dqt_ref[...] = jnp.zeros_like(dqt_ref)

    def second(block, _):
        offset = offset_ref[block]
        high, low = split(prob_ref[slot_rows(block), :] * (dprob_ref[slot_rows(block), :] - delta))
        rows = q_ref[...]
        both = dot(high, rows) + dot(low, rows)
        sum_ref[slot_rows(offset // SPAN), :] += both[:, :HEAD_DIM] + both[:, HEAD_DIM:]
        keys = block_rows(keys_ref, offset)
        dqt_ref[...] += dot_first(keys, high) + dot_first(keys, low)
        return 0

    lax.fori_loop(0, count, second, 0)
    folded = (dqt_ref[:HEAD_DIM, :] + dqt_ref[HEAD_DIM:, :]) * logit_scale
    for head in range(group):
        dq_ref[:, head * HEAD_DIM : (head + 1) * HEAD_DIM] = folded[:, head * SPAN : (head + 1) * SPAN].T

    @pl.when(step == nb * halves - 1)
    def _():
        write_rows(sum_ref, out_refs, layout)


def attention_calls(scalars, qs, gs, layout, paired, owners, part_rows):
    rows, width = qs[0].shape
    nb, group, halves = len(qs), width // HEAD_DIM, rows // SPAN
    lanes = group * SPAN
    steps = nb * halves
    conf = dict(nb=nb, group=group, rows=rows, owners=owners, layout=layout, paired=paired, sources=1 + len(part_rows), outs=len(part_rows) + 1)
    table_rows = owners * SPAN + nb * rows
    slots = (owners + halves) * SPAN
    sums = [jax.ShapeDtypeStruct((count, HEAD_DIM), f32) for count in part_rows] + [jax.ShapeDtypeStruct((nb * rows, HEAD_DIM), f32)]
    stats = jax.ShapeDtypeStruct((steps, 8, lanes), f32)
    stats_spec = pl.BlockSpec((1, 8, lanes), lambda step: (step, 0, 0))
    table = pltpu.VMEM((table_rows, 2 * HEAD_DIM), bf16)
    table_sum = pltpu.VMEM((table_rows, HEAD_DIM), f32)
    square = pltpu.VMEM((slots, lanes), f32)
    columns = pltpu.VMEM((4 * HEAD_DIM, lanes), bf16)
    lists = [pltpu.SMEM((owners + halves + 1,), jnp.int32)] * 2
    params = pltpu.CompilerParams(vmem_limit_bytes=VMEM_LIMIT)
    work = 2 * steps * 6 * SPAN * lanes * 2 * HEAD_DIM

    def soft(keys):
        return pl.pallas_call(
            functools.partial(soft_body, conf=conf),
            grid=(steps,),
            in_specs=[smem_spec] * 3 + [whole_spec(a) for a in (*qs, *gs, *keys)],
            out_specs=[stats_spec] + [whole_spec(a) for a in sums],
            out_shape=[stats] + sums,
            scratch_shapes=[table, table_sum, square, columns, pltpu.VMEM((lanes, 2 * HEAD_DIM), bf16)] + lists,
            compiler_params=params,
            cost_estimate=pl.CostEstimate(flops=2 * work, bytes_accessed=4 * rows * width, transcendentals=0),
        )(*scalars, *qs, *gs, *keys)

    def grad(keys, values, stats_in):
        dq = jax.ShapeDtypeStruct((nb * rows, width), f32)
        return pl.pallas_call(
            functools.partial(grad_body, conf=conf),
            grid=(steps,),
            in_specs=[smem_spec] * 3 + [whole_spec(a) for a in (*qs, *gs, *keys, *values)] + [stats_spec],
            out_specs=[pl.BlockSpec((SPAN, width), lambda step: (step, 0))] + [whole_spec(a) for a in sums],
            out_shape=[dq] + sums,
            scratch_shapes=[
                table,
                table,
                table_sum,
                square,
                square,
                columns,
                columns,
                pltpu.VMEM((lanes, 2 * HEAD_DIM), bf16),
                pltpu.VMEM((2 * HEAD_DIM, lanes), f32),
            ]
            + lists,
            compiler_params=params,
            cost_estimate=pl.CostEstimate(flops=4 * work, bytes_accessed=4 * rows * width, transcendentals=0),
        )(*scalars, *qs, *gs, *keys, *values, stats_in)

    return soft, grad


def flip(array, mask):
    count = lax.axis_size("tok")
    return lax.ppermute(array, "tok", [(index, index ^ mask) for index in range(count)])


def gather_square(array, cut):
    across = flip(array, 2)
    down = flip(array, 4)
    return across, down, flip(across[:cut], 4), flip(down[cut:], 2)


def scatter_square(across, down, corner_head, corner_tail, cut):
    from_across = flip(corner_head, 2)
    from_down = flip(corner_tail, 4)
    down = down.at[:cut].add(from_across)
    across = across.at[cut:].add(from_down)
    return flip(across, 2), flip(down, 4)


def shards_paired(hidden, queries, out_grad, w_key, w_value, fork_tile, live_len):
    owners = lax.axis_size("tok")
    depth = lax.axis_size("head")
    tok = lax.axis_index("tok").astype(jnp.int32)
    core = tok % 2
    rows = hidden.shape[0]
    width = queries.shape[1] // 2
    scalars = (tok.reshape(1), fork_tile, live_len)
    place = (tok // 2) ^ jnp.arange(depth, dtype=jnp.int32)
    half_depth = w_key.shape[0] // 2

    def gather_weight(w):
        across, down, head, tail = gather_square(w, half_depth)
        return [w, across, down, jnp.concatenate([head, tail], axis=0)]

    def mine(array):
        return lax.dynamic_slice_in_dim(array, core * width, width, 1)

    def partners(array):
        return flip(lax.dynamic_slice_in_dim(array, (1 - core) * width, width, 1), 1)

    xs = [hidden, flip(hidden, 1)]
    qs = [mine(queries), partners(queries)]
    gs = [mine(out_grad), partners(out_grad)]
    keys = lax.psum_scatter(project(place, xs, gather_weight(w_key)), "head", scatter_dimension=0, tiled=True)[0]
    values = lax.psum_scatter(project(place, xs, gather_weight(w_value)), "head", scatter_dimension=0, tiled=True)[0]

    def lead(array):
        return jnp.concatenate([array[:SPAN], array[rows : rows + SPAN]], axis=0)

    base = owners * SPAN
    layout = (
        (0, 0, base, 2 * rows),
        (0, 0, 0, SPAN),
        (0, rows, SPAN, SPAN),
        (1, 0, 2 * SPAN, 2 * SPAN),
        (2, 0, 4 * SPAN, 2 * SPAN),
        (3, 0, 6 * SPAN, SPAN),
        (4, 0, 7 * SPAN, SPAN),
    )
    soft, grad = attention_calls(scalars, qs, gs, layout, True, owners, (2 * SPAN, 2 * SPAN, SPAN, SPAN))

    def returned(own, across, down, head, tail):
        first, second = scatter_square(across, down, head, tail, SPAN)
        both = first + second
        return own.at[:SPAN].add(both[:SPAN]).at[rows : rows + SPAN].add(both[SPAN:])

    def weight(grads):
        every = lax.all_gather(grads, "head", axis=0, tiled=False)
        own, across, down, corner = weight_grad(place, xs, every)
        first, second = scatter_square(across, down, corner[:half_depth], corner[half_depth:], half_depth)
        return own + first + second

    def home(array):
        kept, received = array[:rows], flip(array[rows:], 1)
        return jnp.where(core == 0, jnp.concatenate([kept, received], axis=1), jnp.concatenate([received, kept], axis=1))

    key_parts = [keys, *gather_square(lead(keys), SPAN)]
    stats, *value_sums = soft(key_parts)
    value_grads = returned(value_sums[-1], *value_sums[:-1])
    grad_w_value = weight(value_grads)
    value_parts = [values, *gather_square(lead(values), SPAN)]
    grad_query, *key_sums = grad(key_parts, value_parts, stats)
    key_grads = returned(key_sums[-1], *key_sums[:-1])
    grad_w_key = weight(key_grads)
    return home(grad_query), home(key_grads), home(value_grads), grad_w_key, grad_w_value


def shards_single(hidden, queries, out_grad, w_key, w_value, fork_tile, live_len):
    owners = lax.axis_size("tok")
    depth = lax.axis_size("head")
    tok = lax.axis_index("tok").astype(jnp.int32)
    scalars = (tok.reshape(1), fork_tile, live_len)
    place = jnp.arange(depth, dtype=jnp.int32)

    def projected(w):
        every = lax.all_gather(w, "tok", axis=1, tiled=True)
        pieces = [every[:, index * HEAD_DIM : (index + 1) * HEAD_DIM] for index in range(depth)]
        return lax.psum_scatter(project(place, [hidden], pieces), "head", scatter_dimension=0, tiled=True)[0]

    keys, values = projected(w_key), projected(w_value)
    layout = ((0, 0, owners * SPAN, hidden.shape[0]), (1, 0, 0, owners * SPAN))
    soft, grad = attention_calls(scalars, [queries], [out_grad], layout, False, owners, (owners * SPAN,))

    def parts(array):
        return [array, lax.all_gather(array[:SPAN], "tok", axis=0, tiled=True)]

    def returned(remote, own):
        return own.at[:SPAN].add(lax.psum_scatter(remote, "tok", scatter_dimension=0, tiled=True))

    def weight(grads):
        every = lax.all_gather(grads, "head", axis=0, tiled=False)
        columns = jnp.concatenate(weight_grad(place, [hidden], every), axis=1)
        return lax.psum_scatter(columns, "tok", scatter_dimension=1, tiled=True)

    key_parts = parts(keys)
    stats, *value_sums = soft(key_parts)
    value_grads = returned(*value_sums)
    grad_query, *key_sums = grad(key_parts, parts(values), stats)
    key_grads = returned(*key_sums)
    return grad_query, key_grads, value_grads, weight(key_grads), weight(value_grads)


def solution(mesh):
    owners, depth = mesh.shape["tok"], mesh.shape["head"]
    paired = owners == 8 and depth == 4

    placed = (P("tok", "head"), P("tok", "head"), P("tok", "head"), P("head", "tok"), P("head", "tok"), P(), P())
    return jax.shard_map(
        shards_paired if paired else shards_single,
        mesh=mesh,
        in_specs=placed,
        out_specs=(P("tok", "head"), P("tok", "head"), P("tok", "head"), P("head", "tok"), P("head", "tok")),
        check_vma=False,
    )
```

```python
import functools

import jax
import jax.numpy as jnp
from jax import lax
from jax.experimental import pallas as pl
from jax.experimental.pallas import tpu as pltpu
from jax.sharding import PartitionSpec as P

HEAD_DIM = 128
TILE = 128
CAP = 2
SPAN = CAP * TILE

logit_scale = 168.0 ** (-0.5)
f32 = jnp.float32
bf16 = jnp.bfloat16
VMEM_LIMIT = 56 * 1024 * 1024


def split(rows):
    high = rows.astype(bf16)
    return high, (rows - high.astype(f32)).astype(bf16)


def pair_cat(rows, axis):
    return jnp.concatenate(split(rows), axis=axis)


def dot(left, right):
    return jnp.dot(left, right, preferred_element_type=f32)


def dot_first(left, right):
    return lax.dot_general(left, right, (((0,), (0,)), ((), ())), preferred_element_type=f32)


def whole_spec(array):
    return pl.BlockSpec(array.shape, lambda *_: (0,) * len(array.shape))


smem_spec = pl.BlockSpec(memory_space=pltpu.SMEM)


def project_body(place_ref, *refs, row_inputs, weights, steps_each):
    x_refs = refs[:row_inputs]
    count = 1 + max(part for part, _ in weights)
    w_refs = refs[row_inputs : row_inputs + len(weights)]
    out_ref, pair_ref = refs[row_inputs + len(weights) :]
    step = pl.program_id(0)
    columns = count * HEAD_DIM

    @pl.when(step == 0)
    def _():
        for (part, start), w_ref in zip(weights, w_refs):
            high, low = split(w_ref[...].T)
            stop = start + w_ref.shape[0]
            pair_ref[part * HEAD_DIM : (part + 1) * HEAD_DIM, start:stop] = high
            pair_ref[columns + part * HEAD_DIM : columns + (part + 1) * HEAD_DIM, start:stop] = low

    for source in range(row_inputs):

        @pl.when(step // steps_each == source)
        def _():
            x_high, x_low = split(x_refs[source][...])
            both = dot(pair_ref[...], x_high)
            total = both[:columns] + both[columns:] + dot(pair_ref[:columns], x_low)
            for part in range(count):
                out_ref[place_ref[part]] = total[part * HEAD_DIM : (part + 1) * HEAD_DIM]


def project(place, xs, ws, weights):
    depth, rows = xs[0].shape
    parts = place.shape[0]
    block = 256
    steps_each = rows // block

    def x_map(source):
        return lambda step: (0, jnp.clip(step - source * steps_each, 0, steps_each - 1))

    return pl.pallas_call(
        functools.partial(project_body, row_inputs=len(xs), weights=weights, steps_each=steps_each),
        grid=(steps_each * len(xs),),
        in_specs=[smem_spec]
        + [pl.BlockSpec((depth, block), x_map(source)) for source in range(len(xs))]
        + [whole_spec(w) for w in ws],
        out_specs=pl.BlockSpec((parts, HEAD_DIM, block), lambda step: (0, 0, step)),
        out_shape=jax.ShapeDtypeStruct((parts, HEAD_DIM, rows * len(xs)), f32),
        scratch_shapes=[pltpu.VMEM((2 * parts * HEAD_DIM, depth), bf16)],
        compiler_params=pltpu.CompilerParams(vmem_limit_bytes=VMEM_LIMIT),
        cost_estimate=pl.CostEstimate(
            flops=6 * rows * len(xs) * depth * parts * HEAD_DIM, bytes_accessed=4 * rows * len(xs) * depth, transcendentals=0
        ),
    )(place, *xs, *ws)


def weight_grad_body(place_ref, *refs, row_inputs, parts, cut):
    x_refs = refs[:row_inputs]
    g_ref = refs[row_inputs]
    out_refs = refs[row_inputs + 1 : -1]
    pair_ref = refs[-1]
    rows = x_refs[0].shape[1]
    columns = parts * HEAD_DIM
    step = pl.program_id(0)

    @pl.when(step == 0)
    def _():
        for part in range(parts):
            high, low = split(g_ref[place_ref[part]])
            pair_ref[:, part * HEAD_DIM : (part + 1) * HEAD_DIM] = high
            pair_ref[:, columns + part * HEAD_DIM : columns + (part + 1) * HEAD_DIM] = low

    total = jnp.zeros((x_refs[0].shape[0], columns), f32)
    for source in range(row_inputs):
        x_high, x_low = split(x_refs[source][...])
        pair = pair_ref[source * rows : (source + 1) * rows]
        both = dot(x_high, pair)
        total += both[:, :columns] + both[:, columns:] + dot(x_low, pair[:, :columns])
    for part in range(parts - 1 if cut else parts):
        out_refs[part][...] = total[:, part * HEAD_DIM : (part + 1) * HEAD_DIM]
    if cut:
        for piece in range(2):

            @pl.when(step == piece)
            def _():
                out_refs[parts - 1 + piece][...] = total[:, (parts - 1) * HEAD_DIM :]


def weight_grad(place, xs, grads, cut):
    depth, rows = xs[0].shape
    parts = grads.shape[0]
    block = depth // 2
    piece = jax.ShapeDtypeStruct((block, HEAD_DIM), f32)
    full = parts - 1 if cut else parts
    return pl.pallas_call(
        functools.partial(weight_grad_body, row_inputs=len(xs), parts=parts, cut=cut),
        grid=(2,),
        in_specs=[smem_spec] + [pl.BlockSpec((block, rows), lambda step: (step, 0))] * len(xs) + [whole_spec(grads)],
        out_specs=[pl.BlockSpec((block, HEAD_DIM), lambda step: (step, 0))] * full + [whole_spec(piece)] * (2 if cut else 0),
        out_shape=[jax.ShapeDtypeStruct((depth, HEAD_DIM), f32)] * full + [piece] * (2 if cut else 0),
        scratch_shapes=[pltpu.VMEM((rows * len(xs), 2 * parts * HEAD_DIM), bf16)],
        compiler_params=pltpu.CompilerParams(vmem_limit_bytes=VMEM_LIMIT),
        cost_estimate=pl.CostEstimate(
            flops=6 * rows * len(xs) * depth * parts * HEAD_DIM, bytes_accessed=4 * rows * len(xs) * depth, transcendentals=0
        ),
    )(place, *xs, grads)


def list_blocks(own_ref, fork_ref, offset_ref, limit_ref, step, tok, owners, halves, tiles, paired):
    branch_slot = step // halves
    half = step % halves
    branch = tok ^ branch_slot
    for block in range(halves):
        offset_ref[block] = (owners + branch_slot * halves + block) * SPAN
        limit_ref[block] = -1
    own_count = half + 1

    def climb(_, carry):
        current, count = carry
        fork_at = fork_ref[jnp.maximum(current - 1, 0)]
        parent = lax.div(fork_at, jnp.int32(tiles))
        inside = lax.rem(fork_at, jnp.int32(tiles))

        @pl.when(current > 0)
        def _():
            offset_ref[count] = ((tok ^ parent) if paired else parent) * SPAN
            limit_ref[count] = (inside + 1) * TILE - 1

        return jnp.where(current > 0, parent, 0), count + (current > 0).astype(jnp.int32)

    _, count = lax.fori_loop(0, owners, climb, (branch, own_count))
    return branch, branch_slot, half, count, own_count


def key_limits(block, limit_ref, own_count, half, live, lanes):
    lane = lax.broadcasted_iota(jnp.int32, (1, lanes), 1)
    position = half * SPAN + lax.rem(lane, jnp.int32(SPAN))
    own_limit = jnp.minimum(position, live - 1) - block * SPAN
    return jnp.where(block < own_count, own_limit, limit_ref[block])


def transposed_pair(rows):
    high, low = split(rows.T)
    return jnp.concatenate([high, high, low, low], axis=0)


def load_rows(ref, half, head):
    return ref[pl.ds(pl.multiple_of(half * SPAN, SPAN), SPAN), head * HEAD_DIM : (head + 1) * HEAD_DIM]


def live_column(half, live):
    position = half * SPAN + lax.broadcasted_iota(jnp.int32, (SPAN, 1), 0)
    return (position < live).astype(f32)


def block_rows(ref, offset):
    return ref[pl.ds(pl.multiple_of(offset, SPAN), SPAN), :]


def slot_rows(block):
    return pl.ds(pl.multiple_of(block * SPAN, SPAN), SPAN)


def stage_rows(target_ref, source_refs, layout):
    for index, start, offset, count in layout:
        for piece in range(0, count, SPAN):
            target_ref[offset + piece : offset + piece + SPAN, :] = pair_cat(
                source_refs[index][:, start + piece : start + piece + SPAN].T, 1
            )


def write_rows(source_ref, target_refs, layout):
    for index, start, offset, count in layout:
        if index > 0:
            target_refs[index - 1][start : start + count, :] = source_ref[offset : offset + count, :]
    own = layout[0]
    target_refs[-1][...] = source_ref[own[2] : own[2] + own[3], :]
    for index, start, offset, count in layout[1:]:
        if index == 0:
            target_refs[-1][start : start + count, :] += source_ref[offset : offset + count, :]


def scores(keys_ref, offset, queries, limits):
    keys = block_rows(keys_ref, offset)
    result = dot(jnp.concatenate([keys, keys], axis=1), queries)
    row = lax.broadcasted_iota(jnp.int32, result.shape, 0)
    return jnp.where(row <= limits, result, -1e30)


def fold(value, how):
    return how(value.reshape(SPAN // 8, 8, value.shape[1]), axis=0)


def soft_body(tok_ref, fork_ref, live_ref, *refs, conf):
    nb, group, owners, layout, sources, outs = conf["nb"], conf["group"], conf["owners"], conf["layout"], conf["sources"], conf["outs"]
    halves = conf["rows"] // SPAN
    lanes = group * SPAN
    q_refs, g_refs = refs[:nb], refs[nb : 2 * nb]
    key_refs = refs[2 * nb : 2 * nb + sources]
    prob_ref = refs[2 * nb + sources]
    out_refs = refs[2 * nb + sources + 1 : 2 * nb + sources + 1 + outs]
    keys_ref, sum_ref, score_ref, qt_ref, grad_ref, offset_ref, limit_ref = refs[2 * nb + sources + 1 + outs :]
    step = pl.program_id(0)
    tok = tok_ref[0]

    @pl.when(step == 0)
    def _():
        stage_rows(keys_ref, key_refs, layout)
        sum_ref[...] = jnp.zeros_like(sum_ref)

    branch, slot, half, count, own_count = list_blocks(
        tok_ref, fork_ref, offset_ref, limit_ref, step, tok, owners, halves, conf["rows"] // TILE, conf["paired"]
    )
    live = live_ref[branch]
    for source in range(nb):

        @pl.when(slot == source)
        def _():
            for head in range(group):
                qt_ref[:, head * SPAN : (head + 1) * SPAN] = transposed_pair(load_rows(q_refs[source], half, head) * logit_scale)
                grad_ref[head * SPAN : (head + 1) * SPAN, :] = pair_cat(
                    load_rows(g_refs[source], half, head) * live_column(half, live), 1
                )

    def first(block, largest):
        value = scores(keys_ref, offset_ref[block], qt_ref[...], key_limits(block, limit_ref, own_count, half, live, lanes))
        score_ref[slot_rows(block), :] = value
        return jnp.maximum(largest, fold(value, jnp.max))

    largest = lax.fori_loop(0, count, first, jnp.full((8, lanes), -1e30, f32))
    largest = jnp.max(largest, axis=0, keepdims=True)

    def second(block, total):
        value = jnp.exp(score_ref[slot_rows(block), :] - largest)
        score_ref[slot_rows(block), :] = value
        return total + fold(value, jnp.sum)

    total = lax.fori_loop(0, count, second, jnp.zeros((8, lanes), f32))
    inverse = 1.0 / jnp.sum(total, axis=0, keepdims=True)

    def third(block, _):
        prob = score_ref[slot_rows(block), :] * inverse
        prob_ref[0, slot_rows(block), :] = prob
        high, low = split(prob)
        grads = grad_ref[...]
        both = dot(high, grads) + dot(low, grads)
        offset = offset_ref[block]
        sum_ref[slot_rows(offset // SPAN), :] += both[:, :HEAD_DIM] + both[:, HEAD_DIM:]
        return 0

    lax.fori_loop(0, count, third, 0)

    @pl.when(step == nb * halves - 1)
    def _():
        write_rows(sum_ref, out_refs, layout)


def grad_body(tok_ref, fork_ref, live_ref, *refs, conf):
    nb, group, owners, layout, sources, outs = conf["nb"], conf["group"], conf["owners"], conf["layout"], conf["sources"], conf["outs"]
    halves = conf["rows"] // SPAN
    lanes = group * SPAN
    q_refs, g_refs = refs[:nb], refs[nb : 2 * nb]
    at = 2 * nb
    key_refs, value_refs = refs[at : at + sources], refs[at + sources : at + 2 * sources]
    at += 2 * sources
    prob_ref = refs[at]
    dq_ref = refs[at + 1]
    out_refs = refs[at + 2 : at + 2 + outs]
    (keys_ref, values_ref, sum_ref, dprob_ref, gt_ref, q_ref, dqt_ref, offset_ref, limit_ref) = refs[at + 2 + outs :]
    step = pl.program_id(0)
    tok = tok_ref[0]

    @pl.when(step == 0)
    def _():
        stage_rows(keys_ref, key_refs, layout)
        stage_rows(values_ref, value_refs, layout)
        sum_ref[...] = jnp.zeros_like(sum_ref)

    branch, slot, half, count, own_count = list_blocks(
        tok_ref, fork_ref, offset_ref, limit_ref, step, tok, owners, halves, conf["rows"] // TILE, conf["paired"]
    )
    live = live_ref[branch]
    for source in range(nb):

        @pl.when(slot == source)
        def _():
            for head in range(group):
                rows = load_rows(q_refs[source], half, head) * logit_scale
                q_ref[head * SPAN : (head + 1) * SPAN, :] = pair_cat(rows, 1)
                gt_ref[:, head * SPAN : (head + 1) * SPAN] = transposed_pair(
                    load_rows(g_refs[source], half, head) * live_column(half, live)
                )

    def first(block, delta):
        values = block_rows(values_ref, offset_ref[block])
        dprob = dot(jnp.concatenate([values, values], axis=1), gt_ref[...])
        dprob_ref[slot_rows(block), :] = dprob
        return delta + fold(prob_ref[0, slot_rows(block), :] * dprob, jnp.sum)

    delta = lax.fori_loop(0, count, first, jnp.zeros((8, lanes), f32))
    delta = jnp.sum(delta, axis=0, keepdims=True)
    dqt_ref[...] = jnp.zeros_like(dqt_ref)

    def second(block, _):
        offset = offset_ref[block]
        high, low = split(prob_ref[0, slot_rows(block), :] * (dprob_ref[slot_rows(block), :] - delta))
        rows = q_ref[...]
        both = dot(high, rows) + dot(low, rows)
        sum_ref[slot_rows(offset // SPAN), :] += both[:, :HEAD_DIM] + both[:, HEAD_DIM:]
        keys = block_rows(keys_ref, offset)
        dqt_ref[...] += dot_first(keys, high) + dot_first(keys, low)
        return 0

    lax.fori_loop(0, count, second, 0)
    folded = (dqt_ref[:HEAD_DIM, :] + dqt_ref[HEAD_DIM:, :]) * logit_scale
    for head in range(group):
        dq_ref[:, head * HEAD_DIM : (head + 1) * HEAD_DIM] = folded[:, head * SPAN : (head + 1) * SPAN].T

    @pl.when(step == nb * halves - 1)
    def _():
        write_rows(sum_ref, out_refs, layout)


def attention_calls(scalars, qs, gs, layout, paired, owners, part_rows):
    rows, width = qs[0].shape
    nb, group, halves = len(qs), width // HEAD_DIM, rows // SPAN
    lanes = group * SPAN
    steps = nb * halves
    conf = dict(nb=nb, group=group, rows=rows, owners=owners, layout=layout, paired=paired, sources=1 + len(part_rows), outs=len(part_rows) + 1)
    table_rows = owners * SPAN + nb * rows
    slots = (owners - 1 + halves) * SPAN
    sums = [jax.ShapeDtypeStruct((count, HEAD_DIM), f32) for count in part_rows] + [jax.ShapeDtypeStruct((nb * rows, HEAD_DIM), f32)]
    probs = jax.ShapeDtypeStruct((steps, slots, lanes), f32)
    probs_spec = pl.BlockSpec((1, slots, lanes), lambda step: (step, 0, 0))
    table = pltpu.VMEM((table_rows, 2 * HEAD_DIM), bf16)
    table_sum = pltpu.VMEM((table_rows, HEAD_DIM), f32)
    square = pltpu.VMEM((slots, lanes), f32)
    columns = pltpu.VMEM((4 * HEAD_DIM, lanes), bf16)
    lists = [pltpu.SMEM((owners + halves + 1,), jnp.int32)] * 2
    params = pltpu.CompilerParams(vmem_limit_bytes=VMEM_LIMIT)
    work = 2 * steps * 6 * SPAN * lanes * 2 * HEAD_DIM

    def soft(keys):
        return pl.pallas_call(
            functools.partial(soft_body, conf=conf),
            grid=(steps,),
            in_specs=[smem_spec] * 3 + [whole_spec(a) for a in (*qs, *gs, *keys)],
            out_specs=[probs_spec] + [whole_spec(a) for a in sums],
            out_shape=[probs] + sums,
            scratch_shapes=[table, table_sum, square, columns, pltpu.VMEM((lanes, 2 * HEAD_DIM), bf16)] + lists,
            compiler_params=params,
            cost_estimate=pl.CostEstimate(flops=2 * work, bytes_accessed=4 * rows * width, transcendentals=0),
        )(*scalars, *qs, *gs, *keys)

    def grad(keys, values, probs_in):
        dq = jax.ShapeDtypeStruct((nb * rows, width), f32)
        return pl.pallas_call(
            functools.partial(grad_body, conf=conf),
            grid=(steps,),
            in_specs=[smem_spec] * 3 + [whole_spec(a) for a in (*qs, *gs, *keys, *values)] + [probs_spec],
            out_specs=[pl.BlockSpec((SPAN, width), lambda step: (step, 0))] + [whole_spec(a) for a in sums],
            out_shape=[dq] + sums,
            scratch_shapes=[
                table,
                table,
                table_sum,
                square,
                columns,
                pltpu.VMEM((lanes, 2 * HEAD_DIM), bf16),
                pltpu.VMEM((2 * HEAD_DIM, lanes), f32),
            ]
            + lists,
            compiler_params=params,
            cost_estimate=pl.CostEstimate(flops=4 * work, bytes_accessed=4 * rows * width, transcendentals=0),
        )(*scalars, *qs, *gs, *keys, *values, probs_in)

    return soft, grad


def flip(array, mask):
    count = lax.axis_size("tok")
    return lax.ppermute(array, "tok", [(index, index ^ mask) for index in range(count)])


def together(*arrays):
    return lax.optimization_barrier(arrays)


def gather_square(array, cut, axis):
    across, down = flip(array, 2), flip(array, 4)
    head = lax.slice_in_dim(across, 0, cut, axis=axis)
    tail = lax.slice_in_dim(down, cut, down.shape[axis], axis=axis)
    return across, down, flip(head, 4), flip(tail, 2)


def scatter_square(across, down, head, tail):
    cut = head.shape[0]
    from_across, from_down = flip(head, 2), flip(tail, 4)
    down = down.at[:cut].add(from_across)
    across = across.at[cut:].add(from_down)
    return flip(across, 2), flip(down, 4)


def shards_paired(hidden, queries, out_grad, w_key, w_value, fork_tile, live_len):
    owners = lax.axis_size("tok")
    depth = lax.axis_size("head")
    tok = lax.axis_index("tok").astype(jnp.int32)
    core = tok & 1
    rows = hidden.shape[0]
    width = queries.shape[1] // 2
    scalars = (tok.reshape(1), fork_tile, live_len)
    place = (tok >> 1) ^ jnp.arange(depth, dtype=jnp.int32)
    cut = w_key.shape[0] // (2 * HEAD_DIM) * HEAD_DIM
    weights = ((0, 0), (1, 0), (2, 0), (3, 0), (3, cut))

    def mine(array):
        return lax.dynamic_slice_in_dim(array, core * width, width, 1)

    def partners(array):
        return flip(lax.dynamic_slice_in_dim(array, (1 - core) * width, width, 1), 1)

    def sum_heads(partial):
        return lax.psum_scatter(partial, "head", scatter_dimension=0, tiled=True)[0]

    def all_heads(grads):
        return lax.all_gather(grads, "head", axis=0, tiled=False)

    def lead(array):
        return jnp.concatenate([array[:, :SPAN], array[:, rows : rows + SPAN]], axis=1)

    def returned(own, across, down, head, tail):
        first, second = scatter_square(across, down, head, tail)
        both = first + second
        return own.at[:SPAN].add(both[:SPAN]).at[rows : rows + SPAN].add(both[SPAN:])

    def weight(every):
        own, *others = weight_grad(place, xs, every, True)
        first, second = scatter_square(*others)
        return own + first + second

    def home(array):
        kept, received = array[:rows], flip(array[rows:], 1)
        return jnp.where(core == 0, jnp.concatenate([kept, received], axis=1), jnp.concatenate([received, kept], axis=1))

    hidden = hidden.T
    xs = [hidden, flip(hidden, 1)]
    qs = [mine(queries), partners(queries)]
    gs = [mine(out_grad), partners(out_grad)]
    keys = sum_heads(project(place, xs, [w_key, *gather_square(w_key, cut, 0)], weights))
    values = sum_heads(project(place, xs, [w_value, *gather_square(w_value, cut, 0)], weights))

    base = owners * SPAN
    layout = (
        (0, 0, base, 2 * rows),
        (0, 0, 0, SPAN),
        (0, rows, SPAN, SPAN),
        (1, 0, 2 * SPAN, 2 * SPAN),
        (2, 0, 4 * SPAN, 2 * SPAN),
        (3, 0, 6 * SPAN, SPAN),
        (4, 0, 7 * SPAN, SPAN),
    )
    soft, grad = attention_calls(scalars, qs, gs, layout, True, owners, (2 * SPAN, 2 * SPAN, SPAN, SPAN))

    key_parts = [keys, *gather_square(lead(keys), SPAN, 1)]
    probs, *value_sums = soft(key_parts)
    values, probs = together(values, probs)
    value_parts = [values, *gather_square(lead(values), SPAN, 1)]
    value_grads = returned(value_sums[-1], *value_sums[:-1])
    every_value = all_heads(value_grads)
    probs, value_grads = together(probs, value_grads)
    grad_query, *key_sums = grad(key_parts, value_parts, probs)
    key_grads = returned(key_sums[-1], *key_sums[:-1])
    every_key = all_heads(key_grads)
    every_value, key_grads = together(every_value, key_grads)
    grad_w_value = weight(every_value)
    grad_query, grad_key, grad_value = home(grad_query), home(key_grads), home(value_grads)
    every_key, grad_w_value, grad_query, grad_key, grad_value = together(every_key, grad_w_value, grad_query, grad_key, grad_value)
    grad_w_key = weight(every_key)
    return grad_query, grad_key, grad_value, grad_w_key, grad_w_value


def shards_single(hidden, queries, out_grad, w_key, w_value, fork_tile, live_len):
    owners = lax.axis_size("tok")
    depth = lax.axis_size("head")
    tok = lax.axis_index("tok").astype(jnp.int32)
    scalars = (tok.reshape(1), fork_tile, live_len)
    place = jnp.arange(depth, dtype=jnp.int32)
    hidden = hidden.T

    def projected(w):
        every = lax.all_gather(w, "tok", axis=1, tiled=True)
        pieces = [every[:, index * HEAD_DIM : (index + 1) * HEAD_DIM] for index in range(depth)]
        partial = project(place, [hidden], pieces, tuple((index, 0) for index in range(depth)))
        return lax.psum_scatter(partial, "head", scatter_dimension=0, tiled=True)[0]

    keys, values = projected(w_key), projected(w_value)
    layout = ((0, 0, owners * SPAN, hidden.shape[1]), (1, 0, 0, owners * SPAN))
    soft, grad = attention_calls(scalars, [queries], [out_grad], layout, False, owners, (owners * SPAN,))

    def parts(array):
        return [array, lax.all_gather(array[:, :SPAN], "tok", axis=1, tiled=True)]

    def returned(remote, own):
        return own.at[:SPAN].add(lax.psum_scatter(remote, "tok", scatter_dimension=0, tiled=True))

    def weight(grads):
        every = lax.all_gather(grads, "head", axis=0, tiled=False)
        columns = jnp.concatenate(weight_grad(place, [hidden], every, False), axis=1)
        return lax.psum_scatter(columns, "tok", scatter_dimension=1, tiled=True)

    key_parts = parts(keys)
    probs, *value_sums = soft(key_parts)
    value_grads = returned(*value_sums)
    grad_query, *key_sums = grad(key_parts, parts(values), probs)
    key_grads = returned(*key_sums)
    return grad_query, key_grads, value_grads, weight(key_grads), weight(value_grads)


def solution(mesh):
    owners, depth = mesh.shape["tok"], mesh.shape["head"]
    paired = owners == 8 and depth == 4

    placed = (P("tok", "head"), P("tok", "head"), P("tok", "head"), P("head", "tok"), P("head", "tok"), P(), P())
    return jax.shard_map(
        shards_paired if paired else shards_single,
        mesh=mesh,
        in_specs=placed,
        out_specs=(P("tok", "head"), P("tok", "head"), P("tok", "head"), P("head", "tok"), P("head", "tok")),
        check_vma=False,
    )
```

```python
import functools

import jax
import jax.numpy as jnp
from jax import lax
from jax.experimental import pallas as pl
from jax.experimental.pallas import tpu as pltpu
from jax.sharding import PartitionSpec as P

HEAD_DIM = 128
TILE = 128
CAP = 2
SPAN = CAP * TILE

logit_scale = 168.0 ** (-0.5)
f32 = jnp.float32
bf16 = jnp.bfloat16
MIB = 1024 * 1024


def split(rows):
    high = rows.astype(bf16)
    return high, (rows - high.astype(f32)).astype(bf16)


def pair_cat(rows, axis):
    return jnp.concatenate(split(rows), axis=axis)


def dot(left, right):
    return jnp.dot(left, right, preferred_element_type=f32)


def dot_first(left, right):
    return lax.dot_general(left, right, (((0,), (0,)), ((), ())), preferred_element_type=f32)


def whole_spec(array):
    return pl.BlockSpec(array.shape, lambda *_: (0,) * len(array.shape))


smem_spec = pl.BlockSpec(memory_space=pltpu.SMEM)


def project_body(place_ref, *refs, row_inputs, pieces, parts, steps_each):
    x_refs = refs[:row_inputs]
    w_refs = refs[row_inputs : row_inputs + len(pieces)]
    out_ref, pair_ref, x_ref = refs[-3:]
    step, part_step = pl.program_id(0), pl.program_id(1)
    columns = x_refs[0].shape[1]

    @pl.when((step == 0) & (part_step == 0))
    def _():
        for (part, start), w_ref in zip(pieces, w_refs):
            high, low = split(w_ref[...].T)
            stop = start + w_ref.shape[0]
            pair_ref[part, :HEAD_DIM, start:stop] = high
            pair_ref[part, HEAD_DIM:, start:stop] = low

    for source in range(row_inputs):

        @pl.when((step // steps_each == source) & (part_step == 0))
        def _():
            high, low = split(x_refs[source][...])
            x_ref[:, :columns] = high
            x_ref[:, columns:] = low

    total = dot(pair_ref[part_step], x_ref[...])
    total = total[:, :columns] + total[:, columns:]
    out_ref[0] = total[:HEAD_DIM] + total[HEAD_DIM:]


def project(place, slots, xs, pieces, ws, before=None):
    depth, rows = xs[0].shape
    block = 256
    steps_each = rows // block
    first = slots[0]

    def x_map(source):
        return lambda step, part, place_ref: (0, jnp.clip(step - source * steps_each, 0, steps_each - 1))

    extra = [] if before is None else [before]
    return pl.pallas_call(
        functools.partial(project_body, row_inputs=len(xs), pieces=pieces, parts=len(slots), steps_each=steps_each),
        grid_spec=pltpu.PrefetchScalarGridSpec(
            num_scalar_prefetch=1,
            grid=(steps_each * len(xs), len(slots)),
            in_specs=[pl.BlockSpec((depth, block), x_map(source)) for source in range(len(xs))]
            + [whole_spec(w) for w in ws]
            + [pl.BlockSpec(memory_space=pl.ANY)] * len(extra),
            out_specs=pl.BlockSpec((1, HEAD_DIM, block), lambda step, part, place_ref: (place_ref[first + part], 0, step)),
            scratch_shapes=[pltpu.VMEM((len(slots), 2 * HEAD_DIM, depth), bf16), pltpu.VMEM((depth, 2 * block), bf16)],
        ),
        out_shape=jax.ShapeDtypeStruct((place.shape[0], HEAD_DIM, rows * len(xs)), f32),
        input_output_aliases={1 + len(xs) + len(ws): 0} if extra else {},
        compiler_params=pltpu.CompilerParams(vmem_limit_bytes=24 * MIB),
        cost_estimate=pl.CostEstimate(
            flops=6 * rows * len(xs) * depth * len(slots) * HEAD_DIM, bytes_accessed=4 * rows * len(xs) * depth, transcendentals=0
        ),
    )(place, *xs, *ws, *extra)


def weight_grad_body(place_ref, *refs, row_inputs, parts):
    x_refs = refs[:row_inputs]
    g_refs = refs[row_inputs : row_inputs + parts]
    out_refs, pair_ref = refs[row_inputs + parts : -1], refs[-1]
    rows = x_refs[0].shape[1]
    step, half = pl.program_id(0), pl.num_programs(0) // 2

    @pl.when(step == 0)
    def _():
        for part in range(parts):
            pair_ref[:, 2 * part * HEAD_DIM : 2 * (part + 1) * HEAD_DIM] = pair_cat(g_refs[part][0], 1)

    total = 0.0
    for source in range(row_inputs):
        high, low = split(x_refs[source][...])
        pair = pair_ref[source * rows : (source + 1) * rows]
        total += dot(high, pair) + dot(low, pair)
    for part in range(parts):
        value = total[:, 2 * part * HEAD_DIM : (2 * part + 1) * HEAD_DIM] + total[:, (2 * part + 1) * HEAD_DIM : 2 * (part + 1) * HEAD_DIM]
        for piece in range(2):

            @pl.when(step // half == piece)
            def _():
                out_refs[2 * part + piece][...] = value


def weight_grad(place, slots, xs, grads):
    depth, rows = xs[0].shape
    parts = len(slots)
    steps = 4
    half = steps // 2
    block = depth // steps

    def g_map(slot):
        return lambda step, place_ref: (place_ref[slot], 0, 0)

    head = pl.BlockSpec((block, HEAD_DIM), lambda step, place_ref: (jnp.minimum(step, half - 1), 0))
    tail = pl.BlockSpec((block, HEAD_DIM), lambda step, place_ref: (jnp.maximum(step - half, 0), 0))
    return pl.pallas_call(
        functools.partial(weight_grad_body, row_inputs=len(xs), parts=parts),
        grid_spec=pltpu.PrefetchScalarGridSpec(
            num_scalar_prefetch=1,
            grid=(steps,),
            in_specs=[pl.BlockSpec((block, rows), lambda step, place_ref: (step, 0))] * len(xs)
            + [pl.BlockSpec((1, *grads.shape[1:]), g_map(slot)) for slot in slots],
            out_specs=[head, tail] * parts,
            scratch_shapes=[pltpu.VMEM((rows * len(xs), 2 * parts * HEAD_DIM), bf16)],
        ),
        out_shape=[jax.ShapeDtypeStruct((block * half, HEAD_DIM), f32)] * (2 * parts),
        compiler_params=pltpu.CompilerParams(vmem_limit_bytes=24 * MIB),
        cost_estimate=pl.CostEstimate(
            flops=6 * rows * len(xs) * depth * parts * HEAD_DIM, bytes_accessed=4 * rows * len(xs) * depth, transcendentals=0
        ),
    )(place, *xs, *[grads] * parts)


def combine_body(own_ref, *refs, starts):
    out_ref = refs[-1]
    out_ref[...] = own_ref[...]
    for index, start in enumerate(starts):
        first, second = refs[2 * index], refs[2 * index + 1]
        out_ref[start : start + first.shape[0], :] += first[...] + second[...]


def combine(own, starts, arrivals):
    return pl.pallas_call(
        functools.partial(combine_body, starts=starts),
        out_shape=jax.ShapeDtypeStruct(own.shape, f32),
        compiler_params=pltpu.CompilerParams(vmem_limit_bytes=24 * MIB),
        cost_estimate=pl.CostEstimate(flops=own.size, bytes_accessed=12 * own.size, transcendentals=0),
    )(own, *arrivals)


def list_ancestors(fork_ref, offset_ref, limit_ref, many_ref, tok, slots, tiles, paired):
    for slot in range(slots):

        def climb(carry, slot=slot):
            current, count = carry
            fork_at = fork_ref[current - 1]
            parent = lax.div(fork_at, jnp.int32(tiles))
            offset_ref[slot, count] = ((tok ^ parent) if paired else parent) * SPAN
            limit_ref[slot, count] = (lax.rem(fork_at, jnp.int32(tiles)) + 1) * TILE - 1
            return parent, count + 1

        _, count = lax.while_loop(lambda carry: carry[0] > 0, climb, (tok ^ slot, jnp.int32(0)))
        many_ref[slot] = count
        offset_ref[slot, count] = 0
        limit_ref[slot, count] = -1


def find_step(many_ref, step, tok, halves):
    slot, half = lax.div(step, jnp.int32(halves)), lax.rem(step, jnp.int32(halves))
    return tok ^ slot, slot, half, half + 1 + many_ref[slot]


def block_offset(offset_ref, base, slot, half, halves, block):
    later = jnp.maximum(block - half - 1, 0)
    return jnp.where(block <= half, base + (slot * halves + block) * SPAN, offset_ref[slot, later])


def even(count):
    return 2 * lax.div(count + 1, jnp.int32(2))


def paired_loop(count, body, start, before=None):
    def both(pair, carry):
        if before is not None:
            before(2 * pair)
            before(2 * pair + 1)
        return body(2 * pair + 1, body(2 * pair, carry))

    return lax.fori_loop(0, lax.div(count + 1, jnp.int32(2)), both, start)


def key_limits(limit_ref, slot, half, live, block, lanes):
    lane = lax.broadcasted_iota(jnp.int32, (1, lanes), 1)
    position = half * SPAN + lax.rem(lane, jnp.int32(SPAN))
    own_limit = jnp.minimum(position, live - 1) - block * SPAN
    return jnp.where(block <= half, own_limit, limit_ref[slot, jnp.maximum(block - half - 1, 0)])


def transposed_pair(rows):
    high, low = split(rows.T)
    return jnp.concatenate([high, high, low, low], axis=0)


def load_rows(ref, half, head):
    return ref[pl.ds(pl.multiple_of(half * SPAN, SPAN), SPAN), head * HEAD_DIM : (head + 1) * HEAD_DIM]


def live_column(half, live):
    position = half * SPAN + lax.broadcasted_iota(jnp.int32, (SPAN, 1), 0)
    return (position < live).astype(f32)


def block_rows(ref, offset):
    return ref[pl.ds(pl.multiple_of(offset, SPAN), SPAN), :]


def slot_rows(block):
    return pl.ds(pl.multiple_of(block * SPAN, SPAN), SPAN)


def stage_rows(target_ref, source_refs, layout):
    for index, start, offset, count in layout:
        for piece in range(0, count, SPAN):
            target_ref[offset + piece : offset + piece + SPAN, :] = pair_cat(
                source_refs[index][:, start + piece : start + piece + SPAN].T, 1
            )


def write_rows(source_ref, target_refs, layout, sums):
    for target_ref, (start, offset, count) in zip(target_refs, sums):
        target_ref[start : start + count, :] = source_ref[offset : offset + count, :]
    own = layout[0]
    target_refs[-1][...] = source_ref[own[2] : own[2] + own[3], :]
    for index, start, offset, count in layout[1:]:
        if index == 0:
            target_refs[-1][start : start + count, :] += source_ref[offset : offset + count, :]


def scores(keys_ref, offset, queries, limits):
    keys = block_rows(keys_ref, offset)
    result = dot(jnp.concatenate([keys, keys], axis=1), queries)
    row = lax.broadcasted_iota(jnp.int32, result.shape, 0)
    return jnp.where(row <= limits, result, -1e30)


def fold(value, how):
    return how(value.reshape(SPAN // 8, 8, value.shape[1]), axis=0)


def soft_body(tok_ref, fork_ref, live_ref, *refs, conf):
    nb, group, owners, layout, sources, outs = conf["nb"], conf["group"], conf["owners"], conf["layout"], conf["sources"], conf["outs"]
    halves = conf["rows"] // SPAN
    lanes = group * SPAN
    q_refs, g_refs = refs[:nb], refs[nb : 2 * nb]
    key_refs = refs[2 * nb : 2 * nb + sources]
    prob_ref = refs[2 * nb + sources]
    out_refs = refs[2 * nb + sources + 1 : 2 * nb + sources + 1 + outs]
    keys_ref, sum_ref, scores_ref, qt_ref, grad_ref, offset_ref, limit_ref, many_ref, sems = refs[2 * nb + sources + 1 + outs :]
    step = pl.program_id(0)
    tok = tok_ref[0]
    turn = lax.rem(step, 2)
    score_ref = scores_ref.at[turn]

    def copy_out(of_step, block):
        side = lax.rem(of_step, 2)
        rows = slot_rows(block)
        return pltpu.make_async_copy(scores_ref.at[side, rows], prob_ref.at[of_step, rows], sems.at[side, block])

    def wait_out(of_step):
        def wait(block, _):
            copy_out(of_step, block).wait()
            return 0

        lax.fori_loop(0, even(find_step(many_ref, of_step, tok, halves)[3]), wait, 0)

    @pl.when(step == 0)
    def _():
        list_ancestors(fork_ref, offset_ref, limit_ref, many_ref, tok, nb, conf["rows"] // TILE, conf["paired"])
        stage_rows(keys_ref, key_refs, layout)
        sum_ref[...] = jnp.zeros_like(sum_ref)

    branch, slot, half, count = find_step(many_ref, step, tok, halves)
    place_of = functools.partial(block_offset, offset_ref, owners * SPAN, slot, half, halves)
    live = live_ref[branch]
    for source in range(nb):

        @pl.when(slot == source)
        def _():
            for head in range(group):
                qt_ref[:, head * SPAN : (head + 1) * SPAN] = transposed_pair(load_rows(q_refs[source], half, head) * logit_scale)
                grad_ref[head * SPAN : (head + 1) * SPAN, :] = pair_cat(
                    load_rows(g_refs[source], half, head) * live_column(half, live), 1
                )

    def first(block, largest):
        value = scores(keys_ref, place_of(block), qt_ref[...], key_limits(limit_ref, slot, half, live, block, lanes))
        score_ref[slot_rows(block), :] = value
        return jnp.maximum(largest, fold(value, jnp.max))

    largest = paired_loop(count, first, jnp.full((8, lanes), -1e30, f32))
    largest = jnp.max(largest, axis=0, keepdims=True)

    def second(block, total):
        value = jnp.exp(score_ref[slot_rows(block), :] - largest)
        score_ref[slot_rows(block), :] = value
        return total + fold(value, jnp.sum)

    total = paired_loop(count, second, jnp.zeros((8, lanes), f32))
    inverse = 1.0 / jnp.sum(total, axis=0, keepdims=True)

    def third(block, _):
        prob = score_ref[slot_rows(block), :] * inverse
        score_ref[slot_rows(block), :] = prob
        copy_out(step, block).start()
        high, low = split(prob)
        grads = grad_ref[...]
        both = dot(high, grads) + dot(low, grads)
        offset = place_of(block)
        sum_ref[slot_rows(offset // SPAN), :] += both[:, :HEAD_DIM] + both[:, HEAD_DIM:]
        return 0

    paired_loop(count, third, 0)

    @pl.when(step > 0)
    def _():
        wait_out(step - 1)

    @pl.when(step == nb * halves - 1)
    def _():
        wait_out(step)
        write_rows(sum_ref, out_refs, layout, conf["sums"])


def grad_body(tok_ref, fork_ref, live_ref, *refs, conf):
    nb, group, owners, layout, sources, outs = conf["nb"], conf["group"], conf["owners"], conf["layout"], conf["sources"], conf["outs"]
    halves = conf["rows"] // SPAN
    lanes = group * SPAN
    q_refs, g_refs = refs[:nb], refs[nb : 2 * nb]
    at = 2 * nb
    key_refs, value_refs = refs[at : at + sources], refs[at + sources : at + 2 * sources]
    at += 2 * sources
    prob_ref = refs[at]
    dq_ref = refs[at + 1]
    out_refs = refs[at + 2 : at + 2 + outs]
    (keys_ref, values_ref, sum_ref, probs_ref, dprob_ref, gt_ref, q_ref, dqt_ref, offset_ref, limit_ref, many_ref, sems) = refs[at + 2 + outs :]
    step = pl.program_id(0)
    tok = tok_ref[0]
    held_ref = probs_ref.at[lax.rem(step, 2)]

    def copy_in(of_step, block):
        side = lax.rem(of_step, 2)
        rows = slot_rows(block)
        return pltpu.make_async_copy(prob_ref.at[of_step, rows], probs_ref.at[side, rows], sems.at[side, block])

    def start_in(of_step):
        def start(block, _):
            copy_in(of_step, block).start()
            return 0

        lax.fori_loop(0, even(find_step(many_ref, of_step, tok, halves)[3]), start, 0)

    @pl.when(step == 0)
    def _():
        list_ancestors(fork_ref, offset_ref, limit_ref, many_ref, tok, nb, conf["rows"] // TILE, conf["paired"])
        start_in(step)
        stage_rows(keys_ref, key_refs, layout)
        stage_rows(values_ref, value_refs, layout)
        sum_ref[...] = jnp.zeros_like(sum_ref)

    @pl.when(step < nb * halves - 1)
    def _():
        start_in(step + 1)

    branch, slot, half, count = find_step(many_ref, step, tok, halves)
    place_of = functools.partial(block_offset, offset_ref, owners * SPAN, slot, half, halves)
    live = live_ref[branch]
    for source in range(nb):

        @pl.when(slot == source)
        def _():
            for head in range(group):
                rows = load_rows(q_refs[source], half, head) * logit_scale
                q_ref[head * SPAN : (head + 1) * SPAN, :] = pair_cat(rows, 1)
                gt_ref[:, head * SPAN : (head + 1) * SPAN] = transposed_pair(
                    load_rows(g_refs[source], half, head) * live_column(half, live)
                )

    def first(block, delta):
        values = block_rows(values_ref, place_of(block))
        dprob = dot(jnp.concatenate([values, values], axis=1), gt_ref[...])
        dprob_ref[slot_rows(block), :] = dprob
        return delta + fold(held_ref[slot_rows(block), :] * dprob, jnp.sum)

    delta = paired_loop(count, first, jnp.zeros((8, lanes), f32), lambda block: copy_in(step, block).wait())
    delta = jnp.sum(delta, axis=0, keepdims=True)
    dqt_ref[...] = jnp.zeros_like(dqt_ref)

    def second(block, _):
        offset = place_of(block)
        high, low = split(held_ref[slot_rows(block), :] * (dprob_ref[slot_rows(block), :] - delta))
        rows = q_ref[...]
        both = dot(high, rows) + dot(low, rows)
        sum_ref[slot_rows(offset // SPAN), :] += both[:, :HEAD_DIM] + both[:, HEAD_DIM:]
        keys = block_rows(keys_ref, offset)
        dqt_ref[...] += dot_first(keys, high) + dot_first(keys, low)
        return 0

    paired_loop(count, second, 0)
    folded = (dqt_ref[:HEAD_DIM, :] + dqt_ref[HEAD_DIM:, :]) * logit_scale
    for head in range(group):
        dq_ref[:, head * HEAD_DIM : (head + 1) * HEAD_DIM] = folded[:, head * SPAN : (head + 1) * SPAN].T

    @pl.when(step == nb * halves - 1)
    def _():
        write_rows(sum_ref, out_refs, layout, conf["sums"])


def attention_calls(scalars, qs, gs, layout, sum_rows, paired, owners, parts):
    rows, width = qs[0].shape
    nb, group, halves = len(qs), width // HEAD_DIM, rows // SPAN
    lanes = group * SPAN
    steps = nb * halves
    conf = dict(nb=nb, group=group, rows=rows, owners=owners, layout=layout, paired=paired, sources=1 + parts, sums=sum_rows, outs=len(sum_rows) + 1)
    table_rows = owners * SPAN + nb * rows
    slots = (owners + halves) * SPAN
    sums = [jax.ShapeDtypeStruct((count, HEAD_DIM), f32) for _, _, count in sum_rows] + [jax.ShapeDtypeStruct((nb * rows, HEAD_DIM), f32)]
    probs = jax.ShapeDtypeStruct((steps, slots, lanes), f32)
    probs_spec = pl.BlockSpec(memory_space=pl.ANY)
    two_squares = pltpu.VMEM((2, slots, lanes), f32)
    sems = pltpu.SemaphoreType.DMA((2, slots // SPAN))
    table = pltpu.VMEM((table_rows, 2 * HEAD_DIM), bf16)
    table_sum = pltpu.VMEM((table_rows, HEAD_DIM), f32)
    square = pltpu.VMEM((slots, lanes), f32)
    columns = pltpu.VMEM((4 * HEAD_DIM, lanes), bf16)
    lists = [pltpu.SMEM((nb, owners + 1), jnp.int32)] * 2 + [pltpu.SMEM((nb,), jnp.int32)]
    params = pltpu.CompilerParams(vmem_limit_bytes=56 * MIB)
    work = 2 * steps * 6 * SPAN * lanes * 2 * HEAD_DIM

    def soft(keys):
        return pl.pallas_call(
            functools.partial(soft_body, conf=conf),
            grid=(steps,),
            in_specs=[smem_spec] * 3 + [whole_spec(a) for a in (*qs, *gs, *keys)],
            out_specs=[probs_spec] + [whole_spec(a) for a in sums],
            out_shape=[probs] + sums,
            scratch_shapes=[table, table_sum, two_squares, columns, pltpu.VMEM((lanes, 2 * HEAD_DIM), bf16)]
            + lists
            + [sems],
            compiler_params=params,
            cost_estimate=pl.CostEstimate(flops=2 * work, bytes_accessed=4 * rows * width, transcendentals=0),
        )(*scalars, *qs, *gs, *keys)

    def grad(keys, values, probs_in):
        dq = jax.ShapeDtypeStruct((nb * rows, width), f32)
        return pl.pallas_call(
            functools.partial(grad_body, conf=conf),
            grid=(steps,),
            in_specs=[smem_spec] * 3 + [whole_spec(a) for a in (*qs, *gs, *keys, *values)] + [probs_spec],
            out_specs=[pl.BlockSpec((SPAN, width), lambda step: (step, 0))] + [whole_spec(a) for a in sums],
            out_shape=[dq] + sums,
            scratch_shapes=[
                table,
                table,
                table_sum,
                two_squares,
                square,
                columns,
                pltpu.VMEM((lanes, 2 * HEAD_DIM), bf16),
                pltpu.VMEM((2 * HEAD_DIM, lanes), f32),
            ]
            + lists
            + [sems],
            compiler_params=params,
            cost_estimate=pl.CostEstimate(flops=4 * work, bytes_accessed=4 * rows * width, transcendentals=0),
        )(*scalars, *qs, *gs, *keys, *values, probs_in)

    return soft, grad


def flip(array, mask):
    count = lax.axis_size("tok")
    return lax.ppermute(array, "tok", [(index, index ^ mask) for index in range(count)])


def together(*arrays):
    return lax.optimization_barrier(arrays)


def gather_square(array, cut, axis):
    across, down = flip(array, 2), flip(array, 4)
    head = lax.slice_in_dim(across, 0, cut, axis=axis)
    tail = lax.slice_in_dim(down, cut, down.shape[axis], axis=axis)
    return across, down, flip(head, 4), flip(tail, 2)


def scatter_square(across, down, corner):
    from_across, from_down = flip(corner[0], 2), flip(corner[1], 4)
    across_head, down_tail = flip(across[0], 2), flip(down[1], 4)
    across_tail, down_head = flip(across[1] + from_down, 2), flip(down[0] + from_across, 4)
    return across_head, down_head, across_tail, down_tail


def shards_paired(hidden, queries, out_grad, w_key, w_value, fork_tile, live_len):
    owners = lax.axis_size("tok")
    depth = lax.axis_size("head")
    tok = lax.axis_index("tok").astype(jnp.int32)
    core = tok & 1
    rows = hidden.shape[0]
    width = queries.shape[1] // 2
    scalars = (tok.reshape(1), fork_tile, live_len)
    place = (tok >> 1) ^ jnp.arange(depth, dtype=jnp.int32)
    cut = w_key.shape[0] // (2 * HEAD_DIM) * HEAD_DIM

    def mine(array):
        return lax.dynamic_slice_in_dim(array, core * width, width, 1)

    def partners(array):
        return flip(lax.dynamic_slice_in_dim(array, (1 - core) * width, width, 1), 1)

    def project_all(w):
        partial = project(place, (0,), xs, ((0, 0),), [w])
        across, down = flip(w, 2), flip(w, 4)
        across, down, partial = together(across, down, partial)
        head, tail = flip(across[:cut], 4), flip(down[cut:], 2)
        partial = project(place, (1, 2), xs, ((0, 0), (1, 0)), [across, down], partial)
        return project(place, (3,), xs, ((0, 0), (0, cut)), [head, tail], partial)

    def sum_heads(partial):
        return lax.psum_scatter(partial, "head", scatter_dimension=0, tiled=True)[0]

    def all_heads(grads):
        return lax.all_gather(grads, "head", axis=0, tiled=False)

    def lead(array):
        return jnp.concatenate([array[:, :SPAN], array[:, rows : rows + SPAN]], axis=1)

    def returned(across_head, across_tail, down_head, down_tail, corner_head, corner_tail, own):
        arrivals = scatter_square((across_head, across_tail), (down_head, down_tail), (corner_head, corner_tail))
        return combine(own, (0, rows), arrivals)

    def weight(every):
        corner = weight_grad(place, (3,), xs, every)
        across_head, across_tail, down_head, down_tail = weight_grad(place, (1, 2), xs, every)
        kept = weight_grad(place, (0,), xs, every)
        arrivals = scatter_square((across_head, across_tail), (down_head, down_tail), corner)
        return kept, arrivals

    def finish(kept, arrivals):
        across_head, down_head, across_tail, down_tail = arrivals
        return jnp.concatenate([kept[0] + across_head + down_head, kept[1] + across_tail + down_tail], axis=0)

    def home(array):
        kept, received = array[:rows], flip(array[rows:], 1)
        return jnp.where(core == 0, jnp.concatenate([kept, received], axis=1), jnp.concatenate([received, kept], axis=1))

    hidden = hidden.T
    xs = [hidden, flip(hidden, 1)]
    qs = [mine(queries), partners(queries)]
    gs = [mine(out_grad), partners(out_grad)]
    keys = sum_heads(project_all(w_key))
    values = sum_heads(project_all(w_value))

    base = owners * SPAN
    layout = (
        (0, 0, base, 2 * rows),
        (0, 0, 0, SPAN),
        (0, rows, SPAN, SPAN),
        (1, 0, 2 * SPAN, 2 * SPAN),
        (2, 0, 4 * SPAN, 2 * SPAN),
        (3, 0, 6 * SPAN, SPAN),
        (4, 0, 7 * SPAN, SPAN),
    )
    sums = tuple((0, (2 + index) * SPAN, SPAN) for index in range(6))
    soft, grad = attention_calls(scalars, qs, gs, layout, sums, True, owners, 4)

    key_parts = [keys, *gather_square(lead(keys), SPAN, 1)]
    probs, *value_sums = soft(key_parts)
    values, *value_sums = together(values, *value_sums)
    across_head, across_tail, down_head, down_tail, corner_head, corner_tail, own = value_sums
    leading = lead(values)
    value_across, value_down = flip(leading, 2), flip(leading, 4)
    from_across, from_down = flip(corner_head, 2), flip(corner_tail, 4)
    across_head, down_tail = flip(across_head, 2), flip(down_tail, 4)
    value_across, value_down, from_across, from_down = together(value_across, value_down, from_across, from_down)
    value_parts = [values, value_across, value_down, flip(value_across[:, :SPAN], 4), flip(value_down[:, SPAN:], 2)]
    across_tail, down_head = flip(across_tail + from_down, 2), flip(down_head + from_across, 4)
    *value_parts, across_tail, down_head = together(*value_parts, across_tail, down_head)
    value_grads = combine(own, (0, rows), (across_head, down_head, across_tail, down_tail))
    every_value = all_heads(value_grads)
    probs, value_grads = together(probs, value_grads)
    grad_query, *key_sums = grad(key_parts, value_parts, probs)
    key_grads = returned(*key_sums)
    every_key = all_heads(key_grads)
    every_value, key_grads = together(every_value, key_grads)
    grad_w_value = finish(*weight(every_value))
    grad_query, grad_key, grad_value = home(grad_query), home(key_grads), home(value_grads)
    every_key, grad_w_value, grad_query, grad_key, grad_value = together(every_key, grad_w_value, grad_query, grad_key, grad_value)
    grad_w_key = finish(*weight(every_key))
    return grad_query, grad_key, grad_value, grad_w_key, grad_w_value


def shards_single(hidden, queries, out_grad, w_key, w_value, fork_tile, live_len):
    owners = lax.axis_size("tok")
    tok = lax.axis_index("tok").astype(jnp.int32)
    scalars = (tok.reshape(1), fork_tile, live_len)

    def projected(w):
        every = lax.all_gather(w, "tok", axis=1, tiled=True)
        partial = lax.dot_general(every, hidden, (((0,), (1,)), ((), ())), precision=lax.Precision.HIGHEST)
        return lax.psum_scatter(partial, "head", scatter_dimension=0, tiled=True)

    keys, values = projected(w_key), projected(w_value)
    layout = ((0, 0, owners * SPAN, hidden.shape[0]), (1, 0, 0, owners * SPAN))
    sums = ((0, 0, owners * SPAN),)
    soft, grad = attention_calls(scalars, [queries], [out_grad], layout, sums, False, owners, 1)

    def parts(array):
        return [array, lax.all_gather(array[:, :SPAN], "tok", axis=1, tiled=True)]

    def returned(remote, own):
        return own.at[:SPAN].add(lax.psum_scatter(remote, "tok", scatter_dimension=0, tiled=True))

    def weight(grads):
        every = lax.all_gather(grads, "head", axis=1, tiled=True)
        columns = lax.dot_general(hidden, every, (((0,), (0,)), ((), ())), precision=lax.Precision.HIGHEST)
        return lax.psum_scatter(columns, "tok", scatter_dimension=1, tiled=True)

    key_parts = parts(keys)
    probs, *value_sums = soft(key_parts)
    value_grads = returned(*value_sums)
    grad_query, *key_sums = grad(key_parts, parts(values), probs)
    key_grads = returned(*key_sums)
    return grad_query, key_grads, value_grads, weight(key_grads), weight(value_grads)


def shards(hidden, queries, out_grad, w_key, w_value, fork_tile, live_len):
    pairs = lax.axis_size("tok") // 2
    whole_heads = w_key.shape[1] == HEAD_DIM
    paired = whole_heads and pairs == lax.axis_size("head") and pairs == 4
    run = shards_paired if paired else shards_single
    return run(hidden, queries, out_grad, w_key, w_value, fork_tile, live_len)


def solution(mesh):
    placed = (P("tok", "head"), P("tok", "head"), P("tok", "head"), P("head", "tok"), P("head", "tok"), P(), P())
    return jax.shard_map(
        shards,
        mesh=mesh,
        in_specs=placed,
        out_specs=(P("tok", "head"), P("tok", "head"), P("tok", "head"), P("head", "tok"), P("head", "tok")),
        check_vma=False,
    )
```

```python
import functools

import jax
import jax.numpy as jnp
from jax import lax
from jax.experimental import pallas as pl
from jax.experimental.pallas import tpu as pltpu
from jax.sharding import PartitionSpec as P

HEAD_DIM = 128
TILE = 128
CAP = 2
SPAN = CAP * TILE

logit_scale = 168.0 ** (-0.5)
f32 = jnp.float32
bf16 = jnp.bfloat16
MIB = 1024 * 1024


def split(rows):
    high = rows.astype(bf16)
    return high, (rows - high.astype(f32)).astype(bf16)


def pair_cat(rows, axis):
    return jnp.concatenate(split(rows), axis=axis)


def dot(left, right):
    return jnp.dot(left, right, preferred_element_type=f32)


def dot_first(left, right):
    return lax.dot_general(left, right, (((0,), (0,)), ((), ())), preferred_element_type=f32)


def whole_spec(array):
    return pl.BlockSpec(array.shape, lambda *_: (0,) * len(array.shape))


smem_spec = pl.BlockSpec(memory_space=pltpu.SMEM)


def halve_body(x_ref, out_ref):
    out_ref[...] = pair_cat(x_ref[...], 1)


def halve(x):
    depth, rows = x.shape
    block = depth // 4
    return pl.pallas_call(
        halve_body,
        grid=(4,),
        in_specs=[pl.BlockSpec((block, rows), lambda step: (step, 0))],
        out_specs=pl.BlockSpec((block, 2 * rows), lambda step: (step, 0)),
        out_shape=jax.ShapeDtypeStruct((depth, 2 * rows), bf16),
        compiler_params=pltpu.CompilerParams(vmem_limit_bytes=12 * MIB),
        cost_estimate=pl.CostEstimate(flops=4 * x.size, bytes_accessed=8 * x.size, transcendentals=0),
    )(x)


def project_body(place_ref, *refs, row_inputs, pieces, outs):
    x_refs = refs[:row_inputs]
    w_refs = refs[row_inputs : row_inputs + len(pieces)]
    out_refs, pair_ref = refs[-1 - outs : -1], refs[-1]
    step, part_step = pl.program_id(0), pl.program_id(1)
    columns = x_refs[0].shape[1] // 2
    width = columns // outs

    @pl.when((step == 0) & (part_step == 0))
    def _():
        for (part, start), w_ref in zip(pieces, w_refs):
            high, low = split(w_ref[...].T)
            stop = start + w_ref.shape[0]
            pair_ref[part, :HEAD_DIM, start:stop] = high
            pair_ref[part, HEAD_DIM:, start:stop] = low

    for source in range(row_inputs):

        @pl.when(step == source)
        def _():
            total = dot(pair_ref[part_step], x_refs[source][...])
            total = total[:, :columns] + total[:, columns:]
            total = total[:HEAD_DIM] + total[HEAD_DIM:]
            for index, out_ref in enumerate(out_refs):
                out_ref[0] = total[:, index * width : (index + 1) * width]


def project(place, slots, xs, pieces, ws, outs, before=()):
    depth, rows = xs[0].shape
    rows = rows // 2
    first = slots[0]
    width = rows // outs
    inputs = 1 + len(xs) + len(ws)
    return pl.pallas_call(
        functools.partial(project_body, row_inputs=len(xs), pieces=pieces, outs=outs),
        grid_spec=pltpu.PrefetchScalarGridSpec(
            num_scalar_prefetch=1,
            grid=(len(xs), len(slots)),
            in_specs=[whole_spec(x) for x in xs]
            + [whole_spec(w) for w in ws]
            + [pl.BlockSpec(memory_space=pl.ANY)] * len(before),
            out_specs=[pl.BlockSpec((1, HEAD_DIM, width), lambda step, part, place_ref: (place_ref[first + part], 0, step))] * outs,
            scratch_shapes=[pltpu.VMEM((len(slots), 2 * HEAD_DIM, depth), bf16)],
        ),
        out_shape=[jax.ShapeDtypeStruct((place.shape[0], HEAD_DIM, width * len(xs)), f32)] * outs,
        input_output_aliases={inputs + index: index for index in range(len(before))},
        compiler_params=pltpu.CompilerParams(vmem_limit_bytes=24 * MIB),
        cost_estimate=pl.CostEstimate(
            flops=6 * rows * len(xs) * depth * len(slots) * HEAD_DIM, bytes_accessed=4 * rows * len(xs) * depth, transcendentals=0
        ),
    )(place, *xs, *ws, *before)


def weight_grad_body(place_ref, *refs, row_inputs, parts):
    x_refs = refs[:row_inputs]
    g_refs = refs[row_inputs : row_inputs + parts]
    out_refs, pair_ref = refs[row_inputs + parts : -1], refs[-1]
    rows = x_refs[0].shape[1] // 2
    step, half = pl.program_id(0), pl.num_programs(0) // 2

    @pl.when(step == 0)
    def _():
        for part in range(parts):
            pair_ref[:, 2 * part * HEAD_DIM : 2 * (part + 1) * HEAD_DIM] = pair_cat(g_refs[part][0], 1)

    total = 0.0
    for source in range(row_inputs):
        pair = pair_ref[source * rows : (source + 1) * rows]
        total += dot(x_refs[source][:, :rows], pair) + dot(x_refs[source][:, rows:], pair)
    for part in range(parts):
        value = total[:, 2 * part * HEAD_DIM : (2 * part + 1) * HEAD_DIM] + total[:, (2 * part + 1) * HEAD_DIM : 2 * (part + 1) * HEAD_DIM]
        for piece in range(2):

            @pl.when(step // half == piece)
            def _():
                out_refs[2 * part + piece][...] = value


def weight_grad(place, slots, xs, grads):
    depth, rows = xs[0].shape
    rows = rows // 2
    parts = len(slots)
    steps = 4
    half = steps // 2
    block = depth // steps

    def g_map(slot):
        return lambda step, place_ref: (place_ref[slot], 0, 0)

    head = pl.BlockSpec((block, HEAD_DIM), lambda step, place_ref: (jnp.minimum(step, half - 1), 0))
    tail = pl.BlockSpec((block, HEAD_DIM), lambda step, place_ref: (jnp.maximum(step - half, 0), 0))
    return pl.pallas_call(
        functools.partial(weight_grad_body, row_inputs=len(xs), parts=parts),
        grid_spec=pltpu.PrefetchScalarGridSpec(
            num_scalar_prefetch=1,
            grid=(steps,),
            in_specs=[pl.BlockSpec((block, 2 * rows), lambda step, place_ref: (step, 0))] * len(xs)
            + [pl.BlockSpec((1, *grads.shape[1:]), g_map(slot)) for slot in slots],
            out_specs=[head, tail] * parts,
            scratch_shapes=[pltpu.VMEM((rows * len(xs), 2 * parts * HEAD_DIM), bf16)],
        ),
        out_shape=[jax.ShapeDtypeStruct((block * half, HEAD_DIM), f32)] * (2 * parts),
        compiler_params=pltpu.CompilerParams(vmem_limit_bytes=24 * MIB),
        cost_estimate=pl.CostEstimate(
            flops=6 * rows * len(xs) * depth * parts * HEAD_DIM, bytes_accessed=4 * rows * len(xs) * depth, transcendentals=0
        ),
    )(place, *xs, *[grads] * parts)


def combine_body(own_ref, *refs, plan):
    out_ref = refs[-1]
    out_ref[...] = own_ref[...]
    for index, source, target, count in plan:
        out_ref[target : target + count, :] += refs[index][source : source + count, :]


def combine(own, arrivals, plan):
    return pl.pallas_call(
        functools.partial(combine_body, plan=plan),
        out_shape=jax.ShapeDtypeStruct(own.shape, f32),
        compiler_params=pltpu.CompilerParams(vmem_limit_bytes=24 * MIB),
        cost_estimate=pl.CostEstimate(flops=own.size, bytes_accessed=12 * own.size, transcendentals=0),
    )(own, *arrivals)


def list_ancestors(fork_ref, offset_ref, limit_ref, many_ref, tok, slots, tiles, paired):
    for slot in range(slots):

        def climb(carry, slot=slot):
            current, count = carry
            fork_at = fork_ref[current - 1]
            parent = lax.div(fork_at, jnp.int32(tiles))
            offset_ref[slot, count] = ((tok ^ parent) if paired else parent) * SPAN
            limit_ref[slot, count] = (lax.rem(fork_at, jnp.int32(tiles)) + 1) * TILE - 1
            return parent, count + 1

        _, count = lax.while_loop(lambda carry: carry[0] > 0, climb, (tok ^ slot, jnp.int32(0)))
        many_ref[slot] = count
        offset_ref[slot, count] = 0
        limit_ref[slot, count] = -1


def find_step(many_ref, step, tok, halves):
    slot, half = lax.div(step, jnp.int32(halves)), lax.rem(step, jnp.int32(halves))
    return tok ^ slot, slot, half, half + 1 + many_ref[slot]


def block_offset(offset_ref, base, slot, half, halves, block):
    later = jnp.maximum(block - half - 1, 0)
    return jnp.where(block <= half, base + (slot * halves + block) * SPAN, offset_ref[slot, later])


def even(count):
    return 2 * lax.div(count + 1, jnp.int32(2))


def paired_loop(count, body, start, before=None):
    def both(pair, carry):
        if before is not None:
            before(2 * pair)
            before(2 * pair + 1)
        return body(2 * pair + 1, body(2 * pair, carry))

    return lax.fori_loop(0, lax.div(count + 1, jnp.int32(2)), both, start)


def key_limits(limit_ref, slot, half, live, block, lanes):
    lane = lax.broadcasted_iota(jnp.int32, (1, lanes), 1)
    position = half * SPAN + lax.rem(lane, jnp.int32(SPAN))
    own_limit = jnp.minimum(position, live - 1) - block * SPAN
    return jnp.where(block <= half, own_limit, limit_ref[slot, jnp.maximum(block - half - 1, 0)])


def transposed_pair(rows):
    high, low = split(rows.T)
    return jnp.concatenate([high, high, low, low], axis=0)


def load_rows(ref, half, head):
    return ref[pl.ds(pl.multiple_of(half * SPAN, SPAN), SPAN), head * HEAD_DIM : (head + 1) * HEAD_DIM]


def live_column(half, live):
    position = half * SPAN + lax.broadcasted_iota(jnp.int32, (SPAN, 1), 0)
    return (position < live).astype(f32)


def block_rows(ref, offset):
    return ref[pl.ds(pl.multiple_of(offset, SPAN), SPAN), :]


def slot_rows(block):
    return pl.ds(pl.multiple_of(block * SPAN, SPAN), SPAN)


def stage_rows(target_ref, source_refs, layout):
    for index, start, offset, count in layout:
        for piece in range(0, count, SPAN):
            target_ref[offset + piece : offset + piece + SPAN, :] = pair_cat(
                source_refs[index][:, start + piece : start + piece + SPAN].T, 1
            )


def write_rows(source_ref, target_refs, layout, sums):
    for target_ref, (start, offset, count) in zip(target_refs, sums):
        target_ref[start : start + count, :] = source_ref[offset : offset + count, :]
    own = layout[0]
    target_refs[-1][...] = source_ref[own[2] : own[2] + own[3], :]
    for index, start, offset, count in layout[1:]:
        if index == 0:
            target_refs[-1][start : start + count, :] += source_ref[offset : offset + count, :]


def scores(keys_ref, offset, queries, limits):
    keys = block_rows(keys_ref, offset)
    result = dot(jnp.concatenate([keys, keys], axis=1), queries)
    row = lax.broadcasted_iota(jnp.int32, result.shape, 0)
    return jnp.where(row <= limits, result, -1e30)


def fold(value, how):
    return how(value.reshape(SPAN // 8, 8, value.shape[1]), axis=0)


def soft_body(tok_ref, fork_ref, live_ref, *refs, conf):
    nb, group, owners, layout, sources, outs = conf["nb"], conf["group"], conf["owners"], conf["layout"], conf["sources"], conf["outs"]
    halves = conf["rows"] // SPAN
    lanes = group * SPAN
    q_refs, g_refs = refs[:nb], refs[nb : 2 * nb]
    key_refs = refs[2 * nb : 2 * nb + sources]
    prob_ref = refs[2 * nb + sources]
    out_refs = refs[2 * nb + sources + 1 : 2 * nb + sources + 1 + outs]
    keys_ref, sum_ref, scores_ref, qt_ref, grad_ref, offset_ref, limit_ref, many_ref, sems = refs[2 * nb + sources + 1 + outs :]
    step = pl.program_id(0)
    tok = tok_ref[0]
    turn = lax.rem(step, 2)
    score_ref = scores_ref.at[turn]

    def copy_out(of_step, block):
        side = lax.rem(of_step, 2)
        rows = slot_rows(block)
        return pltpu.make_async_copy(scores_ref.at[side, rows], prob_ref.at[of_step, rows], sems.at[side, block])

    def wait_out(of_step):
        def wait(block, _):
            copy_out(of_step, block).wait()
            return 0

        lax.fori_loop(0, even(find_step(many_ref, of_step, tok, halves)[3]), wait, 0)

    @pl.when(step == 0)
    def _():
        list_ancestors(fork_ref, offset_ref, limit_ref, many_ref, tok, nb, conf["rows"] // TILE, conf["paired"])
        stage_rows(keys_ref, key_refs, layout)
        sum_ref[...] = jnp.zeros_like(sum_ref)

    branch, slot, half, count = find_step(many_ref, step, tok, halves)
    place_of = functools.partial(block_offset, offset_ref, owners * SPAN, slot, half, halves)
    live = live_ref[branch]
    for source in range(nb):

        @pl.when(slot == source)
        def _():
            for head in range(group):
                qt_ref[:, head * SPAN : (head + 1) * SPAN] = transposed_pair(load_rows(q_refs[source], half, head) * logit_scale)
                grad_ref[head * SPAN : (head + 1) * SPAN, :] = pair_cat(
                    load_rows(g_refs[source], half, head) * live_column(half, live), 1
                )

    def first(block, largest):
        value = scores(keys_ref, place_of(block), qt_ref[...], key_limits(limit_ref, slot, half, live, block, lanes))
        score_ref[slot_rows(block), :] = value
        return jnp.maximum(largest, fold(value, jnp.max))

    largest = paired_loop(count, first, jnp.full((8, lanes), -1e30, f32))
    largest = jnp.max(largest, axis=0, keepdims=True)

    def second(block, total):
        value = jnp.exp(score_ref[slot_rows(block), :] - largest)
        score_ref[slot_rows(block), :] = value
        return total + fold(value, jnp.sum)

    total = paired_loop(count, second, jnp.zeros((8, lanes), f32))
    inverse = 1.0 / jnp.sum(total, axis=0, keepdims=True)

    def third(block, _):
        prob = score_ref[slot_rows(block), :] * inverse
        score_ref[slot_rows(block), :] = prob
        copy_out(step, block).start()
        high, low = split(prob)
        grads = grad_ref[...]
        both = dot(high, grads) + dot(low, grads)
        offset = place_of(block)
        sum_ref[slot_rows(offset // SPAN), :] += both[:, :HEAD_DIM] + both[:, HEAD_DIM:]
        return 0

    paired_loop(count, third, 0)

    @pl.when(step > 0)
    def _():
        wait_out(step - 1)

    @pl.when(step == nb * halves - 1)
    def _():
        wait_out(step)
        write_rows(sum_ref, out_refs, layout, conf["sums"])


def grad_body(tok_ref, fork_ref, live_ref, *refs, conf):
    nb, group, owners, layout, sources, outs = conf["nb"], conf["group"], conf["owners"], conf["layout"], conf["sources"], conf["outs"]
    halves = conf["rows"] // SPAN
    lanes = group * SPAN
    q_refs, g_refs = refs[:nb], refs[nb : 2 * nb]
    at = 2 * nb
    value_sources = conf["value_sources"]
    key_refs, value_refs = refs[at : at + sources], refs[at + sources : at + sources + value_sources]
    at += sources + value_sources
    prob_ref = refs[at]
    dq_ref = refs[at + 1]
    out_refs = refs[at + 2 : at + 2 + outs]
    (keys_ref, values_ref, sum_ref, probs_ref, dprob_ref, gt_ref, q_ref, dqt_ref, offset_ref, limit_ref, many_ref, sems) = refs[at + 2 + outs :]
    step = pl.program_id(0)
    tok = tok_ref[0]
    held_ref = probs_ref.at[lax.rem(step, 2)]

    def copy_in(of_step, block):
        side = lax.rem(of_step, 2)
        rows = slot_rows(block)
        return pltpu.make_async_copy(prob_ref.at[of_step, rows], probs_ref.at[side, rows], sems.at[side, block])

    def start_in(of_step):
        def start(block, _):
            copy_in(of_step, block).start()
            return 0

        lax.fori_loop(0, even(find_step(many_ref, of_step, tok, halves)[3]), start, 0)

    @pl.when(step == 0)
    def _():
        list_ancestors(fork_ref, offset_ref, limit_ref, many_ref, tok, nb, conf["rows"] // TILE, conf["paired"])
        start_in(step)
        stage_rows(keys_ref, key_refs, layout)
        stage_rows(values_ref, value_refs, conf["value_layout"])
        sum_ref[...] = jnp.zeros_like(sum_ref)

    @pl.when(step < nb * halves - 1)
    def _():
        start_in(step + 1)

    branch, slot, half, count = find_step(many_ref, step, tok, halves)
    place_of = functools.partial(block_offset, offset_ref, owners * SPAN, slot, half, halves)
    live = live_ref[branch]
    for source in range(nb):

        @pl.when(slot == source)
        def _():
            for head in range(group):
                rows = load_rows(q_refs[source], half, head) * logit_scale
                q_ref[head * SPAN : (head + 1) * SPAN, :] = pair_cat(rows, 1)
                gt_ref[:, head * SPAN : (head + 1) * SPAN] = transposed_pair(
                    load_rows(g_refs[source], half, head) * live_column(half, live)
                )

    def first(block, delta):
        values = block_rows(values_ref, place_of(block))
        dprob = dot(jnp.concatenate([values, values], axis=1), gt_ref[...])
        dprob_ref[slot_rows(block), :] = dprob
        return delta + fold(held_ref[slot_rows(block), :] * dprob, jnp.sum)

    delta = paired_loop(count, first, jnp.zeros((8, lanes), f32), lambda block: copy_in(step, block).wait())
    delta = jnp.sum(delta, axis=0, keepdims=True)
    dqt_ref[...] = jnp.zeros_like(dqt_ref)

    def second(block, _):
        offset = place_of(block)
        high, low = split(held_ref[slot_rows(block), :] * (dprob_ref[slot_rows(block), :] - delta))
        rows = q_ref[...]
        both = dot(high, rows) + dot(low, rows)
        sum_ref[slot_rows(offset // SPAN), :] += both[:, :HEAD_DIM] + both[:, HEAD_DIM:]
        keys = block_rows(keys_ref, offset)
        dqt_ref[...] += dot_first(keys, high) + dot_first(keys, low)
        return 0

    paired_loop(count, second, 0)
    folded = (dqt_ref[:HEAD_DIM, :] + dqt_ref[HEAD_DIM:, :]) * logit_scale
    for head in range(group):
        dq_ref[:, head * HEAD_DIM : (head + 1) * HEAD_DIM] = folded[:, head * SPAN : (head + 1) * SPAN].T

    @pl.when(step == nb * halves - 1)
    def _():
        write_rows(sum_ref, out_refs, layout, conf["sums"])


def attention_calls(scalars, qs, gs, layout, value_layout, key_sum_rows, value_sum_rows, paired, owners):
    rows, width = qs[0].shape
    nb, group, halves = len(qs), width // HEAD_DIM, rows // SPAN
    lanes = group * SPAN
    steps = nb * halves
    conf = dict(nb=nb, group=group, rows=rows, owners=owners, layout=layout, value_layout=value_layout, paired=paired)
    conf["sources"] = 1 + max(entry[0] for entry in layout)
    conf["value_sources"] = 1 + max(entry[0] for entry in value_layout)
    table_rows = owners * SPAN + nb * rows
    slots = (owners + halves) * SPAN

    def sums_of(sum_rows):
        shapes = [jax.ShapeDtypeStruct((count, HEAD_DIM), f32) for _, _, count in sum_rows]
        return shapes + [jax.ShapeDtypeStruct((nb * rows, HEAD_DIM), f32)], dict(conf, sums=sum_rows, outs=len(sum_rows) + 1)

    key_sums, key_conf = sums_of(key_sum_rows)
    value_sums, value_conf = sums_of(value_sum_rows)
    probs = jax.ShapeDtypeStruct((steps, slots, lanes), f32)
    probs_spec = pl.BlockSpec(memory_space=pl.ANY)
    two_squares = pltpu.VMEM((2, slots, lanes), f32)
    sems = pltpu.SemaphoreType.DMA((2, slots // SPAN))
    table = pltpu.VMEM((table_rows, 2 * HEAD_DIM), bf16)
    table_sum = pltpu.VMEM((table_rows, HEAD_DIM), f32)
    square = pltpu.VMEM((slots, lanes), f32)
    columns = pltpu.VMEM((4 * HEAD_DIM, lanes), bf16)
    lists = [pltpu.SMEM((nb, owners + 1), jnp.int32)] * 2 + [pltpu.SMEM((nb,), jnp.int32)]
    params = pltpu.CompilerParams(vmem_limit_bytes=56 * MIB)
    work = 2 * steps * 6 * SPAN * lanes * 2 * HEAD_DIM

    def soft(keys):
        return pl.pallas_call(
            functools.partial(soft_body, conf=value_conf),
            grid=(steps,),
            in_specs=[smem_spec] * 3 + [whole_spec(a) for a in (*qs, *gs, *keys)],
            out_specs=[probs_spec] + [whole_spec(a) for a in value_sums],
            out_shape=[probs] + value_sums,
            scratch_shapes=[table, table_sum, two_squares, columns, pltpu.VMEM((lanes, 2 * HEAD_DIM), bf16)]
            + lists
            + [sems],
            compiler_params=params,
            cost_estimate=pl.CostEstimate(flops=2 * work, bytes_accessed=4 * rows * width, transcendentals=0),
        )(*scalars, *qs, *gs, *keys)

    def grad(keys, values, probs_in):
        dq = jax.ShapeDtypeStruct((nb * rows, width), f32)
        return pl.pallas_call(
            functools.partial(grad_body, conf=key_conf),
            grid=(steps,),
            in_specs=[smem_spec] * 3 + [whole_spec(a) for a in (*qs, *gs, *keys, *values)] + [probs_spec],
            out_specs=[pl.BlockSpec((SPAN, width), lambda step: (step, 0))] + [whole_spec(a) for a in key_sums],
            out_shape=[dq] + key_sums,
            scratch_shapes=[
                table,
                table,
                table_sum,
                two_squares,
                square,
                columns,
                pltpu.VMEM((lanes, 2 * HEAD_DIM), bf16),
                pltpu.VMEM((2 * HEAD_DIM, lanes), f32),
            ]
            + lists
            + [sems],
            compiler_params=params,
            cost_estimate=pl.CostEstimate(flops=4 * work, bytes_accessed=4 * rows * width, transcendentals=0),
        )(*scalars, *qs, *gs, *keys, *values, probs_in)

    return soft, grad


def flip(array, mask):
    count = lax.axis_size("tok")
    return lax.ppermute(array, "tok", [(index, index ^ mask) for index in range(count)])


def together(*arrays):
    return lax.optimization_barrier(arrays)


def gather_square(array, cut, axis):
    across, down = flip(array, 2), flip(array, 4)
    head = lax.slice_in_dim(across, 0, cut, axis=axis)
    tail = lax.slice_in_dim(down, cut, down.shape[axis], axis=axis)
    return across, down, flip(head, 4), flip(tail, 2)


def scatter_square(across, down, corner):
    from_across, from_down = flip(corner[0], 2), flip(corner[1], 4)
    across_head, down_tail = flip(across[0], 2), flip(down[1], 4)
    across_tail, down_head = flip(across[1] + from_down, 2), flip(down[0] + from_across, 4)
    return across_head, down_head, across_tail, down_tail


def shards_paired(hidden, queries, out_grad, w_key, w_value, fork_tile, live_len):
    owners = lax.axis_size("tok")
    depth = lax.axis_size("head")
    tok = lax.axis_index("tok").astype(jnp.int32)
    core = tok & 1
    rows = hidden.shape[0]
    width = queries.shape[1] // 2
    scalars = (tok.reshape(1), fork_tile, live_len)
    place = (tok >> 1) ^ jnp.arange(depth, dtype=jnp.int32)
    cut = w_key.shape[0] // (2 * HEAD_DIM) * HEAD_DIM

    def mine(array):
        return lax.dynamic_slice_in_dim(array, core * width, width, 1)

    def partners(array):
        return flip(lax.dynamic_slice_in_dim(array, (1 - core) * width, width, 1), 1)

    def project_all(w, outs):
        partial = project(place, (0,), xs, ((0, 0),), [w], outs)
        across, down = flip(w, 2), flip(w, 4)
        across, down, *partial = together(across, down, *partial)
        head, tail = flip(across[:cut], 4), flip(down[cut:], 2)
        partial = project(place, (1, 2), xs, ((0, 0), (1, 0)), [across, down], outs, partial)
        return project(place, (3,), xs, ((0, 0), (0, cut)), [head, tail], outs, partial)

    def sum_heads(partial):
        return lax.psum_scatter(partial, "head", scatter_dimension=0, tiled=True)[0]

    def all_heads(grads):
        return lax.all_gather(grads, "head", axis=0, tiled=False)

    def lead(array):
        return jnp.concatenate([array[:, :SPAN], array[:, rows : rows + SPAN]], axis=1)

    def returned(across_head, across_tail, down_head, down_tail, corner_head, corner_tail, own):
        arrivals = scatter_square((across_head, across_tail), (down_head, down_tail), (corner_head, corner_tail))
        plan = tuple((index, 0, rows * (index // 2), SPAN) for index in range(4))
        return combine(own, arrivals, plan)

    def returned_at_once(across, down, corner, own):
        plan = tuple((index, slot * SPAN, slot * rows, SPAN) for index in range(3) for slot in range(2))
        return combine(own, [flip(across, 2), flip(down, 4), flip(corner, 6)], plan)

    def weight(every, xs):
        corner = weight_grad(place, (3,), xs, every)
        across_head, across_tail, down_head, down_tail = weight_grad(place, (1, 2), xs, every)
        kept = weight_grad(place, (0,), xs, every)
        arrivals = scatter_square((across_head, across_tail), (down_head, down_tail), corner)
        return kept, arrivals

    def finish(kept, arrivals):
        across_head, down_head, across_tail, down_tail = arrivals
        return jnp.concatenate([kept[0] + across_head + down_head, kept[1] + across_tail + down_tail], axis=0)

    def home(array):
        kept, received = array[:rows], flip(array[rows:], 1)
        return jnp.where(core == 0, jnp.concatenate([kept, received], axis=1), jnp.concatenate([received, kept], axis=1))

    hidden = hidden.T
    both = [hidden, flip(hidden, 1)]
    xs = [halve(x) for x in both]
    qs = [mine(queries), partners(queries)]
    gs = [mine(out_grad), partners(out_grad)]
    keys = sum_heads(project_all(w_key, 1)[0])
    leading, trailing = map(sum_heads, project_all(w_value, 2))

    base = owners * SPAN
    layout = (
        (0, 0, base, 2 * rows),
        (0, 0, 0, SPAN),
        (0, rows, SPAN, SPAN),
        (1, 0, 2 * SPAN, 2 * SPAN),
        (2, 0, 4 * SPAN, 2 * SPAN),
        (3, 0, 6 * SPAN, SPAN),
        (4, 0, 7 * SPAN, SPAN),
    )
    value_layout = (
        (0, 0, base, SPAN),
        (0, SPAN, base + rows, SPAN),
        (0, 0, 0, 2 * SPAN),
        (1, 0, base + SPAN, SPAN),
        (1, SPAN, base + rows + SPAN, SPAN),
    ) + tuple((index + 1, *rest) for index, *rest in layout[3:])
    key_sum_rows = tuple((0, (2 + index) * SPAN, SPAN) for index in range(6))
    value_sum_rows = tuple((0, 2 * (1 + index) * SPAN, 2 * SPAN) for index in range(3))
    soft, grad = attention_calls(scalars, qs, gs, layout, value_layout, key_sum_rows, value_sum_rows, True, owners)

    key_parts = [keys, *gather_square(lead(keys), SPAN, 1)]
    probs, *value_sums = soft(key_parts)
    value_parts = list(together(leading, *value_sums))[:1]
    value_parts += gather_square(value_parts[0], SPAN, 1)
    value_grads = returned_at_once(*value_sums)
    probs, value_grads, *value_parts = together(probs, value_grads, *value_parts)
    trailing, value_grads = together(trailing, value_grads)
    every_value = all_heads(value_grads)
    value_parts = [value_parts[0], trailing, *value_parts[1:]]
    grad_query, *key_sums = grad(key_parts, value_parts, probs)
    key_grads = returned(*key_sums)
    every_key = all_heads(key_grads)
    every_value, key_grads = together(every_value, key_grads)
    grad_w_value = finish(*weight(every_value, xs))
    grad_query, grad_key, grad_value = home(grad_query), home(key_grads), home(value_grads)
    *both, grad_w_value = together(*both, grad_w_value)
    late = [halve(x) for x in both]
    every_key, grad_w_value, grad_query, grad_key, grad_value, *late = together(every_key, grad_w_value, grad_query, grad_key, grad_value, *late)
    grad_w_key = finish(*weight(every_key, late))
    return grad_query, grad_key, grad_value, grad_w_key, grad_w_value


def shards_single(hidden, queries, out_grad, w_key, w_value, fork_tile, live_len):
    owners = lax.axis_size("tok")
    tok = lax.axis_index("tok").astype(jnp.int32)
    scalars = (tok.reshape(1), fork_tile, live_len)

    def projected(w):
        every = lax.all_gather(w, "tok", axis=1, tiled=True)
        partial = lax.dot_general(every, hidden, (((0,), (1,)), ((), ())), precision=lax.Precision.HIGHEST)
        return lax.psum_scatter(partial, "head", scatter_dimension=0, tiled=True)

    keys, values = projected(w_key), projected(w_value)
    layout = ((0, 0, owners * SPAN, hidden.shape[0]), (1, 0, 0, owners * SPAN))
    sums = ((0, 0, owners * SPAN),)
    soft, grad = attention_calls(scalars, [queries], [out_grad], layout, layout, sums, sums, False, owners)

    def parts(array):
        return [array, lax.all_gather(array[:, :SPAN], "tok", axis=1, tiled=True)]

    def returned(remote, own):
        return own.at[:SPAN].add(lax.psum_scatter(remote, "tok", scatter_dimension=0, tiled=True))

    def weight(grads):
        every = lax.all_gather(grads, "head", axis=1, tiled=True)
        columns = lax.dot_general(hidden, every, (((0,), (0,)), ((), ())), precision=lax.Precision.HIGHEST)
        return lax.psum_scatter(columns, "tok", scatter_dimension=1, tiled=True)

    key_parts = parts(keys)
    probs, *value_sums = soft(key_parts)
    value_grads = returned(*value_sums)
    grad_query, *key_sums = grad(key_parts, parts(values), probs)
    key_grads = returned(*key_sums)
    return grad_query, key_grads, value_grads, weight(key_grads), weight(value_grads)


def shards(hidden, queries, out_grad, w_key, w_value, fork_tile, live_len):
    pairs = lax.axis_size("tok") // 2
    whole_heads = w_key.shape[1] == HEAD_DIM
    paired = whole_heads and pairs == lax.axis_size("head") and pairs == 4
    run = shards_paired if paired else shards_single
    return run(hidden, queries, out_grad, w_key, w_value, fork_tile, live_len)


def solution(mesh):
    placed = (P("tok", "head"), P("tok", "head"), P("tok", "head"), P("head", "tok"), P("head", "tok"), P(), P())
    return jax.shard_map(
        shards,
        mesh=mesh,
        in_specs=placed,
        out_specs=(P("tok", "head"), P("tok", "head"), P("tok", "head"), P("head", "tok"), P("head", "tok")),
        check_vma=False,
    )
```

```python
import functools

import jax
import jax.numpy as jnp
from jax import lax
from jax.experimental import pallas as pl
from jax.experimental.pallas import tpu as pltpu
from jax.sharding import PartitionSpec as P

HEAD_DIM = 128
TILE = 128
CAP = 2
SPAN = CAP * TILE

logit_scale = 168.0 ** (-0.5)
f32 = jnp.float32
bf16 = jnp.bfloat16
MIB = 1024 * 1024


def split(rows):
    high = rows.astype(bf16)
    return high, (rows - high.astype(f32)).astype(bf16)


def pair_cat(rows, axis):
    return jnp.concatenate(split(rows), axis=axis)


def dot(left, right):
    return jnp.dot(left, right, preferred_element_type=f32)


def dot_first(left, right):
    return lax.dot_general(left, right, (((0,), (0,)), ((), ())), preferred_element_type=f32)


def whole_spec(array):
    return pl.BlockSpec(array.shape, lambda *_: (0,) * len(array.shape))


smem_spec = pl.BlockSpec(memory_space=pltpu.SMEM)


def halve_body(x_ref, out_ref):
    out_ref[...] = pair_cat(x_ref[...], 1)


def halve(x):
    depth, rows = x.shape
    block = depth // 4
    return pl.pallas_call(
        halve_body,
        grid=(4,),
        in_specs=[pl.BlockSpec((block, rows), lambda step: (step, 0))],
        out_specs=pl.BlockSpec((block, 2 * rows), lambda step: (step, 0)),
        out_shape=jax.ShapeDtypeStruct((depth, 2 * rows), bf16),
        compiler_params=pltpu.CompilerParams(vmem_limit_bytes=12 * MIB),
        cost_estimate=pl.CostEstimate(flops=4 * x.size, bytes_accessed=8 * x.size, transcendentals=0),
    )(x)


def project_body(place_ref, *refs, row_inputs, pieces, outs):
    x_refs = refs[:row_inputs]
    w_refs = refs[row_inputs : row_inputs + len(pieces)]
    out_refs, pair_ref = refs[-1 - outs : -1], refs[-1]
    step, part_step = pl.program_id(0), pl.program_id(1)
    columns = x_refs[0].shape[1] // 2
    width = columns // outs

    @pl.when((step == 0) & (part_step == 0))
    def _():
        for (part, start), w_ref in zip(pieces, w_refs):
            high, low = split(w_ref[...].T)
            stop = start + w_ref.shape[0]
            pair_ref[part, :HEAD_DIM, start:stop] = high
            pair_ref[part, HEAD_DIM:, start:stop] = low

    for source in range(row_inputs):

        @pl.when(step == source)
        def _():
            total = dot(pair_ref[part_step], x_refs[source][...])
            total = total[:, :columns] + total[:, columns:]
            total = total[:HEAD_DIM] + total[HEAD_DIM:]
            for index, out_ref in enumerate(out_refs):
                out_ref[0] = total[:, index * width : (index + 1) * width]


def project(place, slots, xs, pieces, ws, outs, before=()):
    depth, rows = xs[0].shape
    rows = rows // 2
    first = slots[0]
    width = rows // outs
    inputs = 1 + len(xs) + len(ws)
    return pl.pallas_call(
        functools.partial(project_body, row_inputs=len(xs), pieces=pieces, outs=outs),
        grid_spec=pltpu.PrefetchScalarGridSpec(
            num_scalar_prefetch=1,
            grid=(len(xs), len(slots)),
            in_specs=[whole_spec(x) for x in xs]
            + [whole_spec(w) for w in ws]
            + [pl.BlockSpec(memory_space=pl.ANY)] * len(before),
            out_specs=[pl.BlockSpec((1, HEAD_DIM, width), lambda step, part, place_ref: (place_ref[first + part], 0, step))] * outs,
            scratch_shapes=[pltpu.VMEM((len(slots), 2 * HEAD_DIM, depth), bf16)],
        ),
        out_shape=[jax.ShapeDtypeStruct((place.shape[0], HEAD_DIM, width * len(xs)), f32)] * outs,
        input_output_aliases={inputs + index: index for index in range(len(before))},
        compiler_params=pltpu.CompilerParams(vmem_limit_bytes=24 * MIB),
        cost_estimate=pl.CostEstimate(
            flops=6 * rows * len(xs) * depth * len(slots) * HEAD_DIM, bytes_accessed=4 * rows * len(xs) * depth, transcendentals=0
        ),
    )(place, *xs, *ws, *before)


def weight_grad_body(place_ref, *refs, row_inputs, parts):
    x_refs = refs[:row_inputs]
    g_refs = refs[row_inputs : row_inputs + parts]
    out_refs, pair_ref = refs[row_inputs + parts : -1], refs[-1]
    rows = x_refs[0].shape[1] // 2
    step, half = pl.program_id(0), pl.num_programs(0) // 2

    @pl.when(step == 0)
    def _():
        for part in range(parts):
            pair_ref[:, 2 * part * HEAD_DIM : 2 * (part + 1) * HEAD_DIM] = pair_cat(g_refs[part][0], 1)

    total = 0.0
    for source in range(row_inputs):
        pair = pair_ref[source * rows : (source + 1) * rows]
        total += dot(x_refs[source][:, :rows], pair) + dot(x_refs[source][:, rows:], pair)
    for part in range(parts):
        value = total[:, 2 * part * HEAD_DIM : (2 * part + 1) * HEAD_DIM] + total[:, (2 * part + 1) * HEAD_DIM : 2 * (part + 1) * HEAD_DIM]
        for piece in range(2):

            @pl.when(step // half == piece)
            def _():
                out_refs[2 * part + piece][...] = value


def weight_grad(place, slots, xs, grads):
    depth, rows = xs[0].shape
    rows = rows // 2
    parts = len(slots)
    steps = 4
    half = steps // 2
    block = depth // steps

    def g_map(slot):
        return lambda step, place_ref: (place_ref[slot], 0, 0)

    head = pl.BlockSpec((block, HEAD_DIM), lambda step, place_ref: (jnp.minimum(step, half - 1), 0))
    tail = pl.BlockSpec((block, HEAD_DIM), lambda step, place_ref: (jnp.maximum(step - half, 0), 0))
    return pl.pallas_call(
        functools.partial(weight_grad_body, row_inputs=len(xs), parts=parts),
        grid_spec=pltpu.PrefetchScalarGridSpec(
            num_scalar_prefetch=1,
            grid=(steps,),
            in_specs=[pl.BlockSpec((block, 2 * rows), lambda step, place_ref: (step, 0))] * len(xs)
            + [pl.BlockSpec((1, *grads.shape[1:]), g_map(slot)) for slot in slots],
            out_specs=[head, tail] * parts,
            scratch_shapes=[pltpu.VMEM((rows * len(xs), 2 * parts * HEAD_DIM), bf16)],
        ),
        out_shape=[jax.ShapeDtypeStruct((block * half, HEAD_DIM), f32)] * (2 * parts),
        compiler_params=pltpu.CompilerParams(vmem_limit_bytes=24 * MIB),
        cost_estimate=pl.CostEstimate(
            flops=6 * rows * len(xs) * depth * parts * HEAD_DIM, bytes_accessed=4 * rows * len(xs) * depth, transcendentals=0
        ),
    )(place, *xs, *[grads] * parts)


def combine_body(own_ref, *refs, plan):
    out_ref = refs[-1]
    out_ref[...] = own_ref[...]
    for index, source, target, count in plan:
        out_ref[target : target + count, :] += refs[index][source : source + count, :]


def combine(own, arrivals, plan):
    return pl.pallas_call(
        functools.partial(combine_body, plan=plan),
        out_shape=jax.ShapeDtypeStruct(own.shape, f32),
        compiler_params=pltpu.CompilerParams(vmem_limit_bytes=24 * MIB),
        cost_estimate=pl.CostEstimate(flops=own.size, bytes_accessed=12 * own.size, transcendentals=0),
    )(own, *arrivals)


def list_ancestors(fork_ref, offset_ref, limit_ref, many_ref, tok, slots, tiles, paired):
    for slot in range(slots):

        def climb(carry, slot=slot):
            current, count = carry
            fork_at = fork_ref[current - 1]
            parent = lax.div(fork_at, jnp.int32(tiles))
            offset_ref[slot, count] = ((tok ^ parent) if paired else parent) * SPAN
            limit_ref[slot, count] = (lax.rem(fork_at, jnp.int32(tiles)) + 1) * TILE - 1
            return parent, count + 1

        _, count = lax.while_loop(lambda carry: carry[0] > 0, climb, (tok ^ slot, jnp.int32(0)))
        many_ref[slot] = count
        offset_ref[slot, count] = 0
        limit_ref[slot, count] = -1


def find_step(many_ref, step, tok, halves):
    slot, half = lax.div(step, jnp.int32(halves)), lax.rem(step, jnp.int32(halves))
    return tok ^ slot, slot, half, half + 1 + many_ref[slot]


def block_offset(offset_ref, base, slot, half, halves, block):
    later = jnp.maximum(block - half - 1, 0)
    return jnp.where(block <= half, base + (slot * halves + block) * SPAN, offset_ref[slot, later])


def even(count):
    return 2 * lax.div(count + 1, jnp.int32(2))


def paired_loop(count, body, start, before=None):
    def both(pair, carry):
        if before is not None:
            before(2 * pair)
            before(2 * pair + 1)
        return body(2 * pair + 1, body(2 * pair, carry))

    return lax.fori_loop(0, lax.div(count + 1, jnp.int32(2)), both, start)


def key_limits(limit_ref, slot, half, live, block, lanes):
    lane = lax.broadcasted_iota(jnp.int32, (1, lanes), 1)
    position = half * SPAN + lax.rem(lane, jnp.int32(SPAN))
    own_limit = jnp.minimum(position, live - 1) - block * SPAN
    return jnp.where(block <= half, own_limit, limit_ref[slot, jnp.maximum(block - half - 1, 0)])


def transposed_pair(rows):
    high, low = split(rows.T)
    return jnp.concatenate([high, high, low, low], axis=0)


def load_rows(ref, half, head):
    return ref[pl.ds(pl.multiple_of(half * SPAN, SPAN), SPAN), head * HEAD_DIM : (head + 1) * HEAD_DIM]


def live_column(half, live):
    position = half * SPAN + lax.broadcasted_iota(jnp.int32, (SPAN, 1), 0)
    return (position < live).astype(f32)


def block_rows(ref, offset):
    return ref[pl.ds(pl.multiple_of(offset, SPAN), SPAN), :]


def slot_rows(block):
    return pl.ds(pl.multiple_of(block * SPAN, SPAN), SPAN)


def stage_rows(target_ref, source_refs, layout):
    for index, start, offset, count in layout:
        for piece in range(0, count, SPAN):
            target_ref[offset + piece : offset + piece + SPAN, :] = pair_cat(
                source_refs[index][:, start + piece : start + piece + SPAN].T, 1
            )


def write_rows(source_ref, target_refs, layout, sums):
    for target_ref, (start, offset, count) in zip(target_refs, sums):
        target_ref[start : start + count, :] = source_ref[offset : offset + count, :]
    own = layout[0]
    target_refs[-1][...] = source_ref[own[2] : own[2] + own[3], :]
    for index, start, offset, count in layout[1:]:
        if index == 0:
            target_refs[-1][start : start + count, :] += source_ref[offset : offset + count, :]


def scores(keys_ref, offset, queries, limits):
    keys = block_rows(keys_ref, offset)
    result = dot(jnp.concatenate([keys, keys], axis=1), queries)
    row = lax.broadcasted_iota(jnp.int32, result.shape, 0)
    return jnp.where(row <= limits, result, -1e30)


def fold(value, how):
    return how(value.reshape(SPAN // 8, 8, value.shape[1]), axis=0)


def stage_body(tok_ref, live_ref, *refs, nb, group, halves):
    q_refs, g_refs = refs[:nb], refs[nb : 2 * nb]
    qt_ref, q_ref, gt_ref, grad_ref = refs[2 * nb :]
    step = pl.program_id(0)
    slot, half = lax.div(step, jnp.int32(halves)), lax.rem(step, jnp.int32(halves))
    live = live_ref[tok_ref[0] ^ slot]
    for source in range(nb):

        @pl.when(slot == source)
        def _():
            for head in range(group):
                part = slice(head * SPAN, (head + 1) * SPAN)
                rows = load_rows(q_refs[source], half, head) * logit_scale
                qt_ref[0, :, part] = transposed_pair(rows)
                q_ref[0, part, :] = pair_cat(rows, 1)
                rows = load_rows(g_refs[source], half, head) * live_column(half, live)
                gt_ref[0, :, part] = transposed_pair(rows)
                grad_ref[0, part, :] = pair_cat(rows, 1)


def soft_body(tok_ref, fork_ref, live_ref, *refs, conf):
    nb, group, owners, layout, sources, outs = conf["nb"], conf["group"], conf["owners"], conf["layout"], conf["sources"], conf["outs"]
    halves = conf["rows"] // SPAN
    lanes = group * SPAN
    qt_ref, grad_ref = refs[:2]
    key_refs = refs[2 : 2 + sources]
    prob_ref = refs[2 + sources]
    out_refs = refs[3 + sources : 3 + sources + outs]
    keys_ref, sum_ref, scores_ref, offset_ref, limit_ref, many_ref, sems = refs[3 + sources + outs :]
    step = pl.program_id(0)
    tok = tok_ref[0]
    turn = lax.rem(step, 2)
    score_ref = scores_ref.at[turn]

    def copy_out(of_step, block):
        side = lax.rem(of_step, 2)
        rows = slot_rows(block)
        return pltpu.make_async_copy(scores_ref.at[side, rows], prob_ref.at[of_step, rows], sems.at[side, block])

    def wait_out(of_step):
        def wait(block, _):
            copy_out(of_step, block).wait()
            return 0

        lax.fori_loop(0, even(find_step(many_ref, of_step, tok, halves)[3]), wait, 0)

    @pl.when(step == 0)
    def _():
        list_ancestors(fork_ref, offset_ref, limit_ref, many_ref, tok, nb, conf["rows"] // TILE, conf["paired"])
        stage_rows(keys_ref, key_refs, layout)
        sum_ref[...] = jnp.zeros_like(sum_ref)

    branch, slot, half, count = find_step(many_ref, step, tok, halves)
    place_of = functools.partial(block_offset, offset_ref, owners * SPAN, slot, half, halves)
    live = live_ref[branch]
    def first(block, largest):
        value = scores(keys_ref, place_of(block), qt_ref[0], key_limits(limit_ref, slot, half, live, block, lanes))
        score_ref[slot_rows(block), :] = value
        return jnp.maximum(largest, fold(value, jnp.max))

    largest = paired_loop(count, first, jnp.full((8, lanes), -1e30, f32))
    largest = jnp.max(largest, axis=0, keepdims=True)

    def second(block, total):
        value = jnp.exp(score_ref[slot_rows(block), :] - largest)
        score_ref[slot_rows(block), :] = value
        return total + fold(value, jnp.sum)

    total = paired_loop(count, second, jnp.zeros((8, lanes), f32))
    inverse = 1.0 / jnp.sum(total, axis=0, keepdims=True)

    def third(block, _):
        prob = score_ref[slot_rows(block), :] * inverse
        score_ref[slot_rows(block), :] = prob
        copy_out(step, block).start()
        high, low = split(prob)
        grads = grad_ref[0]
        both = dot(high, grads) + dot(low, grads)
        offset = place_of(block)
        sum_ref[slot_rows(offset // SPAN), :] += both[:, :HEAD_DIM] + both[:, HEAD_DIM:]
        return 0

    paired_loop(count, third, 0)

    @pl.when(step > 0)
    def _():
        wait_out(step - 1)

    @pl.when(step == nb * halves - 1)
    def _():
        wait_out(step)
        write_rows(sum_ref, out_refs, layout, conf["sums"])


def grad_body(tok_ref, fork_ref, live_ref, *refs, conf):
    nb, group, owners, layout, sources, outs = conf["nb"], conf["group"], conf["owners"], conf["layout"], conf["sources"], conf["outs"]
    halves = conf["rows"] // SPAN
    lanes = group * SPAN
    gt_ref, q_ref = refs[:2]
    at = 2
    value_sources = conf["value_sources"]
    key_refs, value_refs = refs[at : at + sources], refs[at + sources : at + sources + value_sources]
    at += sources + value_sources
    prob_ref = refs[at]
    dq_ref = refs[at + 1]
    out_refs = refs[at + 2 : at + 2 + outs]
    (keys_ref, values_ref, sum_ref, probs_ref, dprob_ref, dqt_ref, offset_ref, limit_ref, many_ref, sems) = refs[at + 2 + outs :]
    step = pl.program_id(0)
    tok = tok_ref[0]
    held_ref = probs_ref.at[lax.rem(step, 2)]

    def copy_in(of_step, block):
        side = lax.rem(of_step, 2)
        rows = slot_rows(block)
        return pltpu.make_async_copy(prob_ref.at[of_step, rows], probs_ref.at[side, rows], sems.at[side, block])

    def start_in(of_step):
        def start(block, _):
            copy_in(of_step, block).start()
            return 0

        lax.fori_loop(0, even(find_step(many_ref, of_step, tok, halves)[3]), start, 0)

    @pl.when(step == 0)
    def _():
        list_ancestors(fork_ref, offset_ref, limit_ref, many_ref, tok, nb, conf["rows"] // TILE, conf["paired"])
        start_in(step)
        stage_rows(keys_ref, key_refs, layout)
        stage_rows(values_ref, value_refs, conf["value_layout"])
        sum_ref[...] = jnp.zeros_like(sum_ref)

    @pl.when(step < nb * halves - 1)
    def _():
        start_in(step + 1)

    branch, slot, half, count = find_step(many_ref, step, tok, halves)
    place_of = functools.partial(block_offset, offset_ref, owners * SPAN, slot, half, halves)
    def first(block, delta):
        values = block_rows(values_ref, place_of(block))
        dprob = dot(jnp.concatenate([values, values], axis=1), gt_ref[0])
        dprob_ref[slot_rows(block), :] = dprob
        return delta + fold(held_ref[slot_rows(block), :] * dprob, jnp.sum)

    delta = paired_loop(count, first, jnp.zeros((8, lanes), f32), lambda block: copy_in(step, block).wait())
    delta = jnp.sum(delta, axis=0, keepdims=True)
    dqt_ref[...] = jnp.zeros_like(dqt_ref)

    def second(block, _):
        offset = place_of(block)
        high, low = split(held_ref[slot_rows(block), :] * (dprob_ref[slot_rows(block), :] - delta))
        rows = q_ref[0]
        both = dot(high, rows) + dot(low, rows)
        sum_ref[slot_rows(offset // SPAN), :] += both[:, :HEAD_DIM] + both[:, HEAD_DIM:]
        keys = block_rows(keys_ref, offset)
        dqt_ref[...] += dot_first(keys, high) + dot_first(keys, low)
        return 0

    paired_loop(count, second, 0)
    folded = (dqt_ref[:HEAD_DIM, :] + dqt_ref[HEAD_DIM:, :]) * logit_scale
    for head in range(group):
        dq_ref[:, head * HEAD_DIM : (head + 1) * HEAD_DIM] = folded[:, head * SPAN : (head + 1) * SPAN].T

    @pl.when(step == nb * halves - 1)
    def _():
        write_rows(sum_ref, out_refs, layout, conf["sums"])


def attention_calls(scalars, qs, gs, layout, value_layout, key_sum_rows, value_sum_rows, paired, owners):
    rows, width = qs[0].shape
    nb, group, halves = len(qs), width // HEAD_DIM, rows // SPAN
    lanes = group * SPAN
    steps = nb * halves
    conf = dict(nb=nb, group=group, rows=rows, owners=owners, layout=layout, value_layout=value_layout, paired=paired)
    conf["sources"] = 1 + max(entry[0] for entry in layout)
    conf["value_sources"] = 1 + max(entry[0] for entry in value_layout)
    table_rows = owners * SPAN + nb * rows
    slots = (owners + halves) * SPAN

    def sums_of(sum_rows):
        shapes = [jax.ShapeDtypeStruct((count, HEAD_DIM), f32) for _, _, count in sum_rows]
        return shapes + [jax.ShapeDtypeStruct((nb * rows, HEAD_DIM), f32)], dict(conf, sums=sum_rows, outs=len(sum_rows) + 1)

    key_sums, key_conf = sums_of(key_sum_rows)
    value_sums, value_conf = sums_of(value_sum_rows)
    probs = jax.ShapeDtypeStruct((steps, slots, lanes), f32)
    probs_spec = pl.BlockSpec(memory_space=pl.ANY)
    two_squares = pltpu.VMEM((2, slots, lanes), f32)
    sems = pltpu.SemaphoreType.DMA((2, slots // SPAN))
    table = pltpu.VMEM((table_rows, 2 * HEAD_DIM), bf16)
    table_sum = pltpu.VMEM((table_rows, HEAD_DIM), f32)
    square = pltpu.VMEM((slots, lanes), f32)
    columns = jax.ShapeDtypeStruct((steps, 4 * HEAD_DIM, lanes), bf16)
    pairs = jax.ShapeDtypeStruct((steps, lanes, 2 * HEAD_DIM), bf16)

    def by_step(array):
        return pl.BlockSpec((1, *array.shape[1:]), lambda step: (step, 0, 0))

    lists = [pltpu.SMEM((nb, owners + 1), jnp.int32)] * 2 + [pltpu.SMEM((nb,), jnp.int32)]
    params = pltpu.CompilerParams(vmem_limit_bytes=56 * MIB)
    work = 2 * steps * 6 * SPAN * lanes * 2 * HEAD_DIM

    def stage():
        return pl.pallas_call(
            functools.partial(stage_body, nb=nb, group=group, halves=halves),
            grid=(steps,),
            in_specs=[smem_spec] * 2 + [whole_spec(a) for a in (*qs, *gs)],
            out_specs=[by_step(columns), by_step(pairs)] * 2,
            out_shape=[columns, pairs] * 2,
            compiler_params=pltpu.CompilerParams(vmem_limit_bytes=56 * MIB),
            cost_estimate=pl.CostEstimate(flops=8 * steps * lanes * HEAD_DIM, bytes_accessed=16 * steps * lanes * HEAD_DIM, transcendentals=0),
        )(scalars[0], scalars[2], *qs, *gs)

    def soft(staged, keys):
        qt, _, _, g_pairs = staged
        return pl.pallas_call(
            functools.partial(soft_body, conf=value_conf),
            grid=(steps,),
            in_specs=[smem_spec] * 3 + [by_step(qt), by_step(g_pairs)] + [whole_spec(a) for a in keys],
            out_specs=[probs_spec] + [whole_spec(a) for a in value_sums],
            out_shape=[probs] + value_sums,
            scratch_shapes=[table, table_sum, two_squares]
            + lists
            + [sems],
            compiler_params=params,
            cost_estimate=pl.CostEstimate(flops=2 * work, bytes_accessed=4 * rows * width, transcendentals=0),
        )(*scalars, qt, g_pairs, *keys)

    def grad(staged, keys, values, probs_in):
        _, q_pairs, gt, _ = staged
        dq = jax.ShapeDtypeStruct((nb * rows, width), f32)
        return pl.pallas_call(
            functools.partial(grad_body, conf=key_conf),
            grid=(steps,),
            in_specs=[smem_spec] * 3 + [by_step(gt), by_step(q_pairs)] + [whole_spec(a) for a in (*keys, *values)] + [probs_spec],
            out_specs=[pl.BlockSpec((SPAN, width), lambda step: (step, 0))] + [whole_spec(a) for a in key_sums],
            out_shape=[dq] + key_sums,
            scratch_shapes=[
                table,
                table,
                table_sum,
                two_squares,
                square,
                pltpu.VMEM((2 * HEAD_DIM, lanes), f32),
            ]
            + lists
            + [sems],
            compiler_params=params,
            cost_estimate=pl.CostEstimate(flops=4 * work, bytes_accessed=4 * rows * width, transcendentals=0),
        )(*scalars, gt, q_pairs, *keys, *values, probs_in)

    return stage, soft, grad


def flip(array, mask):
    count = lax.axis_size("tok")
    return lax.ppermute(array, "tok", [(index, index ^ mask) for index in range(count)])


def together(*arrays):
    return lax.optimization_barrier(arrays)


def flip_one_way(array, mask, rising):
    count = lax.axis_size("tok")
    pairs = [(index, index ^ mask) for index in range(count) if (index < index ^ mask) == rising]
    return lax.ppermute(array, "tok", pairs)


def gather_square(array, cut, axis):
    across, down = flip(array, 2), flip(array, 4)
    head = lax.slice_in_dim(across, 0, cut, axis=axis)
    tail = lax.slice_in_dim(down, cut, down.shape[axis], axis=axis)
    return across, down, flip(head, 4), flip(tail, 2)


def scatter_square(across, down, corner):
    from_across, from_down = flip(corner[0], 2), flip(corner[1], 4)
    across_head, down_tail = flip(across[0], 2), flip(down[1], 4)
    across_tail, down_head = flip(across[1] + from_down, 2), flip(down[0] + from_across, 4)
    return across_head, down_head, across_tail, down_tail


def shards_paired(hidden, queries, out_grad, w_key, w_value, fork_tile, live_len):
    owners = lax.axis_size("tok")
    depth = lax.axis_size("head")
    tok = lax.axis_index("tok").astype(jnp.int32)
    core = tok & 1
    rows = hidden.shape[0]
    width = queries.shape[1] // 2
    scalars = (tok.reshape(1), fork_tile, live_len)
    place = (tok >> 1) ^ jnp.arange(depth, dtype=jnp.int32)
    cut = w_key.shape[0] // (2 * HEAD_DIM) * HEAD_DIM

    def mine(array):
        return lax.dynamic_slice_in_dim(array, core * width, width, 1)

    def partners(array):
        return flip(lax.dynamic_slice_in_dim(array, (1 - core) * width, width, 1), 1)

    def project_all(w, outs):
        partial = project(place, (0,), xs, ((0, 0),), [w], outs)
        across, down = flip(w, 2), flip(w, 4)
        across, down, *partial = together(across, down, *partial)
        head, tail = flip(across[:cut], 4), flip(down[cut:], 2)
        partial = project(place, (1, 2), xs, ((0, 0), (1, 0)), [across, down], outs, partial)
        return project(place, (3,), xs, ((0, 0), (0, cut)), [head, tail], outs, partial)

    def sum_heads(partial):
        return lax.psum_scatter(partial, "head", scatter_dimension=0, tiled=True)[0]

    def all_heads(grads):
        return lax.all_gather(grads, "head", axis=0, tiled=False)

    def lead(array):
        return jnp.concatenate([array[:, :SPAN], array[:, rows : rows + SPAN]], axis=1)

    def returned(across_head, across_tail, down_head, down_tail, corner_head, corner_tail, own):
        arrivals = scatter_square((across_head, across_tail), (down_head, down_tail), (corner_head, corner_tail))
        plan = tuple((index, 0, rows * (index // 2), SPAN) for index in range(4))
        return combine(own, arrivals, plan)

    def returned_at_once(across, down, corner, own):
        plan = tuple((index, slot * SPAN, slot * rows, SPAN) for index in range(3) for slot in range(2))
        return combine(own, [flip_one_way(across, 2, False), flip_one_way(down, 4, False), flip_one_way(corner, 6, False)], plan)

    def weight(every, xs):
        corner = weight_grad(place, (3,), xs, every)
        across_head, across_tail, down_head, down_tail = weight_grad(place, (1, 2), xs, every)
        kept = weight_grad(place, (0,), xs, every)
        arrivals = scatter_square((across_head, across_tail), (down_head, down_tail), corner)
        return kept, arrivals

    def finish(kept, arrivals):
        across_head, down_head, across_tail, down_tail = arrivals
        return jnp.concatenate([kept[0] + across_head + down_head, kept[1] + across_tail + down_tail], axis=0)

    def home(array):
        kept, received = array[:rows], flip(array[rows:], 1)
        return jnp.where(core == 0, jnp.concatenate([kept, received], axis=1), jnp.concatenate([received, kept], axis=1))

    hidden = hidden.T
    both = [hidden, flip(hidden, 1)]
    xs = [halve(x) for x in both]
    qs = [mine(queries), partners(queries)]
    gs = [mine(out_grad), partners(out_grad)]
    keys = sum_heads(project_all(w_key, 1)[0])
    leading, trailing = map(sum_heads, project_all(w_value, 2))

    base = owners * SPAN
    layout = (
        (0, 0, base, 2 * rows),
        (0, 0, 0, SPAN),
        (0, rows, SPAN, SPAN),
        (1, 0, 2 * SPAN, 2 * SPAN),
        (2, 0, 4 * SPAN, 2 * SPAN),
        (3, 0, 6 * SPAN, SPAN),
        (4, 0, 7 * SPAN, SPAN),
    )
    value_layout = (
        (0, 0, base, SPAN),
        (0, SPAN, base + rows, SPAN),
        (0, 0, 0, 2 * SPAN),
        (1, 0, base + SPAN, SPAN),
        (1, SPAN, base + rows + SPAN, SPAN),
        (2, 0, 2 * SPAN, 2 * SPAN),
        (3, 0, 4 * SPAN, 2 * SPAN),
        (4, 0, 6 * SPAN, 2 * SPAN),
    )
    key_sum_rows = tuple((0, (2 + index) * SPAN, SPAN) for index in range(6))
    value_sum_rows = tuple((0, 2 * (1 + index) * SPAN, 2 * SPAN) for index in range(3))
    stage, soft, grad = attention_calls(scalars, qs, gs, layout, value_layout, key_sum_rows, value_sum_rows, True, owners)

    keys, *staged = together(keys, *stage())
    key_parts = [keys, *gather_square(lead(keys), SPAN, 1)]
    probs, *value_sums = soft(staged, key_parts)
    value_parts = list(together(leading, *value_sums))[:1]
    value_parts += [flip_one_way(value_parts[0], mask, True) for mask in (2, 4, 6)]
    value_grads = returned_at_once(*value_sums)
    probs, value_grads, *value_parts = together(probs, value_grads, *value_parts)
    trailing, value_grads = together(trailing, value_grads)
    every_value = all_heads(value_grads)
    value_parts = [value_parts[0], trailing, *value_parts[1:]]
    grad_query, *key_sums = grad(staged, key_parts, value_parts, probs)
    key_grads = returned(*key_sums)
    every_key = all_heads(key_grads)
    every_value, key_grads = together(every_value, key_grads)
    grad_w_value = finish(*weight(every_value, xs))
    grad_query, grad_key, grad_value = home(grad_query), home(key_grads), home(value_grads)
    *both, grad_w_value = together(*both, grad_w_value)
    late = [halve(x) for x in both]
    every_key, grad_w_value, grad_query, grad_key, grad_value, *late = together(every_key, grad_w_value, grad_query, grad_key, grad_value, *late)
    grad_w_key = finish(*weight(every_key, late))
    return grad_query, grad_key, grad_value, grad_w_key, grad_w_value


def shards_single(hidden, queries, out_grad, w_key, w_value, fork_tile, live_len):
    owners = lax.axis_size("tok")
    tok = lax.axis_index("tok").astype(jnp.int32)
    scalars = (tok.reshape(1), fork_tile, live_len)

    def projected(w):
        every = lax.all_gather(w, "tok", axis=1, tiled=True)
        partial = lax.dot_general(every, hidden, (((0,), (1,)), ((), ())), precision=lax.Precision.HIGHEST)
        return lax.psum_scatter(partial, "head", scatter_dimension=0, tiled=True)

    keys, values = projected(w_key), projected(w_value)
    layout = ((0, 0, owners * SPAN, hidden.shape[0]), (1, 0, 0, owners * SPAN))
    sums = ((0, 0, owners * SPAN),)
    stage, soft, grad = attention_calls(scalars, [queries], [out_grad], layout, layout, sums, sums, False, owners)

    def parts(array):
        return [array, lax.all_gather(array[:, :SPAN], "tok", axis=1, tiled=True)]

    def returned(remote, own):
        return own.at[:SPAN].add(lax.psum_scatter(remote, "tok", scatter_dimension=0, tiled=True))

    def weight(grads):
        every = lax.all_gather(grads, "head", axis=1, tiled=True)
        columns = lax.dot_general(hidden, every, (((0,), (0,)), ((), ())), precision=lax.Precision.HIGHEST)
        return lax.psum_scatter(columns, "tok", scatter_dimension=1, tiled=True)

    staged = stage()
    key_parts = parts(keys)
    probs, *value_sums = soft(staged, key_parts)
    value_grads = returned(*value_sums)
    grad_query, *key_sums = grad(staged, key_parts, parts(values), probs)
    key_grads = returned(*key_sums)
    return grad_query, key_grads, value_grads, weight(key_grads), weight(value_grads)


def shards(hidden, queries, out_grad, w_key, w_value, fork_tile, live_len):
    pairs = lax.axis_size("tok") // 2
    whole_heads = w_key.shape[1] == HEAD_DIM
    paired = whole_heads and pairs == lax.axis_size("head") and pairs == 4
    run = shards_paired if paired else shards_single
    return run(hidden, queries, out_grad, w_key, w_value, fork_tile, live_len)


def solution(mesh):
    placed = (P("tok", "head"), P("tok", "head"), P("tok", "head"), P("head", "tok"), P("head", "tok"), P(), P())
    return jax.shard_map(
        shards,
        mesh=mesh,
        in_specs=placed,
        out_specs=(P("tok", "head"), P("tok", "head"), P("tok", "head"), P("head", "tok"), P("head", "tok")),
        check_vma=False,
    )
```

```python
import functools

import jax
import jax.numpy as jnp
from jax import lax
from jax.experimental import pallas as pl
from jax.experimental.pallas import tpu as pltpu
from jax.sharding import PartitionSpec as P

HEAD_DIM = 128
TILE = 128
CAP = 2
SPAN = CAP * TILE

logit_scale = 168.0 ** (-0.5)
f32 = jnp.float32
bf16 = jnp.bfloat16
MIB = 1024 * 1024


def split(rows):
    high = rows.astype(bf16)
    return high, (rows - high.astype(f32)).astype(bf16)


def pair_cat(rows, axis):
    return jnp.concatenate(split(rows), axis=axis)


def dot(left, right):
    return jnp.dot(left, right, preferred_element_type=f32)


def dot_first(left, right):
    return lax.dot_general(left, right, (((0,), (0,)), ((), ())), preferred_element_type=f32)


def whole_spec(array):
    return pl.BlockSpec(array.shape, lambda *_: (0,) * len(array.shape))


smem_spec = pl.BlockSpec(memory_space=pltpu.SMEM)


def halve_body(x_ref, out_ref):
    out_ref[...] = pair_cat(x_ref[...], 1)


def halve(x):
    depth, rows = x.shape
    block = depth // 4
    return pl.pallas_call(
        halve_body,
        grid=(4,),
        in_specs=[pl.BlockSpec((block, rows), lambda step: (step, 0))],
        out_specs=pl.BlockSpec((block, 2 * rows), lambda step: (step, 0)),
        out_shape=jax.ShapeDtypeStruct((depth, 2 * rows), bf16),
        compiler_params=pltpu.CompilerParams(vmem_limit_bytes=12 * MIB),
        cost_estimate=pl.CostEstimate(flops=4 * x.size, bytes_accessed=8 * x.size, transcendentals=0),
    )(x)


def project_body(place_ref, *refs, row_inputs, pieces, outs):
    x_refs = refs[:row_inputs]
    w_refs = refs[row_inputs : row_inputs + len(pieces)]
    out_refs, pair_ref = refs[-1 - outs : -1], refs[-1]
    step, part_step = pl.program_id(0), pl.program_id(1)
    columns = x_refs[0].shape[1] // 2
    width = columns // outs

    @pl.when((step == 0) & (part_step == 0))
    def _():
        for (part, start), w_ref in zip(pieces, w_refs):
            high, low = split(w_ref[...].T)
            stop = start + w_ref.shape[0]
            pair_ref[part, :HEAD_DIM, start:stop] = high
            pair_ref[part, HEAD_DIM:, start:stop] = low

    for source in range(row_inputs):

        @pl.when(step == source)
        def _():
            total = dot(pair_ref[part_step], x_refs[source][...])
            total = total[:, :columns] + total[:, columns:]
            total = total[:HEAD_DIM] + total[HEAD_DIM:]
            for index, out_ref in enumerate(out_refs):
                out_ref[0] = total[:, index * width : (index + 1) * width]


def project(place, slots, xs, pieces, ws, outs, before=()):
    depth, rows = xs[0].shape
    rows = rows // 2
    first = slots[0]
    width = rows // outs
    inputs = 1 + len(xs) + len(ws)
    return pl.pallas_call(
        functools.partial(project_body, row_inputs=len(xs), pieces=pieces, outs=outs),
        grid_spec=pltpu.PrefetchScalarGridSpec(
            num_scalar_prefetch=1,
            grid=(len(xs), len(slots)),
            in_specs=[whole_spec(x) for x in xs]
            + [whole_spec(w) for w in ws]
            + [pl.BlockSpec(memory_space=pl.ANY)] * len(before),
            out_specs=[pl.BlockSpec((1, HEAD_DIM, width), lambda step, part, place_ref: (place_ref[first + part], 0, step))] * outs,
            scratch_shapes=[pltpu.VMEM((len(slots), 2 * HEAD_DIM, depth), bf16)],
        ),
        out_shape=[jax.ShapeDtypeStruct((place.shape[0], HEAD_DIM, width * len(xs)), f32)] * outs,
        input_output_aliases={inputs + index: index for index in range(len(before))},
        compiler_params=pltpu.CompilerParams(vmem_limit_bytes=18 * MIB),
        cost_estimate=pl.CostEstimate(
            flops=6 * rows * len(xs) * depth * len(slots) * HEAD_DIM, bytes_accessed=4 * rows * len(xs) * depth, transcendentals=0
        ),
    )(place, *xs, *ws, *before)


def weight_grad_body(place_ref, *refs, row_inputs, parts):
    x_refs = refs[:row_inputs]
    g_refs = refs[row_inputs : row_inputs + parts]
    out_refs, pair_ref = refs[row_inputs + parts : -1], refs[-1]
    rows = x_refs[0].shape[1] // 2
    step, half = pl.program_id(0), pl.num_programs(0) // 2

    @pl.when(step == 0)
    def _():
        for part in range(parts):
            pair_ref[:, 2 * part * HEAD_DIM : 2 * (part + 1) * HEAD_DIM] = pair_cat(g_refs[part][0], 1)

    total = 0.0
    for source in range(row_inputs):
        pair = pair_ref[source * rows : (source + 1) * rows]
        total += dot(x_refs[source][:, :rows], pair) + dot(x_refs[source][:, rows:], pair)
    for part in range(parts):
        value = total[:, 2 * part * HEAD_DIM : (2 * part + 1) * HEAD_DIM] + total[:, (2 * part + 1) * HEAD_DIM : 2 * (part + 1) * HEAD_DIM]
        for piece in range(2):

            @pl.when(step // half == piece)
            def _():
                out_refs[2 * part + piece][...] = value


def weight_grad(place, slots, xs, grads):
    depth, rows = xs[0].shape
    rows = rows // 2
    parts = len(slots)
    steps = 4
    half = steps // 2
    block = depth // steps

    def g_map(slot):
        return lambda step, place_ref: (place_ref[slot], 0, 0)

    head = pl.BlockSpec((block, HEAD_DIM), lambda step, place_ref: (jnp.minimum(step, half - 1), 0))
    tail = pl.BlockSpec((block, HEAD_DIM), lambda step, place_ref: (jnp.maximum(step - half, 0), 0))
    return pl.pallas_call(
        functools.partial(weight_grad_body, row_inputs=len(xs), parts=parts),
        grid_spec=pltpu.PrefetchScalarGridSpec(
            num_scalar_prefetch=1,
            grid=(steps,),
            in_specs=[pl.BlockSpec((block, 2 * rows), lambda step, place_ref: (step, 0))] * len(xs)
            + [pl.BlockSpec((1, *grads.shape[1:]), g_map(slot)) for slot in slots],
            out_specs=[head, tail] * parts,
            scratch_shapes=[pltpu.VMEM((rows * len(xs), 2 * parts * HEAD_DIM), bf16)],
        ),
        out_shape=[jax.ShapeDtypeStruct((block * half, HEAD_DIM), f32)] * (2 * parts),
        compiler_params=pltpu.CompilerParams(vmem_limit_bytes=10 * MIB),
        cost_estimate=pl.CostEstimate(
            flops=6 * rows * len(xs) * depth * parts * HEAD_DIM, bytes_accessed=4 * rows * len(xs) * depth, transcendentals=0
        ),
    )(place, *xs, *[grads] * parts)


def combine_body(own_ref, *refs, plan):
    out_ref = refs[-1]
    out_ref[...] = own_ref[...]
    for index, source, target, count in plan:
        out_ref[target : target + count, :] += refs[index][source : source + count, :]


def combine(own, arrivals, plan):
    return pl.pallas_call(
        functools.partial(combine_body, plan=plan),
        out_shape=jax.ShapeDtypeStruct(own.shape, f32),
        compiler_params=pltpu.CompilerParams(vmem_limit_bytes=24 * MIB),
        cost_estimate=pl.CostEstimate(flops=own.size, bytes_accessed=12 * own.size, transcendentals=0),
    )(own, *arrivals)


def list_ancestors(fork_ref, offset_ref, limit_ref, many_ref, tok, slots, tiles, paired):
    for slot in range(slots):

        def climb(carry, slot=slot):
            current, count = carry
            fork_at = fork_ref[current - 1]
            parent = lax.div(fork_at, jnp.int32(tiles))
            offset_ref[slot, count] = ((tok ^ parent) if paired else parent) * SPAN
            limit_ref[slot, count] = (lax.rem(fork_at, jnp.int32(tiles)) + 1) * TILE - 1
            return parent, count + 1

        _, count = lax.while_loop(lambda carry: carry[0] > 0, climb, (tok ^ slot, jnp.int32(0)))
        many_ref[slot] = count
        offset_ref[slot, count] = 0
        limit_ref[slot, count] = -1


def find_step(many_ref, step, tok, halves):
    slot, half = lax.div(step, jnp.int32(halves)), lax.rem(step, jnp.int32(halves))
    return tok ^ slot, slot, half, half + 1 + many_ref[slot]


def block_offset(offset_ref, base, slot, half, halves, block):
    later = jnp.maximum(block - half - 1, 0)
    return jnp.where(block <= half, base + (slot * halves + block) * SPAN, offset_ref[slot, later])


def even(count):
    return 2 * lax.div(count + 1, jnp.int32(2))


def paired_loop(count, body, start, before=None):
    def both(pair, carry):
        if before is not None:
            before(2 * pair)
            before(2 * pair + 1)
        return body(2 * pair + 1, body(2 * pair, carry))

    return lax.fori_loop(0, lax.div(count + 1, jnp.int32(2)), both, start)


def key_limits(limit_ref, slot, half, live, block, lanes):
    lane = lax.broadcasted_iota(jnp.int32, (1, lanes), 1)
    position = half * SPAN + lax.rem(lane, jnp.int32(SPAN))
    own_limit = jnp.minimum(position, live - 1) - block * SPAN
    return jnp.where(block <= half, own_limit, limit_ref[slot, jnp.maximum(block - half - 1, 0)])


def transposed_pair(rows):
    high, low = split(rows.T)
    return jnp.concatenate([high, high, low, low], axis=0)


def load_rows(ref, half, head):
    return ref[pl.ds(pl.multiple_of(half * SPAN, SPAN), SPAN), head * HEAD_DIM : (head + 1) * HEAD_DIM]


def live_column(half, live):
    position = half * SPAN + lax.broadcasted_iota(jnp.int32, (SPAN, 1), 0)
    return (position < live).astype(f32)


def block_rows(ref, offset):
    return ref[pl.ds(pl.multiple_of(offset, SPAN), SPAN), :]


def slot_rows(block):
    return pl.ds(pl.multiple_of(block * SPAN, SPAN), SPAN)


def stage_rows(target_ref, source_refs, layout):
    for index, start, offset, count in layout:
        for piece in range(0, count, SPAN):
            target_ref[offset + piece : offset + piece + SPAN, :] = pair_cat(
                source_refs[index][:, start + piece : start + piece + SPAN].T, 1
            )


def write_rows(source_ref, target_refs, layout, sums):
    for target_ref, (start, offset, count) in zip(target_refs, sums):
        target_ref[start : start + count, :] = source_ref[offset : offset + count, :]
    own = layout[0]
    target_refs[-1][...] = source_ref[own[2] : own[2] + own[3], :]
    for index, start, offset, count in layout[1:]:
        if index == 0:
            target_refs[-1][start : start + count, :] += source_ref[offset : offset + count, :]


def scores(keys_ref, offset, queries, limits):
    keys = block_rows(keys_ref, offset)
    result = dot(jnp.concatenate([keys, keys], axis=1), queries)
    row = lax.broadcasted_iota(jnp.int32, result.shape, 0)
    return jnp.where(row <= limits, result, -1e30)


def fold(value, how):
    return how(value.reshape(SPAN // 8, 8, value.shape[1]), axis=0)


def stage_body(tok_ref, live_ref, *refs, nb, group, halves):
    q_refs, g_refs = refs[:nb], refs[nb : 2 * nb]
    qt_ref, q_ref, gt_ref, grad_ref = refs[2 * nb :]
    step = pl.program_id(0)
    slot, half = lax.div(step, jnp.int32(halves)), lax.rem(step, jnp.int32(halves))
    live = live_ref[tok_ref[0] ^ slot]
    for source in range(nb):

        @pl.when(slot == source)
        def _():
            for head in range(group):
                part = slice(head * SPAN, (head + 1) * SPAN)
                rows = load_rows(q_refs[source], half, head) * logit_scale
                qt_ref[0, :, part] = transposed_pair(rows)
                q_ref[0, part, :] = pair_cat(rows, 1)
                rows = load_rows(g_refs[source], half, head) * live_column(half, live)
                gt_ref[0, :, part] = transposed_pair(rows)
                grad_ref[0, part, :] = pair_cat(rows, 1)


def soft_body(tok_ref, fork_ref, live_ref, *refs, conf):
    nb, group, owners, layout, sources, outs = conf["nb"], conf["group"], conf["owners"], conf["layout"], conf["sources"], conf["outs"]
    halves = conf["rows"] // SPAN
    lanes = group * SPAN
    qt_ref, grad_ref = refs[:2]
    key_refs = refs[2 : 2 + sources]
    prob_ref = refs[2 + sources]
    out_refs = refs[3 + sources : 3 + sources + outs]
    keys_ref, sum_ref, scores_ref, offset_ref, limit_ref, many_ref, sems = refs[3 + sources + outs :]
    step = pl.program_id(0)
    tok = tok_ref[0]
    turn = lax.rem(step, 2)
    score_ref = scores_ref.at[turn]

    def copy_out(of_step, block):
        side = lax.rem(of_step, 2)
        rows = slot_rows(block)
        return pltpu.make_async_copy(scores_ref.at[side, rows], prob_ref.at[of_step, rows], sems.at[side, block])

    def wait_out(of_step):
        def wait(block, _):
            copy_out(of_step, block).wait()
            return 0

        lax.fori_loop(0, even(find_step(many_ref, of_step, tok, halves)[3]), wait, 0)

    @pl.when(step == 0)
    def _():
        list_ancestors(fork_ref, offset_ref, limit_ref, many_ref, tok, nb, conf["rows"] // TILE, conf["paired"])
        stage_rows(keys_ref, key_refs, layout)
        sum_ref[...] = jnp.zeros_like(sum_ref)

    branch, slot, half, count = find_step(many_ref, step, tok, halves)
    place_of = functools.partial(block_offset, offset_ref, owners * SPAN, slot, half, halves)
    live = live_ref[branch]
    def first(block, largest):
        value = scores(keys_ref, place_of(block), qt_ref[0], key_limits(limit_ref, slot, half, live, block, lanes))
        score_ref[slot_rows(block), :] = value
        return jnp.maximum(largest, fold(value, jnp.max))

    largest = paired_loop(count, first, jnp.full((8, lanes), -1e30, f32))
    largest = jnp.max(largest, axis=0, keepdims=True)

    def second(block, total):
        value = jnp.exp(score_ref[slot_rows(block), :] - largest)
        score_ref[slot_rows(block), :] = value
        return total + fold(value, jnp.sum)

    total = paired_loop(count, second, jnp.zeros((8, lanes), f32))
    inverse = 1.0 / jnp.sum(total, axis=0, keepdims=True)

    def third(block, _):
        prob = score_ref[slot_rows(block), :] * inverse
        score_ref[slot_rows(block), :] = prob
        copy_out(step, block).start()
        high, low = split(prob)
        grads = grad_ref[0]
        both = dot(high, grads) + dot(low, grads)
        offset = place_of(block)
        sum_ref[slot_rows(offset // SPAN), :] += both[:, :HEAD_DIM] + both[:, HEAD_DIM:]
        return 0

    paired_loop(count, third, 0)

    @pl.when(step > 0)
    def _():
        wait_out(step - 1)

    @pl.when(step == nb * halves - 1)
    def _():
        wait_out(step)
        write_rows(sum_ref, out_refs, layout, conf["sums"])


def grad_body(tok_ref, fork_ref, live_ref, *refs, conf):
    nb, group, owners, layout, sources, outs = conf["nb"], conf["group"], conf["owners"], conf["layout"], conf["sources"], conf["outs"]
    halves = conf["rows"] // SPAN
    lanes = group * SPAN
    gt_ref, q_ref = refs[:2]
    at = 2
    value_sources = conf["value_sources"]
    key_refs, value_refs = refs[at : at + sources], refs[at + sources : at + sources + value_sources]
    at += sources + value_sources
    prob_ref = refs[at]
    dq_ref = refs[at + 1]
    out_refs = refs[at + 2 : at + 2 + outs]
    (keys_ref, values_ref, sum_ref, probs_ref, dprob_ref, dqt_ref, offset_ref, limit_ref, many_ref, sems) = refs[at + 2 + outs :]
    step = pl.program_id(0)
    tok = tok_ref[0]
    held_ref = probs_ref.at[lax.rem(step, 2)]

    def copy_in(of_step, block):
        side = lax.rem(of_step, 2)
        rows = slot_rows(block)
        return pltpu.make_async_copy(prob_ref.at[of_step, rows], probs_ref.at[side, rows], sems.at[side, block])

    def start_in(of_step):
        def start(block, _):
            copy_in(of_step, block).start()
            return 0

        lax.fori_loop(0, even(find_step(many_ref, of_step, tok, halves)[3]), start, 0)

    @pl.when(step == 0)
    def _():
        list_ancestors(fork_ref, offset_ref, limit_ref, many_ref, tok, nb, conf["rows"] // TILE, conf["paired"])
        start_in(step)
        stage_rows(keys_ref, key_refs, layout)
        stage_rows(values_ref, value_refs, conf["value_layout"])
        sum_ref[...] = jnp.zeros_like(sum_ref)

    @pl.when(step < nb * halves - 1)
    def _():
        start_in(step + 1)

    branch, slot, half, count = find_step(many_ref, step, tok, halves)
    place_of = functools.partial(block_offset, offset_ref, owners * SPAN, slot, half, halves)
    def first(block, delta):
        values = block_rows(values_ref, place_of(block))
        dprob = dot(jnp.concatenate([values, values], axis=1), gt_ref[0])
        dprob_ref[slot_rows(block), :] = dprob
        return delta + fold(held_ref[slot_rows(block), :] * dprob, jnp.sum)

    delta = paired_loop(count, first, jnp.zeros((8, lanes), f32), lambda block: copy_in(step, block).wait())
    delta = jnp.sum(delta, axis=0, keepdims=True)
    dqt_ref[...] = jnp.zeros_like(dqt_ref)

    def second(block, _):
        offset = place_of(block)
        high, low = split(held_ref[slot_rows(block), :] * (dprob_ref[slot_rows(block), :] - delta))
        rows = q_ref[0]
        both = dot(high, rows) + dot(low, rows)
        sum_ref[slot_rows(offset // SPAN), :] += both[:, :HEAD_DIM] + both[:, HEAD_DIM:]
        keys = block_rows(keys_ref, offset)
        dqt_ref[...] += dot_first(keys, high) + dot_first(keys, low)
        return 0

    paired_loop(count, second, 0)
    folded = (dqt_ref[:HEAD_DIM, :] + dqt_ref[HEAD_DIM:, :]) * logit_scale
    for head in range(group):
        dq_ref[:, head * HEAD_DIM : (head + 1) * HEAD_DIM] = folded[:, head * SPAN : (head + 1) * SPAN].T

    @pl.when(step == nb * halves - 1)
    def _():
        write_rows(sum_ref, out_refs, layout, conf["sums"])


def attention_calls(scalars, qs, gs, layout, value_layout, key_sum_rows, value_sum_rows, paired, owners):
    rows, width = qs[0].shape
    nb, group, halves = len(qs), width // HEAD_DIM, rows // SPAN
    lanes = group * SPAN
    steps = nb * halves
    conf = dict(nb=nb, group=group, rows=rows, owners=owners, layout=layout, value_layout=value_layout, paired=paired)
    conf["sources"] = 1 + max(entry[0] for entry in layout)
    conf["value_sources"] = 1 + max(entry[0] for entry in value_layout)
    table_rows = owners * SPAN + nb * rows
    slots = (owners + halves) * SPAN

    def sums_of(sum_rows):
        shapes = [jax.ShapeDtypeStruct((count, HEAD_DIM), f32) for _, _, count in sum_rows]
        return shapes + [jax.ShapeDtypeStruct((nb * rows, HEAD_DIM), f32)], dict(conf, sums=sum_rows, outs=len(sum_rows) + 1)

    key_sums, key_conf = sums_of(key_sum_rows)
    value_sums, value_conf = sums_of(value_sum_rows)
    probs = jax.ShapeDtypeStruct((steps, slots, lanes), f32)
    probs_spec = pl.BlockSpec(memory_space=pl.ANY)
    two_squares = pltpu.VMEM((2, slots, lanes), f32)
    sems = pltpu.SemaphoreType.DMA((2, slots // SPAN))
    table = pltpu.VMEM((table_rows, 2 * HEAD_DIM), bf16)
    table_sum = pltpu.VMEM((table_rows, HEAD_DIM), f32)
    square = pltpu.VMEM((slots, lanes), f32)
    columns = jax.ShapeDtypeStruct((steps, 4 * HEAD_DIM, lanes), bf16)
    pairs = jax.ShapeDtypeStruct((steps, lanes, 2 * HEAD_DIM), bf16)

    def by_step(array):
        return pl.BlockSpec((1, *array.shape[1:]), lambda step: (step, 0, 0))

    lists = [pltpu.SMEM((nb, owners + 1), jnp.int32)] * 2 + [pltpu.SMEM((nb,), jnp.int32)]
    params = pltpu.CompilerParams(vmem_limit_bytes=56 * MIB)
    work = 2 * steps * 6 * SPAN * lanes * 2 * HEAD_DIM

    def stage():
        return pl.pallas_call(
            functools.partial(stage_body, nb=nb, group=group, halves=halves),
            grid=(steps,),
            in_specs=[smem_spec] * 2 + [whole_spec(a) for a in (*qs, *gs)],
            out_specs=[by_step(columns), by_step(pairs)] * 2,
            out_shape=[columns, pairs] * 2,
            compiler_params=pltpu.CompilerParams(vmem_limit_bytes=56 * MIB),
            cost_estimate=pl.CostEstimate(flops=8 * steps * lanes * HEAD_DIM, bytes_accessed=16 * steps * lanes * HEAD_DIM, transcendentals=0),
        )(scalars[0], scalars[2], *qs, *gs)

    def soft(staged, keys):
        qt, _, _, g_pairs = staged
        return pl.pallas_call(
            functools.partial(soft_body, conf=value_conf),
            grid=(steps,),
            in_specs=[smem_spec] * 3 + [by_step(qt), by_step(g_pairs)] + [whole_spec(a) for a in keys],
            out_specs=[probs_spec] + [whole_spec(a) for a in value_sums],
            out_shape=[probs] + value_sums,
            scratch_shapes=[table, table_sum, two_squares]
            + lists
            + [sems],
            compiler_params=params,
            cost_estimate=pl.CostEstimate(flops=2 * work, bytes_accessed=4 * rows * width, transcendentals=0),
        )(*scalars, qt, g_pairs, *keys)

    def grad(staged, keys, values, probs_in):
        _, q_pairs, gt, _ = staged
        dq = jax.ShapeDtypeStruct((nb * rows, width), f32)
        return pl.pallas_call(
            functools.partial(grad_body, conf=key_conf),
            grid=(steps,),
            in_specs=[smem_spec] * 3 + [by_step(gt), by_step(q_pairs)] + [whole_spec(a) for a in (*keys, *values)] + [probs_spec],
            out_specs=[pl.BlockSpec((SPAN, width), lambda step: (step, 0))] + [whole_spec(a) for a in key_sums],
            out_shape=[dq] + key_sums,
            scratch_shapes=[
                table,
                table,
                table_sum,
                two_squares,
                square,
                pltpu.VMEM((2 * HEAD_DIM, lanes), f32),
            ]
            + lists
            + [sems],
            compiler_params=params,
            cost_estimate=pl.CostEstimate(flops=4 * work, bytes_accessed=4 * rows * width, transcendentals=0),
        )(*scalars, gt, q_pairs, *keys, *values, probs_in)

    return stage, soft, grad


def flip(array, mask):
    count = lax.axis_size("tok")
    return lax.ppermute(array, "tok", [(index, index ^ mask) for index in range(count)])


def together(*arrays):
    return lax.optimization_barrier(arrays)


def flip_one_way(array, mask, rising):
    count = lax.axis_size("tok")
    pairs = [(index, index ^ mask) for index in range(count) if (index < index ^ mask) == rising]
    return lax.ppermute(array, "tok", pairs)


def gather_square(array, cut, axis):
    across, down = flip(array, 2), flip(array, 4)
    head = lax.slice_in_dim(across, 0, cut, axis=axis)
    tail = lax.slice_in_dim(down, cut, down.shape[axis], axis=axis)
    return across, down, flip(head, 4), flip(tail, 2)


def scatter_square(across, down, corner):
    from_across, from_down = flip(corner[0], 2), flip(corner[1], 4)
    across_head, down_tail = flip(across[0], 2), flip(down[1], 4)
    across_tail, down_head = flip(across[1] + from_down, 2), flip(down[0] + from_across, 4)
    return across_head, down_head, across_tail, down_tail


def shards_paired(hidden, queries, out_grad, w_key, w_value, fork_tile, live_len):
    owners = lax.axis_size("tok")
    depth = lax.axis_size("head")
    tok = lax.axis_index("tok").astype(jnp.int32)
    core = tok & 1
    rows = hidden.shape[0]
    width = queries.shape[1] // 2
    scalars = (tok.reshape(1), fork_tile, live_len)
    place = (tok >> 1) ^ jnp.arange(depth, dtype=jnp.int32)
    cut = w_key.shape[0] // (2 * HEAD_DIM) * HEAD_DIM

    def mine(array):
        return lax.dynamic_slice_in_dim(array, core * width, width, 1)

    def partners(array):
        return flip(lax.dynamic_slice_in_dim(array, (1 - core) * width, width, 1), 1)

    def project_all(w, outs):
        partial = project(place, (0,), xs, ((0, 0),), [w], outs)
        across, down = flip(w, 2), flip(w, 4)
        across, down, *partial = together(across, down, *partial)
        head, tail = flip(across[:cut], 4), flip(down[cut:], 2)
        partial = project(place, (1, 2), xs, ((0, 0), (1, 0)), [across, down], outs, partial)
        return project(place, (3,), xs, ((0, 0), (0, cut)), [head, tail], outs, partial)

    def sum_heads(partial):
        return lax.psum_scatter(partial, "head", scatter_dimension=0, tiled=True)[0]

    def all_heads(grads):
        return lax.all_gather(grads, "head", axis=0, tiled=False)

    def lead(array):
        return jnp.concatenate([array[:, :SPAN], array[:, rows : rows + SPAN]], axis=1)

    def returned(across_head, across_tail, down_head, down_tail, corner_head, corner_tail, own):
        arrivals = scatter_square((across_head, across_tail), (down_head, down_tail), (corner_head, corner_tail))
        plan = tuple((index, 0, rows * (index // 2), SPAN) for index in range(4))
        return combine(own, arrivals, plan)

    def returned_at_once(across, down, corner, own):
        plan = tuple((index, slot * SPAN, slot * rows, SPAN) for index in range(3) for slot in range(2))
        return combine(own, [flip_one_way(across, 2, False), flip_one_way(down, 4, False), flip_one_way(corner, 6, False)], plan)

    def weight(every, xs):
        first = lax.dynamic_index_in_dim(every, place[3], 0, keepdims=True)
        corner = weight_grad(jnp.zeros_like(place), (0,), xs, first)
        across_head, across_tail, down_head, down_tail = weight_grad(place, (1, 2), xs, every)
        kept = weight_grad(place, (0,), xs, every)
        arrivals = scatter_square((across_head, across_tail), (down_head, down_tail), corner)
        return kept, arrivals

    def finish(kept, arrivals):
        across_head, down_head, across_tail, down_tail = arrivals
        return jnp.concatenate([kept[0] + across_head + down_head, kept[1] + across_tail + down_tail], axis=0)

    def home(array):
        kept, received = array[:rows], flip(array[rows:], 1)
        return jnp.where(core == 0, jnp.concatenate([kept, received], axis=1), jnp.concatenate([received, kept], axis=1))

    hidden = hidden.T
    both = [hidden, flip(hidden, 1)]
    xs = [halve(x) for x in both]
    qs = [mine(queries), partners(queries)]
    gs = [mine(out_grad), partners(out_grad)]
    keys = sum_heads(project_all(w_key, 1)[0])
    leading, trailing = map(sum_heads, project_all(w_value, 2))

    base = owners * SPAN
    layout = (
        (0, 0, base, 2 * rows),
        (0, 0, 0, SPAN),
        (0, rows, SPAN, SPAN),
        (1, 0, 2 * SPAN, 2 * SPAN),
        (2, 0, 4 * SPAN, 2 * SPAN),
        (3, 0, 6 * SPAN, SPAN),
        (4, 0, 7 * SPAN, SPAN),
    )
    value_layout = (
        (0, 0, base, SPAN),
        (0, SPAN, base + rows, SPAN),
        (0, 0, 0, 2 * SPAN),
        (1, 0, base + SPAN, SPAN),
        (1, SPAN, base + rows + SPAN, SPAN),
        (2, 0, 2 * SPAN, 2 * SPAN),
        (3, 0, 4 * SPAN, 2 * SPAN),
        (4, 0, 6 * SPAN, 2 * SPAN),
    )
    key_sum_rows = tuple((0, (2 + index) * SPAN, SPAN) for index in range(6))
    value_sum_rows = tuple((0, 2 * (1 + index) * SPAN, 2 * SPAN) for index in range(3))
    stage, soft, grad = attention_calls(scalars, qs, gs, layout, value_layout, key_sum_rows, value_sum_rows, True, owners)

    keys, *staged = together(keys, *stage())
    key_parts = [keys, *gather_square(lead(keys), SPAN, 1)]
    probs, *value_sums = soft(staged, key_parts)
    value_parts = list(together(leading, *value_sums))[:1]
    value_parts += [flip_one_way(value_parts[0], mask, True) for mask in (2, 4, 6)]
    value_grads = returned_at_once(*value_sums)
    probs, value_grads, *value_parts = together(probs, value_grads, *value_parts)
    trailing, value_grads = together(trailing, value_grads)
    every_value = all_heads(value_grads)
    value_parts = [value_parts[0], trailing, *value_parts[1:]]
    grad_query, *key_sums = grad(staged, key_parts, value_parts, probs)
    key_grads = returned(*key_sums)
    every_key = all_heads(key_grads)
    every_value, key_grads = together(every_value, key_grads)
    grad_w_value = finish(*weight(every_value, xs))
    grad_query, grad_key, grad_value = home(grad_query), home(key_grads), home(value_grads)
    *both, grad_w_value = together(*both, grad_w_value)
    late = [halve(x) for x in both]
    every_key, grad_w_value, grad_query, grad_key, grad_value, *late = together(every_key, grad_w_value, grad_query, grad_key, grad_value, *late)
    grad_w_key = finish(*weight(every_key, late))
    return grad_query, grad_key, grad_value, grad_w_key, grad_w_value


def shards_single(hidden, queries, out_grad, w_key, w_value, fork_tile, live_len):
    owners = lax.axis_size("tok")
    tok = lax.axis_index("tok").astype(jnp.int32)
    scalars = (tok.reshape(1), fork_tile, live_len)

    def projected(w):
        every = lax.all_gather(w, "tok", axis=1, tiled=True)
        partial = lax.dot_general(every, hidden, (((0,), (1,)), ((), ())), precision=lax.Precision.HIGHEST)
        return lax.psum_scatter(partial, "head", scatter_dimension=0, tiled=True)

    keys, values = projected(w_key), projected(w_value)
    layout = ((0, 0, owners * SPAN, hidden.shape[0]), (1, 0, 0, owners * SPAN))
    sums = ((0, 0, owners * SPAN),)
    stage, soft, grad = attention_calls(scalars, [queries], [out_grad], layout, layout, sums, sums, False, owners)

    def parts(array):
        return [array, lax.all_gather(array[:, :SPAN], "tok", axis=1, tiled=True)]

    def returned(remote, own):
        return own.at[:SPAN].add(lax.psum_scatter(remote, "tok", scatter_dimension=0, tiled=True))

    def weight(grads):
        every = lax.all_gather(grads, "head", axis=1, tiled=True)
        columns = lax.dot_general(hidden, every, (((0,), (0,)), ((), ())), precision=lax.Precision.HIGHEST)
        return lax.psum_scatter(columns, "tok", scatter_dimension=1, tiled=True)

    staged = stage()
    key_parts = parts(keys)
    probs, *value_sums = soft(staged, key_parts)
    value_grads = returned(*value_sums)
    grad_query, *key_sums = grad(staged, key_parts, parts(values), probs)
    key_grads = returned(*key_sums)
    return grad_query, key_grads, value_grads, weight(key_grads), weight(value_grads)


def shards(hidden, queries, out_grad, w_key, w_value, fork_tile, live_len):
    pairs = lax.axis_size("tok") // 2
    whole_heads = w_key.shape[1] == HEAD_DIM
    paired = whole_heads and pairs == lax.axis_size("head") and pairs == 4
    run = shards_paired if paired else shards_single
    return run(hidden, queries, out_grad, w_key, w_value, fork_tile, live_len)


def solution(mesh):
    placed = (P("tok", "head"), P("tok", "head"), P("tok", "head"), P("head", "tok"), P("head", "tok"), P(), P())
    return jax.shard_map(
        shards,
        mesh=mesh,
        in_specs=placed,
        out_specs=(P("tok", "head"), P("tok", "head"), P("tok", "head"), P("head", "tok"), P("head", "tok")),
        check_vma=False,
    )
```

```python
import functools

import jax
import jax.numpy as jnp
from jax import lax
from jax.experimental import pallas as pl
from jax.experimental.pallas import tpu as pltpu
from jax.sharding import PartitionSpec as P

HEAD_DIM = 128
TILE = 128
CAP = 2
SPAN = CAP * TILE

logit_scale = 168.0 ** (-0.5)
f32 = jnp.float32
bf16 = jnp.bfloat16
MIB = 1024 * 1024


def split(rows):
    high = rows.astype(bf16)
    return high, (rows - high.astype(f32)).astype(bf16)


def pair_cat(rows, axis):
    return jnp.concatenate(split(rows), axis=axis)


def dot(left, right):
    return jnp.dot(left, right, preferred_element_type=f32)


def dot_first(left, right):
    return lax.dot_general(left, right, (((0,), (0,)), ((), ())), preferred_element_type=f32)


def whole_spec(array):
    return pl.BlockSpec(array.shape, lambda *_: (0,) * len(array.shape))


smem_spec = pl.BlockSpec(memory_space=pltpu.SMEM)


def halve_body(x_ref, out_ref):
    out_ref[...] = pair_cat(x_ref[...], 1)


def halve(x):
    depth, rows = x.shape
    block = depth // 4
    return pl.pallas_call(
        halve_body,
        grid=(4,),
        in_specs=[pl.BlockSpec((block, rows), lambda step: (step, 0))],
        out_specs=pl.BlockSpec((block, 2 * rows), lambda step: (step, 0)),
        out_shape=jax.ShapeDtypeStruct((depth, 2 * rows), bf16),
        compiler_params=pltpu.CompilerParams(vmem_limit_bytes=12 * MIB),
        cost_estimate=pl.CostEstimate(flops=4 * x.size, bytes_accessed=8 * x.size, transcendentals=0),
    )(x)


def project_body(place_ref, *refs, row_inputs, pieces, outs):
    x_refs = refs[:row_inputs]
    w_refs = refs[row_inputs : row_inputs + len(pieces)]
    out_refs, pair_ref = refs[-1 - outs : -1], refs[-1]
    step, part_step = pl.program_id(0), pl.program_id(1)
    columns = x_refs[0].shape[1] // 2
    width = columns // outs

    @pl.when((step == 0) & (part_step == 0))
    def _():
        for (part, start), w_ref in zip(pieces, w_refs):
            high, low = split(w_ref[...].T)
            stop = start + w_ref.shape[0]
            pair_ref[part, :HEAD_DIM, start:stop] = high
            pair_ref[part, HEAD_DIM:, start:stop] = low

    for source in range(row_inputs):

        @pl.when(step == source)
        def _():
            total = dot(pair_ref[part_step], x_refs[source][...])
            total = total[:, :columns] + total[:, columns:]
            total = total[:HEAD_DIM] + total[HEAD_DIM:]
            for index, out_ref in enumerate(out_refs):
                out_ref[0] = total[:, index * width : (index + 1) * width]


def project(place, slots, xs, pieces, ws, outs, before=()):
    depth, rows = xs[0].shape
    rows = rows // 2
    first = slots[0]
    width = rows // outs
    inputs = 1 + len(xs) + len(ws)
    return pl.pallas_call(
        functools.partial(project_body, row_inputs=len(xs), pieces=pieces, outs=outs),
        grid_spec=pltpu.PrefetchScalarGridSpec(
            num_scalar_prefetch=1,
            grid=(len(xs), len(slots)),
            in_specs=[whole_spec(x) for x in xs]
            + [whole_spec(w) for w in ws]
            + [pl.BlockSpec(memory_space=pl.ANY)] * len(before),
            out_specs=[pl.BlockSpec((1, HEAD_DIM, width), lambda step, part, place_ref: (place_ref[first + part], 0, step))] * outs,
            scratch_shapes=[pltpu.VMEM((len(slots), 2 * HEAD_DIM, depth), bf16)],
        ),
        out_shape=[jax.ShapeDtypeStruct((place.shape[0], HEAD_DIM, width * len(xs)), f32)] * outs,
        input_output_aliases={inputs + index: index for index in range(len(before))},
        compiler_params=pltpu.CompilerParams(vmem_limit_bytes=18 * MIB),
        cost_estimate=pl.CostEstimate(
            flops=6 * rows * len(xs) * depth * len(slots) * HEAD_DIM, bytes_accessed=4 * rows * len(xs) * depth, transcendentals=0
        ),
    )(place, *xs, *ws, *before)


def weight_grad_body(place_ref, *refs, row_inputs, parts):
    x_refs = refs[:row_inputs]
    g_refs = refs[row_inputs : row_inputs + parts]
    out_refs, pair_ref = refs[row_inputs + parts : -1], refs[-1]
    rows = x_refs[0].shape[1] // 2
    step, half = pl.program_id(0), pl.num_programs(0) // 2

    @pl.when(step == 0)
    def _():
        for part in range(parts):
            pair_ref[:, 2 * part * HEAD_DIM : 2 * (part + 1) * HEAD_DIM] = pair_cat(g_refs[part][0], 1)

    total = 0.0
    for source in range(row_inputs):
        pair = pair_ref[source * rows : (source + 1) * rows]
        total += dot(x_refs[source][:, :rows], pair) + dot(x_refs[source][:, rows:], pair)
    for part in range(parts):
        value = total[:, 2 * part * HEAD_DIM : (2 * part + 1) * HEAD_DIM] + total[:, (2 * part + 1) * HEAD_DIM : 2 * (part + 1) * HEAD_DIM]
        for piece in range(2):

            @pl.when(step // half == piece)
            def _():
                out_refs[2 * part + piece][...] = value


def weight_grad(place, slots, xs, grads):
    depth, rows = xs[0].shape
    rows = rows // 2
    parts = len(slots)
    steps = 2
    half = steps // 2
    block = depth // steps

    def g_map(slot):
        return lambda step, place_ref: (place_ref[slot], 0, 0)

    head = pl.BlockSpec((block, HEAD_DIM), lambda step, place_ref: (jnp.minimum(step, half - 1), 0))
    tail = pl.BlockSpec((block, HEAD_DIM), lambda step, place_ref: (jnp.maximum(step - half, 0), 0))
    return pl.pallas_call(
        functools.partial(weight_grad_body, row_inputs=len(xs), parts=parts),
        grid_spec=pltpu.PrefetchScalarGridSpec(
            num_scalar_prefetch=1,
            grid=(steps,),
            in_specs=[pl.BlockSpec((block, 2 * rows), lambda step, place_ref: (step, 0))] * len(xs)
            + [pl.BlockSpec((1, *grads.shape[1:]), g_map(slot)) for slot in slots],
            out_specs=[head, tail] * parts,
            scratch_shapes=[pltpu.VMEM((rows * len(xs), 2 * parts * HEAD_DIM), bf16)],
        ),
        out_shape=[jax.ShapeDtypeStruct((block * half, HEAD_DIM), f32)] * (2 * parts),
        compiler_params=pltpu.CompilerParams(vmem_limit_bytes=16 * MIB),
        cost_estimate=pl.CostEstimate(
            flops=6 * rows * len(xs) * depth * parts * HEAD_DIM, bytes_accessed=4 * rows * len(xs) * depth, transcendentals=0
        ),
    )(place, *xs, *[grads] * parts)


def combine_body(own_ref, *refs, plan):
    out_ref = refs[-1]
    out_ref[...] = own_ref[...]
    for index, source, target, count in plan:
        out_ref[target : target + count, :] += refs[index][source : source + count, :]


def combine(own, arrivals, plan):
    return pl.pallas_call(
        functools.partial(combine_body, plan=plan),
        out_shape=jax.ShapeDtypeStruct(own.shape, f32),
        compiler_params=pltpu.CompilerParams(vmem_limit_bytes=24 * MIB),
        cost_estimate=pl.CostEstimate(flops=own.size, bytes_accessed=12 * own.size, transcendentals=0),
    )(own, *arrivals)


def list_ancestors(fork_ref, offset_ref, limit_ref, many_ref, tok, slots, tiles, paired):
    for slot in range(slots):

        def climb(carry, slot=slot):
            current, count = carry
            fork_at = fork_ref[current - 1]
            parent = lax.div(fork_at, jnp.int32(tiles))
            offset_ref[slot, count] = ((tok ^ parent) if paired else parent) * SPAN
            limit_ref[slot, count] = (lax.rem(fork_at, jnp.int32(tiles)) + 1) * TILE - 1
            return parent, count + 1

        _, count = lax.while_loop(lambda carry: carry[0] > 0, climb, (tok ^ slot, jnp.int32(0)))
        many_ref[slot] = count
        offset_ref[slot, count] = 0
        limit_ref[slot, count] = -1


def find_step(many_ref, step, tok, halves):
    slot, half = lax.div(step, jnp.int32(halves)), lax.rem(step, jnp.int32(halves))
    return tok ^ slot, slot, half, half + 1 + many_ref[slot]


def block_offset(offset_ref, base, slot, half, halves, block):
    later = jnp.maximum(block - half - 1, 0)
    return jnp.where(block <= half, base + (slot * halves + block) * SPAN, offset_ref[slot, later])


def even(count):
    return 2 * lax.div(count + 1, jnp.int32(2))


def paired_loop(count, body, start, before=None):
    def both(pair, carry):
        if before is not None:
            before(2 * pair)
            before(2 * pair + 1)
        return body(2 * pair + 1, body(2 * pair, carry))

    return lax.fori_loop(0, lax.div(count + 1, jnp.int32(2)), both, start)


def key_limits(limit_ref, slot, half, live, block, lanes):
    lane = lax.broadcasted_iota(jnp.int32, (1, lanes), 1)
    position = half * SPAN + lax.rem(lane, jnp.int32(SPAN))
    own_limit = jnp.minimum(position, live - 1) - block * SPAN
    return jnp.where(block <= half, own_limit, limit_ref[slot, jnp.maximum(block - half - 1, 0)])


def transposed_pair(rows):
    high, low = split(rows.T)
    return jnp.concatenate([high, high, low, low], axis=0)


def load_rows(ref, half, head):
    return ref[pl.ds(pl.multiple_of(half * SPAN, SPAN), SPAN), head * HEAD_DIM : (head + 1) * HEAD_DIM]


def live_column(half, live):
    position = half * SPAN + lax.broadcasted_iota(jnp.int32, (SPAN, 1), 0)
    return (position < live).astype(f32)


def block_rows(ref, offset):
    return ref[pl.ds(pl.multiple_of(offset, SPAN), SPAN), :]


def slot_rows(block):
    return pl.ds(pl.multiple_of(block * SPAN, SPAN), SPAN)


def stage_rows(target_ref, source_refs, layout):
    for index, start, offset, count in layout:
        for piece in range(0, count, SPAN):
            target_ref[offset + piece : offset + piece + SPAN, :] = pair_cat(
                source_refs[index][:, start + piece : start + piece + SPAN].T, 1
            )


def write_rows(source_ref, target_refs, layout, sums):
    for target_ref, (start, offset, count) in zip(target_refs, sums):
        target_ref[start : start + count, :] = source_ref[offset : offset + count, :]
    own = layout[0]
    target_refs[-1][...] = source_ref[own[2] : own[2] + own[3], :]
    for index, start, offset, count in layout[1:]:
        if index == 0:
            target_refs[-1][start : start + count, :] += source_ref[offset : offset + count, :]


def scores(keys_ref, offset, queries, limits):
    keys = block_rows(keys_ref, offset)
    result = dot(jnp.concatenate([keys, keys], axis=1), queries)
    row = lax.broadcasted_iota(jnp.int32, result.shape, 0)
    return jnp.where(row <= limits, result, -1e30)


def fold(value, how):
    return how(value.reshape(SPAN // 8, 8, value.shape[1]), axis=0)


def stage_body(tok_ref, live_ref, *refs, nb, group, halves):
    q_refs, g_refs = refs[:nb], refs[nb : 2 * nb]
    qt_ref, q_ref, gt_ref, grad_ref = refs[2 * nb :]
    step = pl.program_id(0)
    slot, half = lax.div(step, jnp.int32(halves)), lax.rem(step, jnp.int32(halves))
    live = live_ref[tok_ref[0] ^ slot]
    for source in range(nb):

        @pl.when(slot == source)
        def _():
            for head in range(group):
                part = slice(head * SPAN, (head + 1) * SPAN)
                rows = load_rows(q_refs[source], half, head) * logit_scale
                qt_ref[0, :, part] = transposed_pair(rows)
                q_ref[0, part, :] = pair_cat(rows, 1)
                rows = load_rows(g_refs[source], half, head) * live_column(half, live)
                gt_ref[0, :, part] = transposed_pair(rows)
                grad_ref[0, part, :] = pair_cat(rows, 1)


def soft_body(tok_ref, fork_ref, live_ref, *refs, conf):
    nb, group, owners, layout, sources, outs = conf["nb"], conf["group"], conf["owners"], conf["layout"], conf["sources"], conf["outs"]
    halves = conf["rows"] // SPAN
    lanes = group * SPAN
    qt_ref, grad_ref = refs[:2]
    key_refs = refs[2 : 2 + sources]
    prob_ref = refs[2 + sources]
    out_refs = refs[3 + sources : 3 + sources + outs]
    keys_ref, sum_ref, scores_ref, offset_ref, limit_ref, many_ref, sems = refs[3 + sources + outs :]
    step = pl.program_id(0)
    tok = tok_ref[0]
    turn = lax.rem(step, 2)
    score_ref = scores_ref.at[turn]

    def copy_out(of_step, block):
        side = lax.rem(of_step, 2)
        rows = slot_rows(block)
        return pltpu.make_async_copy(scores_ref.at[side, rows], prob_ref.at[of_step, rows], sems.at[side, block])

    def wait_out(of_step):
        def wait(block, _):
            copy_out(of_step, block).wait()
            return 0

        lax.fori_loop(0, even(find_step(many_ref, of_step, tok, halves)[3]), wait, 0)

    @pl.when(step == 0)
    def _():
        list_ancestors(fork_ref, offset_ref, limit_ref, many_ref, tok, nb, conf["rows"] // TILE, conf["paired"])
        stage_rows(keys_ref, key_refs, layout)
        sum_ref[...] = jnp.zeros_like(sum_ref)

    branch, slot, half, count = find_step(many_ref, step, tok, halves)
    place_of = functools.partial(block_offset, offset_ref, owners * SPAN, slot, half, halves)
    live = live_ref[branch]
    def first(block, largest):
        value = scores(keys_ref, place_of(block), qt_ref[0], key_limits(limit_ref, slot, half, live, block, lanes))
        score_ref[slot_rows(block), :] = value
        return jnp.maximum(largest, fold(value, jnp.max))

    largest = paired_loop(count, first, jnp.full((8, lanes), -1e30, f32))
    largest = jnp.max(largest, axis=0, keepdims=True)

    def second(block, total):
        value = jnp.exp(score_ref[slot_rows(block), :] - largest)
        score_ref[slot_rows(block), :] = value
        return total + fold(value, jnp.sum)

    total = paired_loop(count, second, jnp.zeros((8, lanes), f32))
    inverse = 1.0 / jnp.sum(total, axis=0, keepdims=True)

    def third(block, _):
        prob = score_ref[slot_rows(block), :] * inverse
        score_ref[slot_rows(block), :] = prob
        copy_out(step, block).start()
        high, low = split(prob)
        grads = grad_ref[0]
        both = dot(high, grads) + dot(low, grads)
        offset = place_of(block)
        sum_ref[slot_rows(offset // SPAN), :] += both[:, :HEAD_DIM] + both[:, HEAD_DIM:]
        return 0

    paired_loop(count, third, 0)

    @pl.when(step > 0)
    def _():
        wait_out(step - 1)

    @pl.when(step == nb * halves - 1)
    def _():
        wait_out(step)
        write_rows(sum_ref, out_refs, layout, conf["sums"])


def grad_body(tok_ref, fork_ref, live_ref, *refs, conf):
    nb, group, owners, layout, sources, outs = conf["nb"], conf["group"], conf["owners"], conf["layout"], conf["sources"], conf["outs"]
    halves = conf["rows"] // SPAN
    lanes = group * SPAN
    gt_ref, q_ref = refs[:2]
    at = 2
    value_sources = conf["value_sources"]
    key_refs, value_refs = refs[at : at + sources], refs[at + sources : at + sources + value_sources]
    at += sources + value_sources
    prob_ref = refs[at]
    dq_ref = refs[at + 1]
    out_refs = refs[at + 2 : at + 2 + outs]
    (keys_ref, values_ref, sum_ref, probs_ref, dprob_ref, dqt_ref, offset_ref, limit_ref, many_ref, sems) = refs[at + 2 + outs :]
    step = pl.program_id(0)
    tok = tok_ref[0]
    held_ref = probs_ref.at[lax.rem(step, 2)]

    def copy_in(of_step, block):
        side = lax.rem(of_step, 2)
        rows = slot_rows(block)
        return pltpu.make_async_copy(prob_ref.at[of_step, rows], probs_ref.at[side, rows], sems.at[side, block])

    def start_in(of_step):
        def start(block, _):
            copy_in(of_step, block).start()
            return 0

        lax.fori_loop(0, even(find_step(many_ref, of_step, tok, halves)[3]), start, 0)

    @pl.when(step == 0)
    def _():
        list_ancestors(fork_ref, offset_ref, limit_ref, many_ref, tok, nb, conf["rows"] // TILE, conf["paired"])
        start_in(step)
        stage_rows(keys_ref, key_refs, layout)
        stage_rows(values_ref, value_refs, conf["value_layout"])
        sum_ref[...] = jnp.zeros_like(sum_ref)

    @pl.when(step < nb * halves - 1)
    def _():
        start_in(step + 1)

    branch, slot, half, count = find_step(many_ref, step, tok, halves)
    place_of = functools.partial(block_offset, offset_ref, owners * SPAN, slot, half, halves)
    def first(block, delta):
        values = block_rows(values_ref, place_of(block))
        dprob = dot(jnp.concatenate([values, values], axis=1), gt_ref[0])
        dprob_ref[slot_rows(block), :] = dprob
        return delta + fold(held_ref[slot_rows(block), :] * dprob, jnp.sum)

    delta = paired_loop(count, first, jnp.zeros((8, lanes), f32), lambda block: copy_in(step, block).wait())
    delta = jnp.sum(delta, axis=0, keepdims=True)
    dqt_ref[...] = jnp.zeros_like(dqt_ref)

    def second(block, _):
        offset = place_of(block)
        high, low = split(held_ref[slot_rows(block), :] * (dprob_ref[slot_rows(block), :] - delta))
        rows = q_ref[0]
        both = dot(high, rows) + dot(low, rows)
        sum_ref[slot_rows(offset // SPAN), :] += both[:, :HEAD_DIM] + both[:, HEAD_DIM:]
        keys = block_rows(keys_ref, offset)
        dqt_ref[...] += dot_first(keys, high) + dot_first(keys, low)
        return 0

    paired_loop(count, second, 0)
    folded = (dqt_ref[:HEAD_DIM, :] + dqt_ref[HEAD_DIM:, :]) * logit_scale
    for head in range(group):
        dq_ref[:, head * HEAD_DIM : (head + 1) * HEAD_DIM] = folded[:, head * SPAN : (head + 1) * SPAN].T

    @pl.when(step == nb * halves - 1)
    def _():
        write_rows(sum_ref, out_refs, layout, conf["sums"])


def attention_calls(scalars, qs, gs, layout, value_layout, key_sum_rows, value_sum_rows, paired, owners):
    rows, width = qs[0].shape
    nb, group, halves = len(qs), width // HEAD_DIM, rows // SPAN
    lanes = group * SPAN
    steps = nb * halves
    conf = dict(nb=nb, group=group, rows=rows, owners=owners, layout=layout, value_layout=value_layout, paired=paired)
    conf["sources"] = 1 + max(entry[0] for entry in layout)
    conf["value_sources"] = 1 + max(entry[0] for entry in value_layout)
    table_rows = owners * SPAN + nb * rows
    slots = (owners + halves) * SPAN

    def sums_of(sum_rows):
        shapes = [jax.ShapeDtypeStruct((count, HEAD_DIM), f32) for _, _, count in sum_rows]
        return shapes + [jax.ShapeDtypeStruct((nb * rows, HEAD_DIM), f32)], dict(conf, sums=sum_rows, outs=len(sum_rows) + 1)

    key_sums, key_conf = sums_of(key_sum_rows)
    value_sums, value_conf = sums_of(value_sum_rows)
    probs = jax.ShapeDtypeStruct((steps, slots, lanes), f32)
    probs_spec = pl.BlockSpec(memory_space=pl.ANY)
    two_squares = pltpu.VMEM((2, slots, lanes), f32)
    sems = pltpu.SemaphoreType.DMA((2, slots // SPAN))
    table = pltpu.VMEM((table_rows, 2 * HEAD_DIM), bf16)
    table_sum = pltpu.VMEM((table_rows, HEAD_DIM), f32)
    square = pltpu.VMEM((slots, lanes), f32)
    columns = jax.ShapeDtypeStruct((steps, 4 * HEAD_DIM, lanes), bf16)
    pairs = jax.ShapeDtypeStruct((steps, lanes, 2 * HEAD_DIM), bf16)

    def by_step(array):
        return pl.BlockSpec((1, *array.shape[1:]), lambda step: (step, 0, 0))

    lists = [pltpu.SMEM((nb, owners + 1), jnp.int32)] * 2 + [pltpu.SMEM((nb,), jnp.int32)]
    params = pltpu.CompilerParams(vmem_limit_bytes=56 * MIB)
    work = 2 * steps * 6 * SPAN * lanes * 2 * HEAD_DIM

    def stage():
        return pl.pallas_call(
            functools.partial(stage_body, nb=nb, group=group, halves=halves),
            grid=(steps,),
            in_specs=[smem_spec] * 2 + [whole_spec(a) for a in (*qs, *gs)],
            out_specs=[by_step(columns), by_step(pairs)] * 2,
            out_shape=[columns, pairs] * 2,
            compiler_params=pltpu.CompilerParams(vmem_limit_bytes=56 * MIB),
            cost_estimate=pl.CostEstimate(flops=8 * steps * lanes * HEAD_DIM, bytes_accessed=16 * steps * lanes * HEAD_DIM, transcendentals=0),
        )(scalars[0], scalars[2], *qs, *gs)

    def soft(staged, keys):
        qt, _, _, g_pairs = staged
        return pl.pallas_call(
            functools.partial(soft_body, conf=value_conf),
            grid=(steps,),
            in_specs=[smem_spec] * 3 + [by_step(qt), by_step(g_pairs)] + [whole_spec(a) for a in keys],
            out_specs=[probs_spec] + [whole_spec(a) for a in value_sums],
            out_shape=[probs] + value_sums,
            scratch_shapes=[table, table_sum, two_squares]
            + lists
            + [sems],
            compiler_params=params,
            cost_estimate=pl.CostEstimate(flops=2 * work, bytes_accessed=4 * rows * width, transcendentals=0),
        )(*scalars, qt, g_pairs, *keys)

    def grad(staged, keys, values, probs_in):
        _, q_pairs, gt, _ = staged
        dq = jax.ShapeDtypeStruct((nb * rows, width), f32)
        return pl.pallas_call(
            functools.partial(grad_body, conf=key_conf),
            grid=(steps,),
            in_specs=[smem_spec] * 3 + [by_step(gt), by_step(q_pairs)] + [whole_spec(a) for a in (*keys, *values)] + [probs_spec],
            out_specs=[pl.BlockSpec((SPAN, width), lambda step: (step, 0))] + [whole_spec(a) for a in key_sums],
            out_shape=[dq] + key_sums,
            scratch_shapes=[
                table,
                table,
                table_sum,
                two_squares,
                square,
                pltpu.VMEM((2 * HEAD_DIM, lanes), f32),
            ]
            + lists
            + [sems],
            compiler_params=params,
            cost_estimate=pl.CostEstimate(flops=4 * work, bytes_accessed=4 * rows * width, transcendentals=0),
        )(*scalars, gt, q_pairs, *keys, *values, probs_in)

    return stage, soft, grad


def flip(array, mask):
    count = lax.axis_size("tok")
    return lax.ppermute(array, "tok", [(index, index ^ mask) for index in range(count)])


def together(*arrays):
    return lax.optimization_barrier(arrays)


def flip_one_way(array, mask, rising):
    count = lax.axis_size("tok")
    pairs = [(index, index ^ mask) for index in range(count) if (index < index ^ mask) == rising]
    return lax.ppermute(array, "tok", pairs)


def gather_square(array, cut, axis):
    across, down = flip(array, 2), flip(array, 4)
    head = lax.slice_in_dim(across, 0, cut, axis=axis)
    tail = lax.slice_in_dim(down, cut, down.shape[axis], axis=axis)
    return across, down, flip(head, 4), flip(tail, 2)


def scatter_square(across, down, corner):
    from_across, from_down = flip(corner[0], 2), flip(corner[1], 4)
    across_head, down_tail = flip(across[0], 2), flip(down[1], 4)
    across_tail, down_head = flip(across[1] + from_down, 2), flip(down[0] + from_across, 4)
    return across_head, down_head, across_tail, down_tail


def shards_paired(hidden, queries, out_grad, w_key, w_value, fork_tile, live_len):
    owners = lax.axis_size("tok")
    depth = lax.axis_size("head")
    tok = lax.axis_index("tok").astype(jnp.int32)
    core = tok & 1
    rows = hidden.shape[0]
    width = queries.shape[1] // 2
    scalars = (tok.reshape(1), fork_tile, live_len)
    place = (tok >> 1) ^ jnp.arange(depth, dtype=jnp.int32)
    cut = w_key.shape[0] // (2 * HEAD_DIM) * HEAD_DIM

    def mine(array):
        return lax.dynamic_slice_in_dim(array, core * width, width, 1)

    def partners(array):
        return flip(lax.dynamic_slice_in_dim(array, (1 - core) * width, width, 1), 1)

    def project_all(w, outs):
        partial = project(place, (0,), xs, ((0, 0),), [w], outs)
        across, down = flip(w, 2), flip(w, 4)
        across, down, *partial = together(across, down, *partial)
        head, tail = flip(across[:cut], 4), flip(down[cut:], 2)
        partial = project(place, (1, 2), xs, ((0, 0), (1, 0)), [across, down], outs, partial)
        return project(place, (3,), xs, ((0, 0), (0, cut)), [head, tail], outs, partial)

    def sum_heads(partial):
        return lax.psum_scatter(partial, "head", scatter_dimension=0, tiled=True)[0]

    def all_heads(grads):
        return lax.all_gather(grads, "head", axis=0, tiled=False)

    def lead(array):
        return jnp.concatenate([array[:, :SPAN], array[:, rows : rows + SPAN]], axis=1)

    def returned_at_once(across, down, corner, own):
        plan = tuple((index, slot * SPAN, slot * rows, SPAN) for index in range(3) for slot in range(2))
        return combine(own, [flip_one_way(across, 2, False), flip_one_way(down, 4, False), flip_one_way(corner, 6, False)], plan)

    def weight(every, xs):
        first = lax.dynamic_index_in_dim(every, place[3], 0, keepdims=True)
        corner = weight_grad(jnp.zeros_like(place), (0,), xs, first)
        across_head, across_tail, down_head, down_tail = weight_grad(place, (1, 2), xs, every)
        kept = weight_grad(place, (0,), xs, every)
        arrivals = scatter_square((across_head, across_tail), (down_head, down_tail), corner)
        return kept, arrivals

    def finish(kept, arrivals):
        across_head, down_head, across_tail, down_tail = arrivals
        return jnp.concatenate([kept[0] + across_head + down_head, kept[1] + across_tail + down_tail], axis=0)

    def home(array):
        kept, received = array[:rows], flip(array[rows:], 1)
        return jnp.where(core == 0, jnp.concatenate([kept, received], axis=1), jnp.concatenate([received, kept], axis=1))

    hidden = hidden.T
    both = [hidden, flip(hidden, 1)]
    xs = [halve(x) for x in both]
    qs = [mine(queries), partners(queries)]
    gs = [mine(out_grad), partners(out_grad)]
    keys = sum_heads(project_all(w_key, 1)[0])
    leading, trailing = map(sum_heads, project_all(w_value, 2))

    base = owners * SPAN
    layout = (
        (0, 0, base, 2 * rows),
        (0, 0, 0, SPAN),
        (0, rows, SPAN, SPAN),
        (1, 0, 2 * SPAN, 2 * SPAN),
        (2, 0, 4 * SPAN, 2 * SPAN),
        (3, 0, 6 * SPAN, SPAN),
        (4, 0, 7 * SPAN, SPAN),
    )
    value_layout = (
        (0, 0, base, SPAN),
        (0, SPAN, base + rows, SPAN),
        (0, 0, 0, 2 * SPAN),
        (1, 0, base + SPAN, SPAN),
        (1, SPAN, base + rows + SPAN, SPAN),
        (2, 0, 2 * SPAN, 2 * SPAN),
        (3, 0, 4 * SPAN, 2 * SPAN),
        (4, 0, 6 * SPAN, 2 * SPAN),
    )
    value_sum_rows = tuple((0, 2 * (1 + index) * SPAN, 2 * SPAN) for index in range(3))
    stage, soft, grad = attention_calls(scalars, qs, gs, layout, value_layout, value_sum_rows, value_sum_rows, True, owners)

    keys, *staged = together(keys, *stage())
    key_parts = [keys, *gather_square(lead(keys), SPAN, 1)]
    probs, *value_sums = soft(staged, key_parts)
    value_parts = list(together(leading, *value_sums))[:1]
    value_parts += [flip_one_way(value_parts[0], mask, True) for mask in (2, 4, 6)]
    value_grads = returned_at_once(*value_sums)
    probs, value_grads, *value_parts = together(probs, value_grads, *value_parts)
    trailing, value_grads = together(trailing, value_grads)
    every_value = all_heads(value_grads)
    value_parts = [value_parts[0], trailing, *value_parts[1:]]
    grad_query, *key_sums = grad(staged, key_parts, value_parts, probs)
    key_grads = returned_at_once(*key_sums)
    every_key = all_heads(key_grads)
    every_value, key_grads = together(every_value, key_grads)
    grad_w_value = finish(*weight(every_value, xs))
    grad_query, grad_key, grad_value = home(grad_query), home(key_grads), home(value_grads)
    *both, grad_w_value = together(*both, grad_w_value)
    late = [halve(x) for x in both]
    every_key, grad_w_value, grad_query, grad_key, grad_value, *late = together(every_key, grad_w_value, grad_query, grad_key, grad_value, *late)
    grad_w_key = finish(*weight(every_key, late))
    return grad_query, grad_key, grad_value, grad_w_key, grad_w_value


def shards_single(hidden, queries, out_grad, w_key, w_value, fork_tile, live_len):
    owners = lax.axis_size("tok")
    tok = lax.axis_index("tok").astype(jnp.int32)
    scalars = (tok.reshape(1), fork_tile, live_len)

    def projected(w):
        every = lax.all_gather(w, "tok", axis=1, tiled=True)
        partial = lax.dot_general(every, hidden, (((0,), (1,)), ((), ())), precision=lax.Precision.HIGHEST)
        return lax.psum_scatter(partial, "head", scatter_dimension=0, tiled=True)

    keys, values = projected(w_key), projected(w_value)
    layout = ((0, 0, owners * SPAN, hidden.shape[0]), (1, 0, 0, owners * SPAN))
    sums = ((0, 0, owners * SPAN),)
    stage, soft, grad = attention_calls(scalars, [queries], [out_grad], layout, layout, sums, sums, False, owners)

    def parts(array):
        return [array, lax.all_gather(array[:, :SPAN], "tok", axis=1, tiled=True)]

    def returned(remote, own):
        return own.at[:SPAN].add(lax.psum_scatter(remote, "tok", scatter_dimension=0, tiled=True))

    def weight(grads):
        every = lax.all_gather(grads, "head", axis=1, tiled=True)
        columns = lax.dot_general(hidden, every, (((0,), (0,)), ((), ())), precision=lax.Precision.HIGHEST)
        return lax.psum_scatter(columns, "tok", scatter_dimension=1, tiled=True)

    staged = stage()
    key_parts = parts(keys)
    probs, *value_sums = soft(staged, key_parts)
    value_grads = returned(*value_sums)
    grad_query, *key_sums = grad(staged, key_parts, parts(values), probs)
    key_grads = returned(*key_sums)
    return grad_query, key_grads, value_grads, weight(key_grads), weight(value_grads)


def shards(hidden, queries, out_grad, w_key, w_value, fork_tile, live_len):
    pairs = lax.axis_size("tok") // 2
    whole_heads = w_key.shape[1] == HEAD_DIM
    paired = whole_heads and pairs == lax.axis_size("head") and pairs == 4
    run = shards_paired if paired else shards_single
    return run(hidden, queries, out_grad, w_key, w_value, fork_tile, live_len)


def solution(mesh):
    placed = (P("tok", "head"), P("tok", "head"), P("tok", "head"), P("head", "tok"), P("head", "tok"), P(), P())
    return jax.shard_map(
        shards,
        mesh=mesh,
        in_specs=placed,
        out_specs=(P("tok", "head"), P("tok", "head"), P("tok", "head"), P("head", "tok"), P("head", "tok")),
        check_vma=False,
    )
```
